32 devices in a mesh: dom: 8 (over y, x, core), band: 4 (over z).
Axes of the slice: x: 2, y: 2, z: 4, core: 2. Of those that a mesh axis runs over, the one named last changes fastest.
Arguments:
- wave_block: float32 [4, 96, 16, 128], P('band', 'dom'), may hold values from -6 to 6
- potential: float32 [96, 16, 128], P('dom'), may hold values from -1.5 to 1
- projectors: float32 [256, 8, 2048], P('dom', None, 'band'), may hold values from -0.25 to 0.25
- kb_energy: float32 [128, 8], P('dom'), may hold values from 1 to 6
- slot_atom: int32 [256], P('dom'), may hold values from 0 to 127, as said below
- slot_corner: int32 [3, 256], P(None, 'dom'), may hold values from 0 to 112, as said below
Outputs:
- filtered: float32 [4, 96, 16, 128], P('band', 'dom')
The draws below stay inside these ranges and needn't reach their ends.
Inputs may be any that keep to these rules, and one draw needn't show every extreme that they name: `slot_atom`: the slots of slab t are rows t * 32 to (t + 1) * 32 - 1; each names an atom owned by slab t - 1, t or t + 1, where atom a is owned by slab a // 16. `slot_corner`: rows 0, 1, 2 give the box's first cell inside its slab along the three dimensions, at most 4, 0 and 112.
All inputs are finite; a program needn't handle non-finite values.
Results may differ from the reference program's by a relative error of at most 0.00024.
Values sent between devices are 32-bit elements; how exact they have to be, the bound alone decides.
No kernel may reach another device: no remote copies, remote signals or barrier semaphores. Data moves between devices by JAX's collectives and lax.ppermute only.
A program may use at most 64 MiB of HBM per device.

```python
import jax
import jax.numpy as jnp
from jax import lax

PROJ = 8
SX = 8
SY = 16
SZ = 16
DEGREE = 3
CX = 12
CY = 16
CZ = 128
ATOM_DEV = 16
SLOTS = 32
SUP = 2048
NX = 96
BANDS = 4
ATOMS = 128
TOTAL_SLOTS = 256


def draw_slot_atom(key, part):
    key_side, key_pick = jax.random.split(key)
    slot_ids = jnp.arange(TOTAL_SLOTS, dtype=jnp.int32)
    tile_ids = slot_ids // SLOTS
    within = slot_ids % SLOTS
    tile_count = TOTAL_SLOTS // SLOTS
    side_step = jax.random.randint(key_side, (TOTAL_SLOTS,), -1, 2)
    owner_tile = jnp.clip(tile_ids + side_step, 0, tile_count - 1)
    picked = jax.random.randint(key_pick, (TOTAL_SLOTS,), 0, ATOM_DEV)
    atom_ids = owner_tile * ATOM_DEV + picked
    atom_ids = jnp.where(within == 0, tile_ids * ATOM_DEV + ATOM_DEV - 1, atom_ids)
    atom_ids = jnp.where(within == 1, tile_ids * ATOM_DEV, atom_ids)
    return atom_ids.astype(jnp.int32)


def draw_slot_corner(key, part):
    key_list = jax.random.split(key, 3)
    within = jnp.arange(TOTAL_SLOTS, dtype=jnp.int32) % SLOTS
    corner_rows = []
    for axis_pos, limits in enumerate(((CX, SX), (CY, SY), (CZ, SZ))):
        top_corner = limits[0] - limits[1]
        drawn = jax.random.randint(key_list[axis_pos], (TOTAL_SLOTS,), 0, top_corner + 1)
        drawn = jnp.where(within == 0, 0, drawn)
        drawn = jnp.where(within == 1, top_corner, drawn)
        corner_rows.append(drawn)
    return jnp.stack(corner_rows).astype(jnp.int32)


def levels(rng, shape, cuts, smallest, high):
    def one(axis_at, shards_of):
        steps = jax.random.uniform(jax.random.fold_in(jax.random.fold_in(rng, 6), axis_at), (shards_of,), jnp.float32, smallest / len(cuts), high / len(cuts))
        return jnp.repeat(jnp.exp(steps), shape[axis_at] // shards_of).reshape((-1,) + (1,) * (len(shape) - axis_at - 1))

    gain = one(*cuts[0])
    for cut in cuts[1:]:
        gain = gain * one(*cut)
    return gain


def scatter_about(key, extent, scale, reach, cuts=(), kind=jnp.bfloat16):
    factor_of = levels(key, extent, cuts, -0.22, 0.18) if cuts else 1.0
    entries = jax.random.normal(key, extent, jnp.float32) * scale * factor_of
    return jnp.minimum(jnp.maximum(entries, -reach), reach).astype(kind)


def setup_inputs(seed: int = 0) -> dict:
    key_of = jax.random.split(jax.random.key(seed), 7)
    wave_block = scatter_about(key_of[0], (BANDS, NX, CY, CZ), 1.0, 6.0, ((0, 4), (1, 8)), jnp.float32)
    potential = jnp.clip(-1.5 + 2.5 * jax.random.uniform(key_of[1], (NX, CY, CZ), jnp.float32) ** levels(key_of[1], (NX, CY, CZ), ((0, 8),), -0.2, 0.2), -1.5, 1.0)
    projectors = scatter_about(key_of[2], (TOTAL_SLOTS, PROJ, SUP), (SUP // 4) ** -0.5, 0.25, ((0, 8), (2, 4)), jnp.float32)
    kb_energy = jnp.clip(1.0 + 5.0 * jax.random.uniform(key_of[3], (ATOMS, PROJ), jnp.float32) ** levels(key_of[3], (ATOMS, PROJ), ((0, 8),), -0.2, 0.2), 1.0, 6.0)
    slot_atom = draw_slot_atom(jax.random.fold_in(key_of[6], 71), 0)
    slot_corner = draw_slot_corner(jax.random.fold_in(key_of[6], 71), 0)
    return {"wave_block": wave_block, "potential": potential, "projectors": projectors, "kb_energy": kb_energy, "slot_atom": slot_atom, "slot_corner": slot_corner}


STENCIL_WEIGHTS = (-5369.0 / 1800.0, 12.0 / 7.0, -15.0 / 56.0, 10.0 / 189.0, -1.0 / 112.0, 2.0 / 1925.0, -1.0 / 16632.0)
LOWER_EDGE = 3.0
UPPER_EDGE = 30.0
ANCHOR_POINT = 0.5
EXACT = lax.Precision.HIGHEST


def laplacian(padded, reach_cells):
    extent_list = [padded.shape[axis_pos] - 2 * reach_cells for axis_pos in (-3, -2, -1)]

    def window(shift_x, shift_y, shift_z):
        return padded[..., reach_cells + shift_x:reach_cells + shift_x + extent_list[0],
                      reach_cells + shift_y:reach_cells + shift_y + extent_list[1],
                      reach_cells + shift_z:reach_cells + shift_z + extent_list[2]]

    summed = 3.0 * STENCIL_WEIGHTS[0] * window(0, 0, 0)
    for offset in range(1, reach_cells + 1):
        neighbours = window(offset, 0, 0) + window(-offset, 0, 0)
        neighbours = neighbours + window(0, offset, 0) + window(0, -offset, 0)
        neighbours = neighbours + window(0, 0, offset) + window(0, 0, -offset)
        summed = summed + STENCIL_WEIGHTS[offset] * neighbours
    return summed


def extract_boxes(field_block, corners):
    band_count = field_block.shape[0]

    def one_box(corner_x, corner_y, corner_z):
        zero_index = jnp.zeros((), jnp.int32)
        box_cut = lax.dynamic_slice(field_block, (zero_index, corner_x, corner_y, corner_z), (band_count, SX, SY, SZ))
        return box_cut.reshape(band_count, SX * SY * SZ)

    return jax.vmap(one_box)(corners[0], corners[1], corners[2])


def deposit_boxes(base_field, values, corners):
    band_count = base_field.shape[0]
    piece_shape = (band_count, SX, SY, SZ)

    def add_one(slot_pos, accumulated):
        zero_index = jnp.zeros((), jnp.int32)
        start_list = (zero_index, corners[0, slot_pos], corners[1, slot_pos], corners[2, slot_pos])
        current = lax.dynamic_slice(accumulated, start_list, piece_shape)
        return lax.dynamic_update_slice(accumulated, current + values[slot_pos].reshape(piece_shape), start_list)

    return lax.fori_loop(0, values.shape[0], add_one, base_field)


def chebyshev_filter(start_block, apply_fn):
    half_width = (UPPER_EDGE - LOWER_EDGE) / 2.0
    centre = (UPPER_EDGE + LOWER_EDGE) / 2.0
    sigma_first = half_width / (ANCHOR_POINT - centre)
    previous = start_block
    current = (sigma_first / half_width) * (apply_fn(start_block) - centre * start_block)
    sigma_now = sigma_first
    for degree in range(2, DEGREE + 1):
        sigma_next = 1.0 / (2.0 / sigma_first - sigma_now)
        following = (2.0 * sigma_next / half_width) * (apply_fn(current) - centre * current) - (sigma_now * sigma_next) * previous
        previous, current, sigma_now = current, following, sigma_next
    return current


def reference(wave_block, potential, projectors, kb_energy, slot_atom, slot_corner):
    slot_total = slot_atom.shape[0]
    tile_of_slot = jnp.arange(slot_total, dtype=jnp.int32) // SLOTS
    corners = jnp.stack([slot_corner[0] + tile_of_slot * CX, slot_corner[1], slot_corner[2]]).astype(jnp.int32)
    atom_total = kb_energy.shape[0]
    reach_cells = len(STENCIL_WEIGHTS) - 1

    def apply_h(field_block):
        padded = jnp.pad(field_block, ((0, 0), (reach_cells, reach_cells), (reach_cells, reach_cells), (reach_cells, reach_cells)))
        kinetic = -0.5 * laplacian(padded, reach_cells)
        box_values = extract_boxes(field_block, corners)
        projected = jnp.einsum('spc,sbc->spb', projectors, box_values, precision=EXACT)
        atom_sums = jax.ops.segment_sum(projected, slot_atom, num_segments=atom_total)
        scaled = atom_sums * kb_energy[:, :, None]
        returned = scaled[slot_atom]
        values = jnp.einsum('spc,spb->sbc', projectors, returned, precision=EXACT)
        return deposit_boxes(kinetic + potential[None] * field_block, values, corners)

    def one_band(band_field):
        return chebyshev_filter(band_field[None], apply_h)[0]

    return lax.map(one_band, wave_block)
```

```python
import functools

import jax
import jax.numpy as jnp
from jax import lax
from jax.experimental import pallas as pl
from jax.experimental.pallas import tpu as pltpu
from jax.sharding import PartitionSpec as P

SX = 8
SY = 16
SZ = 16
DEGREE = 3
LANES = 128
ROWS = 8
TILES = SX * SY * SZ // LANES
HALVES = SY // ROWS

STENCIL_WEIGHTS = (
    -5369.0 / 1800.0,
    12.0 / 7.0,
    -15.0 / 56.0,
    10.0 / 189.0,
    -1.0 / 112.0,
    2.0 / 1925.0,
    -1.0 / 16632.0,
)
REACH = len(STENCIL_WEIGHTS) - 1
LOWER_EDGE = 3.0
UPPER_EDGE = 30.0
ANCHOR_POINT = 0.5
EXACT = lax.Precision.HIGHEST
HALF_WIDTH = (UPPER_EDGE - LOWER_EDGE) / 2.0
CENTRE = (UPPER_EDGE + LOWER_EDGE) / 2.0
SIGMA_FIRST = HALF_WIDTH / (ANCHOR_POINT - CENTRE)
COPIES = 4


def step_factors():
    sigma_now = SIGMA_FIRST
    factors = [(SIGMA_FIRST / HALF_WIDTH, 0.0)]
    for _ in range(2, DEGREE + 1):
        sigma_next = 1.0 / (2.0 / SIGMA_FIRST - sigma_now)
        factors.append((2.0 * sigma_next / HALF_WIDTH, sigma_now * sigma_next))
        sigma_now = sigma_next
    return factors


def iota(shape, dim):
    return lax.broadcasted_iota(jnp.int32, shape, dim)


def fold_rows(blocks):
    row = iota((ROWS, LANES), 0)
    distance = 1
    while len(blocks) > 1:
        first = (row // distance) % 2 == 0
        blocks = [
            jnp.where(first, a, b) + pltpu.roll(jnp.where(first, b, a), distance, 0)
            for a, b in zip(blocks[::2], blocks[1::2])
        ]
        distance *= 2
    return blocks[0]


def choose(masks, values):
    result = values[-1]
    for mask, value in zip(masks[:-1], values[:-1]):
        result = jnp.where(mask, value, result)
    return result


def pack_kernel(first_tile, proj_ref, out_ref):
    tiles, groups = out_ref.shape[:2]
    row = iota((ROWS, LANES), 0)
    block = iota((ROWS, LANES), 1) // SZ
    apart = (row - block + ROWS) % ROWS
    block_is = [block == b for b in range(ROWS)]
    row_is = [row == r for r in range(ROWS)]
    apart_is = [apart == d for d in range(ROWS)]

    def one(index, carry):
        tile, group = index // groups, index % groups
        cells = pl.ds(pl.multiple_of((first_tile + tile) * LANES, LANES), LANES)
        given = [proj_ref[group * ROWS + u, :, cells] for u in range(ROWS)]
        by_lane = []
        for d in range(ROWS):
            mixed = choose(block_is, [given[(b - d) % ROWS] for b in range(ROWS)])
            by_lane.append(pltpu.roll(mixed, (LANES - d * SZ) % LANES, 1) if d else mixed)
        by_row = []
        for e in range(ROWS):
            mixed = choose(apart_is, [by_lane[(d + e) % ROWS] for d in range(ROWS)])
            by_row.append(pltpu.roll(mixed, e, 0) if e else mixed)
        for p in range(ROWS):
            out_ref[tile, group, p] = choose(row_is, [by_row[(j - p) % ROWS] for j in range(ROWS)])
        return carry

    lax.fori_loop(0, tiles * groups, one, 0)


def member(atom_row, atoms):
    return (iota((atoms, atom_row.shape[1]), 0) == atom_row).astype(jnp.float32)


def total_of(products):
    while len(products) > 1:
        pairs = [a + b for a, b in zip(products[::2], products[1::2])]
        products = pairs + products[len(pairs) * 2 :]
    return products[0]


def project(field, chunks, corner_ref, flat_ref, start_ref=None):
    groups = flat_ref.shape[0]
    lane_block = iota((ROWS, LANES), 1) // SZ

    def one(group, carry):
        corners = [corner_ref[0, group * ROWS + u] for u in range(ROWS)]
        shifts = [
            lax.rem(LANES + u * SZ - corner_ref[2, group * ROWS + u], LANES) for u in range(ROWS)
        ]
        sums = [[] for _ in range(ROWS)]
        for plane, ref in chunks:
            for half in range(HALVES):
                box = None
                for u in range(ROWS):
                    turned = pltpu.roll(field(corners[u] + plane, half), shifts[u], 1)
                    box = turned if u == 0 else jnp.where(lane_block == u, turned, box)
                for p in range(ROWS):
                    sums[p].append(ref[half, group, p] * box)
        flat = fold_rows([total_of(products) for products in sums])
        flat_ref[group] = flat if start_ref is None else flat + start_ref[group]
        return carry

    lax.fori_loop(0, groups, one, 0)


def sum_atoms(flat_ref, atom_row_ref, atoms):
    flat = jnp.concatenate([flat_ref[g] for g in range(flat_ref.shape[0])], axis=1)
    return lax.dot_general(
        flat, member(atom_row_ref[...], atoms), (((1,), (1,)), ((), ())),
        precision=EXACT, preferred_element_type=jnp.float32,
    )


def deposit(scaled, chunks, corner_ref, atom_row_ref, flat_ref, box_ref, parts_ref):
    groups = chunks[0][1].shape[1]
    copies = parts_ref.shape[0]
    lane_block = iota((ROWS, LANES), 1) // SZ
    flat = jnp.dot(
        scaled, member(atom_row_ref[...], scaled.shape[1]),
        precision=EXACT, preferred_element_type=jnp.float32,
    )
    for g in range(groups):
        flat_ref[g] = flat[:, g * LANES : (g + 1) * LANES]
    parts_ref[...] = jnp.zeros(parts_ref.shape, jnp.float32)

    def one(group, carry):
        factors = [
            jnp.broadcast_to(flat_ref[group, pl.ds(p, 1), :], (ROWS, LANES)) for p in range(ROWS)
        ]
        for plane, ref in chunks:
            for half in range(HALVES):
                box_ref[plane * HALVES + half] = total_of(
                    [ref[half, group, p] * factors[p] for p in range(ROWS)]
                )
        for u in range(ROWS):
            slot = group * ROWS + u
            planes = pl.ds(corner_ref[0, slot], SX)
            shift = lax.rem(LANES + corner_ref[2, slot] - u * SZ, LANES)
            for half in range(HALVES):
                at = (u % copies, planes, pl.ds(half * ROWS, ROWS), slice(None))
                added = [
                    pltpu.roll(
                        jnp.where(lane_block == u, box_ref[x * HALVES + half], 0.0), shift, 1
                    )
                    for x in range(SX)
                ]
                parts_ref[at] = parts_ref[at] + jnp.stack(added)
        return carry

    lax.fori_loop(0, groups, one, 0)


def band_matrix(size, block, centre):
    row = iota((size, size), 0)
    column = iota((size, size), 1)
    apart = jnp.abs(row - column)
    table = jnp.where(apart == 0, centre, 0.0)
    for k in range(1, REACH + 1):
        table = jnp.where(apart == k, STENCIL_WEIGHTS[k], table)
    return jnp.where(row // block == column // block, table, 0.0)


def laplacian(padded_ref, extent):
    inner = padded_ref[REACH : REACH + extent]
    flat = inner.reshape(extent * SY, LANES)
    along_z = jnp.dot(
        flat, band_matrix(LANES, LANES, 3.0 * STENCIL_WEIGHTS[0]),
        precision=EXACT, preferred_element_type=jnp.float32,
    )
    along_y = jnp.dot(
        band_matrix(extent * SY, SY, 0.0), flat,
        precision=EXACT, preferred_element_type=jnp.float32,
    )
    total = (along_z + along_y).reshape(inner.shape)
    for k in range(1, REACH + 1):
        total = total + STENCIL_WEIGHTS[k] * (
            padded_ref[REACH + k : REACH + k + extent] + padded_ref[REACH - k : REACH - k + extent]
        )
    return total


HALO_ROWS = REACH * SY


def to_rows(table):
    blocks = [table[:, at : at + LANES] for at in range(0, table.shape[1], LANES)]
    return jnp.concatenate(blocks, axis=0)


def from_rows(rows):
    blocks = [rows[at : at + ROWS] for at in range(0, rows.shape[0], ROWS)]
    return jnp.concatenate(blocks, axis=1)


def write_sends(field_ref, table, odd, mate_ref, cross_ref):
    extent = field_ref.shape[0]
    mate_start = (1 - odd) * (extent - REACH)
    cross_start = odd * (extent - REACH)
    for start, ref in ((mate_start, mate_ref), (cross_start, cross_ref)):
        ref[:HALO_ROWS] = field_ref[pl.ds(start, REACH)].reshape(HALO_ROWS, LANES)
        ref[HALO_ROWS:] = table


def all_planes(ref):
    return [(x, ref.at[pl.ds(x * HALVES, HALVES)]) for x in range(SX)]


def part_planes(where_ref, parts, refs):
    return [
        (where_ref[2 + part] * 2 + h, refs[2 * i + h]) for i, part in enumerate(parts) for h in range(2)
    ]


def field_reader(ref):
    return lambda x, half: ref[x, pl.ds(half * ROWS, ROWS), :]


def early_kernel(parts, has_start, corner_ref, where_ref, field_ref, other_ref, *refs):
    refs = list(refs)
    outs = refs[-2:]
    starts = [refs.pop(0), refs.pop(0)] if has_start else [None, None]
    chunks = part_planes(where_ref, parts, refs[:-2])

    @pl.when(where_ref[1] == 0)
    def _():
        for source_ref, start_ref, out_ref in zip((field_ref, other_ref), starts, outs):
            project(field_reader(source_ref), chunks, corner_ref, out_ref, start_ref)


def first_kernel(where_ref, atom_row_ref, field_ref, energy_ref, inner_ref, end_ref,
                 mate_ref, cross_ref, flat_ref):
    flat_ref[...] = jnp.where(where_ref[1] == 0, inner_ref[...], end_ref[...])
    energy = energy_ref[...]
    sums = sum_atoms(flat_ref, atom_row_ref, energy.shape[1])
    table = jnp.concatenate([to_rows(sums), to_rows(energy)], axis=0)
    write_sends(field_ref, table, where_ref[0], mate_ref, cross_ref)


def whole_kernel(corner_ref, where_ref, atom_row_ref, field_ref, energy_ref, whole_ref,
                 mate_ref, cross_ref, flat_ref):
    project(field_reader(field_ref), all_planes(whole_ref), corner_ref, flat_ref)
    energy = energy_ref[...]
    sums = sum_atoms(flat_ref, atom_row_ref, energy.shape[1])
    table = jnp.concatenate([to_rows(sums), to_rows(energy)], axis=0)
    write_sends(field_ref, table, where_ref[0], mate_ref, cross_ref)


def assemble(where_ref, shared, inner, end, whole_ref):
    def put(part, pair):
        for h in range(2):
            at = pl.ds((where_ref[2 + part] * 2 + h) * HALVES, HALVES)
            whole_ref[at] = pair[h][...]

    put(0, shared[:2])
    put(1, shared[2:])

    @pl.when(where_ref[1] == 0)
    def _():
        put(2, inner[:2])
        put(3, inner[2:])

    @pl.when(where_ref[1] != 0)
    def _():
        put(2, end[:2])
        put(3, [end[2].at[:HALVES], end[2].at[HALVES:]])


def step_kernel(index, chunk_count, corner_ref, where_ref, atom_row_ref, field_ref, potential_ref,
                own_ref, mate_ref, cross_ref, far_ref, *refs):
    factors = step_factors()
    is_first, is_last = index == 0, index + 1 == len(factors)
    given = refs[:chunk_count]
    refs = list(refs[chunk_count:])
    energy_ref = None if is_first else refs.pop(0)
    before_ref = None if is_first else refs.pop(0)
    next_ref = refs.pop(0)
    if not is_last:
        next_mate_ref, next_cross_ref = refs.pop(0), refs.pop(0)
    if is_first:
        energy_ref = refs.pop(0)
    if chunk_count > 1:
        whole_ref = refs.pop(0)
        assemble(where_ref, given[:4], given[4:8], given[8:], whole_ref)
    else:
        whole_ref = given[0]
    chunks = all_planes(whole_ref)
    flat_ref, box_ref, parts_ref, padded_ref = refs
    extent = field_ref.shape[0]
    odd = where_ref[0]

    table = from_rows(own_ref[HALO_ROWS:] + cross_ref[HALO_ROWS:] + far_ref[...])
    if is_first:
        atoms = table.shape[1] // 2
        energy_ref[...] = table[:, atoms:]
        table = table[:, :atoms]
    scaled = table * energy_ref[...]
    deposit(scaled, chunks, corner_ref, atom_row_ref, flat_ref, box_ref, parts_ref)

    cells = field_ref[...]
    padded_ref[REACH : REACH + extent] = cells
    mate_at = (1 - odd) * (extent + REACH)
    cross_at = odd * (extent + REACH)
    padded_ref[pl.ds(mate_at, REACH)] = mate_ref[:HALO_ROWS].reshape(REACH, SY, LANES)
    padded_ref[pl.ds(cross_at, REACH)] = cross_ref[:HALO_ROWS].reshape(REACH, SY, LANES)
    value = -0.5 * laplacian(padded_ref, extent) + (potential_ref[...] - CENTRE) * cells
    for u in range(parts_ref.shape[0]):
        value = value + parts_ref[u]
    value = factors[index][0] * value
    if not is_first:
        value = value - factors[index][1] * before_ref[...]
    next_ref[...] = value
    if not is_last:
        project(field_reader(next_ref), chunks, corner_ref, flat_ref)
        sums = sum_atoms(flat_ref, atom_row_ref, scaled.shape[1])
        write_sends(next_ref, to_rows(sums), odd, next_mate_ref, next_cross_ref)


VMEM = pl.BlockSpec(memory_space=pltpu.VMEM)
SMEM = pl.BlockSpec(memory_space=pltpu.SMEM)
ANY = pl.BlockSpec(memory_space=pl.ANY)


def swap(values, axis, first):
    count = lax.axis_size(axis)
    pairs = []
    for i in range(first, count - 1, 2):
        pairs += [(i, i + 1), (i + 1, i)]
    return lax.ppermute(values, axis, pairs)


def exchange(to_mate, to_cross):
    mate = swap(to_mate, "dom", 0)
    own = to_cross.at[HALO_ROWS:].add(mate[HALO_ROWS:])
    cross = swap(own, "dom", 1)
    far = swap(cross[HALO_ROWS:], "dom", 0)
    return own, mate, cross, far


def on_device(wave_block, potential, projectors, kb_energy, slot_atom, slot_corner):
    bands, planes, cells_y, cells_z = wave_block.shape
    assert bands == 1 and cells_y == SY and cells_z == LANES
    slots, proj_count = projectors.shape[:2]
    atom_own = kb_energy.shape[0]
    atoms = atom_own * lax.axis_size("dom")
    groups = slots // ROWS
    tiles = projectors.shape[2] // LANES
    assert proj_count == ROWS and slots % ROWS == 0
    place = lax.axis_index("dom")
    field = wave_block[0]

    def shaped(*shape):
        return jax.ShapeDtypeStruct(shape, jnp.float32)

    def call(kernel, name, out_shape, scalars, operands, scratch, after=()):
        inputs = len(scalars) + len(operands)

        def body(*refs):
            kernel(*refs[:inputs], *refs[inputs + len(after) :])

        return pl.pallas_call(
            body,
            out_shape=out_shape,
            in_specs=[SMEM] * len(scalars) + [VMEM] * len(operands) + [ANY] * len(after),
            out_specs=jax.tree.map(lambda _: VMEM, out_shape),
            scratch_shapes=[pltpu.VMEM(shape, jnp.float32) for shape in scratch],
            compiler_params=pltpu.CompilerParams(vmem_limit_bytes=16 * 2**20),
            cost_estimate=pl.CostEstimate(flops=0, bytes_accessed=0, transcendentals=0),
            name=name,
        )(*scalars, *operands, *after)

    atom_row = jnp.repeat(slot_atom, SZ)[None, :]
    own_atoms = (jnp.arange(atoms) // atom_own) == place
    energy = jnp.where(own_atoms[None, :], jnp.tile(kb_energy.T, (1, atoms // atom_own)), 0.0)
    flat = (groups, ROWS, LANES)
    boxes = (TILES, ROWS, LANES)
    parts = (COPIES, planes, SY, LANES)
    padded = (planes + 2 * REACH, SY, LANES)
    table_rows = ROWS * atoms // LANES
    sends = [shaped(HALO_ROWS + table_rows, LANES)] * 2

    def pack(first_tile, count):
        return call(
            functools.partial(pack_kernel, first_tile), "pack_projectors",
            shaped(count, groups, ROWS, ROWS, LANES), [], [projectors], [],
        )

    odd = (place % 2).astype(jnp.int32)
    first_sends = [shaped(HALO_ROWS + 2 * table_rows, LANES)] * 2
    if lax.axis_size("band") == 4 and tiles == 2 * HALVES:
        at = lax.axis_index("band").astype(jnp.int32)
        inner = (at == 1) | (at == 2)
        second = jnp.where(at < 2, 2, 1)
        third = jnp.where(at < 2, 3, 0)
        neighbour = at + 1 - 2 * (at % 2)
        where = jnp.stack([odd, 1 - inner.astype(jnp.int32), at, neighbour, second, third])
        at_ends = [(0, 1), (1, 0), (2, 3), (3, 2)]
        middle = [(1, 2), (2, 1)]
        outward = [(1, 0), (2, 3)]
        inward = [(0, 1), (3, 2)]

        def move(values, pairs):
            return [lax.ppermute(value, "band", pairs) for value in values]

        own_part = [pack(0, HALVES), pack(HALVES, HALVES)]
        beside = move(own_part, at_ends)
        across = move(own_part, middle)
        (other,) = move([field], inward)
        end_across = move(across, outward)
        beyond = move(beside, middle)
        end_beyond = move([jnp.concatenate(beyond)], outward)
        flats = call(
            functools.partial(early_kernel, (0, 1, 2), False), "project_early",
            [shaped(*flat)] * 2, [slot_corner, where],
            [field, other, *own_part, *beside, *across], [],
        )
        flats = call(
            functools.partial(early_kernel, (3,), True), "project_late",
            [shaped(*flat)] * 2, [slot_corner, where], [field, other, *flats, *beyond], [], end_across,
        )
        (returned,) = move(flats[1:], outward)
        sent = call(
            first_kernel, "first_sums", first_sends, [where],
            [atom_row, field, energy, flats[0], returned], [flat],
        )
        chunks = [*own_part, *beside, *across, *beyond, *end_across, *end_beyond]
    else:
        where = jnp.stack([odd, jnp.int32(0)])
        chunks = [lax.all_gather(pack(0, tiles), "band", axis=0, tiled=True)]
        sent = call(
            whole_kernel, "project_first", first_sends, [slot_corner, where],
            [atom_row, field, energy, *chunks], [flat],
        )
    before = None
    for index in range(DEGREE):
        own, mate, cross, far = exchange(*sent)
        operands = [atom_row, field, potential, own, mate, cross, far, *chunks]
        out_shape = [shaped(planes, SY, LANES)]
        if index > 0:
            operands += [energy, before]
        if index + 1 < DEGREE:
            out_shape += sends
        if index == 0:
            out_shape += [shaped(ROWS, atoms)]
        if len(chunks) > 1:
            out_shape += [shaped(TILES, groups, ROWS, ROWS, LANES)]
        result = call(
            functools.partial(step_kernel, index, len(chunks)), f"filter_step_{index + 1}",
            out_shape, [slot_corner, where], operands, [flat, boxes, parts, padded],
        )
        before, field = field, result[0]
        sent = result[1:3]
        if index == 0:
            energy = result[3]
            chunks = chunks if len(chunks) == 1 else [result[4]]
    return field[None]


def solution(mesh):
    placed = (
        P("band", "dom", None, None),
        P("dom", None, None),
        P("dom", None, "band"),
        P("dom", None),
        P("dom"),
        P(None, "dom"),
    )
    return jax.shard_map(
        on_device,
        mesh=mesh,
        in_specs=placed,
        out_specs=P("band", "dom", None, None),
        check_vma=False,
    )
```

```python
import functools

import jax
import jax.numpy as jnp
from jax import lax
from jax.experimental import pallas as pl
from jax.experimental.pallas import tpu as pltpu
from jax.sharding import PartitionSpec as P

SX = 8
SY = 16
SZ = 16
DEGREE = 3
LANES = 128
ROWS = 8
TILES = SX * SY * SZ // LANES
HALVES = SY // ROWS

STENCIL_WEIGHTS = (
    -5369.0 / 1800.0,
    12.0 / 7.0,
    -15.0 / 56.0,
    10.0 / 189.0,
    -1.0 / 112.0,
    2.0 / 1925.0,
    -1.0 / 16632.0,
)
REACH = len(STENCIL_WEIGHTS) - 1
LOWER_EDGE = 3.0
UPPER_EDGE = 30.0
ANCHOR_POINT = 0.5
EXACT = lax.Precision.HIGHEST
HALF_WIDTH = (UPPER_EDGE - LOWER_EDGE) / 2.0
CENTRE = (UPPER_EDGE + LOWER_EDGE) / 2.0
SIGMA_FIRST = HALF_WIDTH / (ANCHOR_POINT - CENTRE)
COPIES = 4
FIRST_CHUNK = 1


def step_factors():
    sigma_now = SIGMA_FIRST
    factors = [(SIGMA_FIRST / HALF_WIDTH, 0.0)]
    for _ in range(2, DEGREE + 1):
        sigma_next = 1.0 / (2.0 / SIGMA_FIRST - sigma_now)
        factors.append((2.0 * sigma_next / HALF_WIDTH, sigma_now * sigma_next))
        sigma_now = sigma_next
    return factors


def iota(shape, dim):
    return lax.broadcasted_iota(jnp.int32, shape, dim)


def fold_rows(blocks):
    row = iota((ROWS, LANES), 0)
    distance = 1
    while len(blocks) > 1:
        first = (row // distance) % 2 == 0
        blocks = [
            jnp.where(first, a, b) + pltpu.roll(jnp.where(first, b, a), distance, 0)
            for a, b in zip(blocks[::2], blocks[1::2])
        ]
        distance *= 2
    return blocks[0]


def choose(masks, values):
    result = values[-1]
    for mask, value in zip(masks[:-1], values[:-1]):
        result = jnp.where(mask, value, result)
    return result


def pack_kernel(first_tile, proj_ref, out_ref):
    tiles, groups = out_ref.shape[:2]
    row = iota((ROWS, LANES), 0)
    block = iota((ROWS, LANES), 1) // SZ
    apart = (row - block + ROWS) % ROWS
    block_is = [block == b for b in range(ROWS)]
    row_is = [row == r for r in range(ROWS)]
    apart_is = [apart == d for d in range(ROWS)]

    def one(index, carry):
        tile, group = index // groups, index % groups
        cells = pl.ds(pl.multiple_of((first_tile + tile) * LANES, LANES), LANES)
        given = [proj_ref[group * ROWS + u, :, cells] for u in range(ROWS)]
        by_lane = []
        for d in range(ROWS):
            mixed = choose(block_is, [given[(b - d) % ROWS] for b in range(ROWS)])
            by_lane.append(pltpu.roll(mixed, (LANES - d * SZ) % LANES, 1) if d else mixed)
        by_row = []
        for e in range(ROWS):
            mixed = choose(apart_is, [by_lane[(d + e) % ROWS] for d in range(ROWS)])
            by_row.append(pltpu.roll(mixed, e, 0) if e else mixed)
        for p in range(ROWS):
            out_ref[tile, group, p] = choose(row_is, [by_row[(j - p) % ROWS] for j in range(ROWS)])
        return carry

    lax.fori_loop(0, tiles * groups, one, 0)


def member(atom_row, atoms):
    return (iota((atoms, atom_row.shape[1]), 0) == atom_row).astype(jnp.float32)


def total_of(products):
    while len(products) > 1:
        pairs = [a + b for a, b in zip(products[::2], products[1::2])]
        products = pairs + products[len(pairs) * 2 :]
    return products[0]


def project(field, chunks, corner_ref, flat_ref, start_ref=None):
    groups = flat_ref.shape[0]
    lane_block = iota((ROWS, LANES), 1) // SZ

    def one(group, carry):
        corners = [corner_ref[0, group * ROWS + u] for u in range(ROWS)]
        shifts = [
            lax.rem(LANES + u * SZ - corner_ref[2, group * ROWS + u], LANES) for u in range(ROWS)
        ]
        sums = [[] for _ in range(ROWS)]
        for plane, ref in chunks:
            for half in range(HALVES):
                box = None
                for u in range(ROWS):
                    turned = pltpu.roll(field(corners[u] + plane, half), shifts[u], 1)
                    box = turned if u == 0 else jnp.where(lane_block == u, turned, box)
                for p in range(ROWS):
                    sums[p].append(ref[half, group, p] * box)
        flat = fold_rows([total_of(products) for products in sums])
        flat_ref[group] = flat if start_ref is None else flat + start_ref[group]
        return carry

    lax.fori_loop(0, groups, one, 0)


def sum_atoms(flat_ref, atom_row_ref, atoms):
    flat = jnp.concatenate([flat_ref[g] for g in range(flat_ref.shape[0])], axis=1)
    return lax.dot_general(
        flat, member(atom_row_ref[...], atoms), (((1,), (1,)), ((), ())),
        precision=EXACT, preferred_element_type=jnp.float32,
    )


def deposit(scaled, chunks, corner_ref, atom_row_ref, flat_ref, box_ref, parts_ref):
    groups = chunks[0][1].shape[1]
    copies = parts_ref.shape[0]
    lane_block = iota((ROWS, LANES), 1) // SZ
    flat = jnp.dot(
        scaled, member(atom_row_ref[...], scaled.shape[1]),
        precision=EXACT, preferred_element_type=jnp.float32,
    )
    for g in range(groups):
        flat_ref[g] = flat[:, g * LANES : (g + 1) * LANES]
    parts_ref[...] = jnp.zeros(parts_ref.shape, jnp.float32)

    def one(group, carry):
        factors = [
            jnp.broadcast_to(flat_ref[group, pl.ds(p, 1), :], (ROWS, LANES)) for p in range(ROWS)
        ]
        for plane, ref in chunks:
            for half in range(HALVES):
                box_ref[plane * HALVES + half] = total_of(
                    [ref[half, group, p] * factors[p] for p in range(ROWS)]
                )
        for u in range(ROWS):
            slot = group * ROWS + u
            planes = pl.ds(corner_ref[0, slot], SX)
            shift = lax.rem(LANES + corner_ref[2, slot] - u * SZ, LANES)
            for half in range(HALVES):
                at = (u % copies, planes, pl.ds(half * ROWS, ROWS), slice(None))
                added = [
                    pltpu.roll(
                        jnp.where(lane_block == u, box_ref[x * HALVES + half], 0.0), shift, 1
                    )
                    for x in range(SX)
                ]
                parts_ref[at] = parts_ref[at] + jnp.stack(added)
        return carry

    lax.fori_loop(0, groups, one, 0)


def band_matrix(size, block, centre):
    row = iota((size, size), 0)
    column = iota((size, size), 1)
    apart = jnp.abs(row - column)
    table = jnp.where(apart == 0, centre, 0.0)
    for k in range(1, REACH + 1):
        table = jnp.where(apart == k, STENCIL_WEIGHTS[k], table)
    return jnp.where(row // block == column // block, table, 0.0)


def laplacian(padded_ref, extent):
    inner = padded_ref[REACH : REACH + extent]
    flat = inner.reshape(extent * SY, LANES)
    along_z = jnp.dot(
        flat, band_matrix(LANES, LANES, 3.0 * STENCIL_WEIGHTS[0]),
        precision=EXACT, preferred_element_type=jnp.float32,
    )
    along_y = jnp.dot(
        band_matrix(extent * SY, SY, 0.0), flat,
        precision=EXACT, preferred_element_type=jnp.float32,
    )
    total = (along_z + along_y).reshape(inner.shape)
    for k in range(1, REACH + 1):
        total = total + STENCIL_WEIGHTS[k] * (
            padded_ref[REACH + k : REACH + k + extent] + padded_ref[REACH - k : REACH - k + extent]
        )
    return total


HALO_ROWS = REACH * SY


def to_rows(table):
    blocks = [table[:, at : at + LANES] for at in range(0, table.shape[1], LANES)]
    return jnp.concatenate(blocks, axis=0)


def from_rows(rows):
    blocks = [rows[at : at + ROWS] for at in range(0, rows.shape[0], ROWS)]
    return jnp.concatenate(blocks, axis=1)


def write_halos(field_ref, odd, mate_ref, cross_ref):
    extent = field_ref.shape[0]
    mate_start = (1 - odd) * (extent - REACH)
    cross_start = odd * (extent - REACH)
    for start, ref in ((mate_start, mate_ref), (cross_start, cross_ref)):
        ref[:HALO_ROWS] = field_ref[pl.ds(start, REACH)].reshape(HALO_ROWS, LANES)


def all_planes(ref):
    return [(x, ref.at[pl.ds(x * HALVES, HALVES)]) for x in range(SX)]


def field_reader(ref):
    return lambda x, half: ref[x, pl.ds(half * ROWS, ROWS), :]


def halo_kernel(where_ref, field_ref, mate_ref, cross_ref):
    write_halos(field_ref, where_ref[0], mate_ref, cross_ref)


def opening_kernel(where_ref, field_hbm, proj_hbm, mate_ref, cross_ref, window_ref, low_ref,
                   field_ref, proj_ref, field_sem, proj_sem):
    field_copy = pltpu.make_async_copy(field_hbm, field_ref, field_sem)
    cells = pl.ds(0, proj_ref.shape[2])
    proj_copy = pltpu.make_async_copy(proj_hbm.at[:, :, cells], proj_ref, proj_sem)
    field_copy.start()
    proj_copy.start()
    field_copy.wait()
    window_ref[...] = field_ref[pl.ds(where_ref[FIRST_CHUNK + 6], REACH)]
    write_halos(field_ref, where_ref[0], mate_ref, cross_ref)
    proj_copy.wait()
    pack_kernel(0, proj_ref, low_ref)


def own_planes_kernel(corner_ref, where_ref, field_ref, window_ref, low_ref, high_ref,
                      own_ref, opposite_ref):
    chunks = [low_ref, high_ref]
    here = [(where_ref[FIRST_CHUNK + h], ref) for h, ref in enumerate(chunks)]
    project(field_reader(field_ref), here, corner_ref, own_ref)
    project(field_reader(window_ref), list(enumerate(chunks)), corner_ref, opposite_ref)


def forward_kernel(above_ref, below_ref, above_out_ref, below_out_ref):
    pass


def beside_kernel(corner_ref, where_ref, field_ref, own_ref, returned_ref, *refs):
    flat_ref = refs[-1]
    flat_ref[...] = own_ref[...] + returned_ref[...]
    chunks = [(where_ref[FIRST_CHUNK + 2 + i], ref) for i, ref in enumerate(refs[:-1])]
    project(field_reader(field_ref), chunks, corner_ref, flat_ref, flat_ref)


def table_kernel(atom_row_ref, energy_ref, *refs):
    flat_refs, out_ref, flat_ref = refs[:-2], refs[-2], refs[-1]
    flat_ref[...] = total_of([ref[...] for ref in flat_refs])
    energy = energy_ref[...]
    sums = sum_atoms(flat_ref, atom_row_ref, energy.shape[1])
    out_ref[...] = jnp.concatenate([to_rows(sums), to_rows(energy)], axis=0)


def whole_kernel(corner_ref, field_ref, whole_ref, out_ref):
    project(field_reader(field_ref), all_planes(whole_ref), corner_ref, out_ref)


def step_kernel(index, chunk_count, corner_ref, where_ref, atom_row_ref, field_ref, potential_ref,
                mate_ref, cross_ref, *refs):
    factors = step_factors()
    is_first, is_last = index == 0, index + 1 == len(factors)
    refs = list(refs)
    odd = where_ref[0]
    own_ref, far_ref = refs.pop(0), refs.pop(0)
    if is_first:
        table = from_rows(own_ref[...] + refs.pop(0)[...] + far_ref[...])
    else:
        table = from_rows(own_ref[HALO_ROWS:] + cross_ref[HALO_ROWS:] + far_ref[...])
    if chunk_count > 1:
        chunks = [(where_ref[FIRST_CHUNK + i], refs[i]) for i in range(chunk_count)]
    else:
        chunks = all_planes(refs[0])
    refs = refs[chunk_count:]
    energy_ref = None if is_first else refs.pop(0)
    before_ref = None if is_first else refs.pop(0)
    next_ref = refs.pop(0)
    if not is_last:
        next_mate_ref, next_cross_ref = refs.pop(0), refs.pop(0)
    if is_first:
        energy_ref = refs.pop(0)
    flat_ref, box_ref, parts_ref, padded_ref = refs
    extent = field_ref.shape[0]
    if is_first:
        atoms = table.shape[1] // 2
        energy_ref[...] = table[:, atoms:]
        table = table[:, :atoms]
    scaled = table * energy_ref[...]
    deposit(scaled, chunks, corner_ref, atom_row_ref, flat_ref, box_ref, parts_ref)

    cells = field_ref[...]
    padded_ref[REACH : REACH + extent] = cells
    mate_at = (1 - odd) * (extent + REACH)
    cross_at = odd * (extent + REACH)
    padded_ref[pl.ds(mate_at, REACH)] = mate_ref[:HALO_ROWS].reshape(REACH, SY, LANES)
    padded_ref[pl.ds(cross_at, REACH)] = cross_ref[:HALO_ROWS].reshape(REACH, SY, LANES)
    value = -0.5 * laplacian(padded_ref, extent) + (potential_ref[...] - CENTRE) * cells
    for u in range(parts_ref.shape[0]):
        value = value + parts_ref[u]
    value = factors[index][0] * value
    if not is_first:
        value = value - factors[index][1] * before_ref[...]
    next_ref[...] = value
    if not is_last:
        project(field_reader(next_ref), chunks, corner_ref, flat_ref)
        sums = sum_atoms(flat_ref, atom_row_ref, scaled.shape[1])
        write_halos(next_ref, odd, next_mate_ref, next_cross_ref)
        next_mate_ref[HALO_ROWS:] = to_rows(sums)
        next_cross_ref[HALO_ROWS:] = to_rows(sums)


VMEM = pl.BlockSpec(memory_space=pltpu.VMEM)
SMEM = pl.BlockSpec(memory_space=pltpu.SMEM)
ANY = pl.BlockSpec(memory_space=pl.ANY)


def swap(values, axis, first):
    count = lax.axis_size(axis)
    pairs = []
    for i in range(first, count - 1, 2):
        pairs += [(i, i + 1), (i + 1, i)]
    return lax.ppermute(values, axis, pairs)


def turn(values, axis, step):
    count = lax.axis_size(axis)
    return lax.ppermute(values, axis, [(i, (i + step) % count) for i in range(count)])


def on_device(wave_block, potential, projectors, kb_energy, slot_atom, slot_corner):
    bands, planes, cells_y, cells_z = wave_block.shape
    assert bands == 1 and cells_y == SY and cells_z == LANES
    slots, proj_count = projectors.shape[:2]
    atom_own = kb_energy.shape[0]
    atoms = atom_own * lax.axis_size("dom")
    groups = slots // ROWS
    tiles = projectors.shape[2] // LANES
    assert proj_count == ROWS and slots % ROWS == 0
    place = lax.axis_index("dom")
    field = wave_block[0]

    def shaped(*shape):
        return jax.ShapeDtypeStruct(shape, jnp.float32)

    def call(kernel, name, out_shape, scalars, operands, scratch, after=(), in_place={}):
        inputs = len(scalars) + len(operands)

        def body(*refs):
            kernel(*refs[:inputs], *refs[inputs + len(after) :])

        return pl.pallas_call(
            body,
            out_shape=out_shape,
            in_specs=[SMEM] * len(scalars) + [VMEM] * len(operands) + [ANY] * len(after),
            out_specs=jax.tree.map(lambda _: VMEM, out_shape),
            scratch_shapes=[pltpu.VMEM(shape, jnp.float32) for shape in scratch],
            compiler_params=pltpu.CompilerParams(vmem_limit_bytes=16 * 2**20),
            input_output_aliases=in_place,
            cost_estimate=pl.CostEstimate(flops=0, bytes_accessed=0, transcendentals=0),
            name=name,
        )(*scalars, *operands, *after)

    atom_row = jnp.repeat(slot_atom, SZ)[None, :]
    own_atoms = (jnp.arange(atoms) // atom_own) == place
    energy = jnp.where(own_atoms[None, :], jnp.tile(kb_energy.T, (1, atoms // atom_own)), 0.0)
    flat = (groups, ROWS, LANES)
    boxes = (TILES, ROWS, LANES)
    parts = (COPIES, planes, SY, LANES)
    padded = (planes + 2 * REACH, SY, LANES)
    table_rows = ROWS * atoms // LANES
    sends = [shaped(HALO_ROWS + table_rows, LANES)] * 2

    def pack(first_tile, count, after=()):
        return call(
            functools.partial(pack_kernel, first_tile), "pack_projectors",
            shaped(count, groups, ROWS, ROWS, LANES), [], [projectors], [], after,
        )

    odd = (place % 2).astype(jnp.int32)
    halos = [shaped(HALO_ROWS, LANES)] * 2
    if lax.axis_size("band") == 4 and tiles == 2 * HALVES:
        at = lax.axis_index("band").astype(jnp.int32)
        owners = [at, (at + 1) % 4, (at + 3) % 4, (at + 2) % 4]
        where = jnp.stack([odd] + [2 * part + h for part in owners for h in range(2)])
        window = shaped(REACH, SY, LANES)
        packed_plane = shaped(HALVES, groups, ROWS, ROWS, LANES)
        mate, cross, opposite, low = pl.pallas_call(
            opening_kernel,
            out_shape=halos + [window, packed_plane],
            in_specs=[SMEM, ANY, ANY],
            out_specs=[VMEM] * 4,
            scratch_shapes=[
                pltpu.VMEM(field.shape, jnp.float32),
                pltpu.VMEM((slots, ROWS, HALVES * LANES), jnp.float32),
                pltpu.SemaphoreType.DMA,
                pltpu.SemaphoreType.DMA,
            ],
            compiler_params=pltpu.CompilerParams(vmem_limit_bytes=16 * 2**20),
            cost_estimate=pl.CostEstimate(flops=0, bytes_accessed=0, transcendentals=0),
            name="open",
        )(where, field, projectors)
        opposite = turn(opposite, "band", 2)
        below_low = turn(low, "band", 1)
        high = pack(HALVES, HALVES, [opposite])
        above_high = turn(high, "band", -1)
        below_high = turn(high, "band", 1)
        above_low = turn(low, "band", -1)
        own, returned = call(
            own_planes_kernel, "project_own", [shaped(*flat)] * 2, [slot_corner, where],
            [field, opposite, low, high], [],
        )
        returned = turn(returned, "band", 2)
        above_high, below_low = call(
            forward_kernel, "forward", [packed_plane] * 2, [], [above_high, below_low], [],
            [returned, above_low, below_high], {0: 0, 1: 1},
        )
        far_low = turn(below_low, "band", 1)
        far_high = turn(above_high, "band", -1)
        beside = [above_low, above_high, below_low, below_high]
        flats = [
            call(
                beside_kernel, "project_beside", shaped(*flat), [slot_corner, where],
                [field, own, returned, *beside], [],
            )
        ]
        chunks = [low, high, *beside, far_low, far_high]
    else:
        where = odd[None]
        mate, cross = call(halo_kernel, "cut_halos", halos, [where], [field], [])
        chunks = [lax.all_gather(pack(0, tiles), "band", axis=0, tiled=True)]
        flats = [
            call(whole_kernel, "project_first", shaped(*flat), [slot_corner], [field, *chunks], [])
        ]
    mate, cross = swap(mate, "dom", 0), swap(cross, "dom", 1)
    own = call(
        table_kernel, "first_sums", shaped(2 * table_rows, LANES), [],
        [atom_row, energy, *flats], [flat],
    )
    own = own + swap(own, "dom", 0)
    other = swap(own, "dom", 1)
    far = swap(other, "dom", 0)
    before = None
    for index in range(DEGREE):
        if index > 0:
            to_mate, to_cross = sent
            mate = swap(to_mate, "dom", 0)
            own = to_cross.at[HALO_ROWS:].add(mate[HALO_ROWS:])
            cross = swap(own, "dom", 1)
            far = swap(cross[HALO_ROWS:], "dom", 0)
        operands = [atom_row, field, potential, mate, cross, own, far]
        if index == 0:
            operands.append(other)
        operands += chunks
        out_shape = [shaped(planes, SY, LANES)]
        if index > 0:
            operands += [energy, before]
        if index + 1 < DEGREE:
            out_shape += sends
        if index == 0:
            out_shape += [shaped(ROWS, atoms)]
        result = call(
            functools.partial(step_kernel, index, len(chunks)), f"filter_step_{index + 1}",
            out_shape, [slot_corner, where], operands, [flat, boxes, parts, padded],
        )
        before, field = field, result[0]
        sent = result[1:3]
        if index == 0:
            energy = result[3]
    return field[None]


def solution(mesh):
    placed = (
        P("band", "dom", None, None),
        P("dom", None, None),
        P("dom", None, "band"),
        P("dom", None),
        P("dom"),
        P(None, "dom"),
    )
    return jax.shard_map(
        on_device,
        mesh=mesh,
        in_specs=placed,
        out_specs=P("band", "dom", None, None),
        check_vma=False,
    )
```

```python
import functools

import jax
import jax.numpy as jnp
from jax import lax
from jax.experimental import pallas as pl
from jax.experimental.pallas import tpu as pltpu
from jax.sharding import PartitionSpec as P

SX = 8
SY = 16
SZ = 16
DEGREE = 3
LANES = 128
ROWS = 8
TILES = SX * SY * SZ // LANES
HALVES = SY // ROWS

STENCIL_WEIGHTS = (
    -5369.0 / 1800.0,
    12.0 / 7.0,
    -15.0 / 56.0,
    10.0 / 189.0,
    -1.0 / 112.0,
    2.0 / 1925.0,
    -1.0 / 16632.0,
)
REACH = len(STENCIL_WEIGHTS) - 1
LOWER_EDGE = 3.0
UPPER_EDGE = 30.0
ANCHOR_POINT = 0.5
HALF_WIDTH = (UPPER_EDGE - LOWER_EDGE) / 2.0
CENTRE = (UPPER_EDGE + LOWER_EDGE) / 2.0
SIGMA_FIRST = HALF_WIDTH / (ANCHOR_POINT - CENTRE)
COPIES = 4
FIRST_CHUNK = 1


def step_factors():
    sigma_now = SIGMA_FIRST
    factors = [(SIGMA_FIRST / HALF_WIDTH, 0.0)]
    for _ in range(2, DEGREE + 1):
        sigma_next = 1.0 / (2.0 / SIGMA_FIRST - sigma_now)
        factors.append((2.0 * sigma_next / HALF_WIDTH, sigma_now * sigma_next))
        sigma_now = sigma_next
    return factors


def iota(shape, dim):
    return lax.broadcasted_iota(jnp.int32, shape, dim)


def fold_rows(blocks):
    row = iota((ROWS, LANES), 0)
    distance = 1
    while len(blocks) > 1:
        first = (row // distance) % 2 == 0
        blocks = [
            jnp.where(first, a, b) + pltpu.roll(jnp.where(first, b, a), distance, 0)
            for a, b in zip(blocks[::2], blocks[1::2])
        ]
        distance *= 2
    return blocks[0]


def choose(masks, values):
    result = values[-1]
    for mask, value in zip(masks[:-1], values[:-1]):
        result = jnp.where(mask, value, result)
    return result


def pack_kernel(first_tile, proj_ref, out_ref):
    tiles, groups = out_ref.shape[:2]
    row = iota((ROWS, LANES), 0)
    block = iota((ROWS, LANES), 1) // SZ
    apart = (row - block + ROWS) % ROWS
    block_is = [block == b for b in range(ROWS)]
    row_is = [row == r for r in range(ROWS)]
    apart_is = [apart == d for d in range(ROWS)]

    def one(index, carry):
        tile, group = index // groups, index % groups
        cells = pl.ds(pl.multiple_of((first_tile + tile) * LANES, LANES), LANES)
        given = [proj_ref[group * ROWS + u, :, cells] for u in range(ROWS)]
        by_lane = []
        for d in range(ROWS):
            mixed = choose(block_is, [given[(b - d) % ROWS] for b in range(ROWS)])
            by_lane.append(pltpu.roll(mixed, (LANES - d * SZ) % LANES, 1) if d else mixed)
        by_row = []
        for e in range(ROWS):
            mixed = choose(apart_is, [by_lane[(d + e) % ROWS] for d in range(ROWS)])
            by_row.append(pltpu.roll(mixed, e, 0) if e else mixed)
        for p in range(ROWS):
            out_ref[tile, group, p] = choose(row_is, [by_row[(j - p) % ROWS] for j in range(ROWS)])
        return carry

    lax.fori_loop(0, tiles * groups, one, 0)


def halves_of(value):
    high = value.astype(jnp.bfloat16)
    return high, (value - high.astype(jnp.float32)).astype(jnp.bfloat16)


def thirds_of(value):
    rest, parts = value, []
    for _ in range(3):
        high = rest.astype(jnp.bfloat16).astype(jnp.float32)
        parts.append(high)
        rest = rest - high
    return jnp.concatenate(parts, axis=0).astype(jnp.bfloat16)


def sum_thirds(value):
    return value[:ROWS] + value[ROWS : 2 * ROWS] + value[2 * ROWS :]


def table_kernel(atom_row_ref, member_ref, along_z_ref, along_y_ref):
    atoms = iota(member_ref.shape, 0)
    member_ref[...] = (atoms == atom_row_ref[...]).astype(jnp.float32).astype(jnp.bfloat16)
    high, low = halves_of(band_matrix(LANES, LANES, 3.0 * STENCIL_WEIGHTS[0]))
    along_z_ref[...] = jnp.concatenate([high, low, high], axis=0)
    high, low = halves_of(band_matrix(along_y_ref.shape[0], SY, 0.0))
    along_y_ref[...] = jnp.concatenate([high, high, low], axis=1)


def total_of(products):
    while len(products) > 1:
        pairs = [a + b for a, b in zip(products[::2], products[1::2])]
        products = pairs + products[len(pairs) * 2 :]
    return products[0]


def project(field, chunks, corner_ref, flat_ref, start_ref=None):
    groups = flat_ref.shape[0]
    lane_block = iota((ROWS, LANES), 1) // SZ

    def one(group, carry):
        corners = [corner_ref[0, group * ROWS + u] for u in range(ROWS)]
        shifts = [
            lax.rem(LANES + u * SZ - corner_ref[2, group * ROWS + u], LANES) for u in range(ROWS)
        ]
        sums = [[] for _ in range(ROWS)]
        for plane, ref in chunks:
            for half in range(HALVES):
                box = None
                for u in range(ROWS):
                    turned = pltpu.roll(field(corners[u] + plane, half), shifts[u], 1)
                    box = turned if u == 0 else jnp.where(lane_block == u, turned, box)
                for p in range(ROWS):
                    sums[p].append(ref[half, group, p] * box)
        flat = fold_rows([total_of(products) for products in sums])
        flat_ref[group] = flat if start_ref is None else flat + start_ref[group]
        return carry

    for group in range(groups):
        one(group, 0)


def sum_atoms(flat_ref, member_ref):
    flat = jnp.concatenate([flat_ref[g] for g in range(flat_ref.shape[0])], axis=1)
    return sum_thirds(
        lax.dot_general(
            thirds_of(flat), member_ref[...], (((1,), (1,)), ((), ())),
            preferred_element_type=jnp.float32,
        )
    )


def deposit(scaled, chunks, corner_ref, member_ref, flat_ref, box_ref, parts_ref):
    groups = chunks[0][1].shape[1]
    copies = parts_ref.shape[0]
    lane_block = iota((ROWS, LANES), 1) // SZ
    flat = sum_thirds(
        jnp.dot(thirds_of(scaled), member_ref[...], preferred_element_type=jnp.float32)
    )
    for g in range(groups):
        flat_ref[g] = flat[:, g * LANES : (g + 1) * LANES]
    parts_ref[...] = jnp.zeros(parts_ref.shape, jnp.float32)

    def one(group, carry):
        factors = [
            jnp.broadcast_to(flat_ref[group, pl.ds(p, 1), :], (ROWS, LANES)) for p in range(ROWS)
        ]
        for plane, ref in chunks:
            for half in range(HALVES):
                box_ref[plane * HALVES + half] = total_of(
                    [ref[half, group, p] * factors[p] for p in range(ROWS)]
                )
        for u in range(ROWS):
            slot = group * ROWS + u
            planes = pl.ds(corner_ref[0, slot], SX)
            shift = lax.rem(LANES + corner_ref[2, slot] - u * SZ, LANES)
            for half in range(HALVES):
                at = (u % copies, planes, pl.ds(half * ROWS, ROWS), slice(None))
                added = [
                    pltpu.roll(
                        jnp.where(lane_block == u, box_ref[x * HALVES + half], 0.0), shift, 1
                    )
                    for x in range(SX)
                ]
                parts_ref[at] = parts_ref[at] + jnp.stack(added)
        return carry

    for group in range(groups):
        one(group, 0)


def band_matrix(size, block, centre):
    row = iota((size, size), 0)
    column = iota((size, size), 1)
    apart = jnp.abs(row - column)
    table = jnp.where(apart == 0, centre, 0.0)
    for k in range(1, REACH + 1):
        table = jnp.where(apart == k, STENCIL_WEIGHTS[k], table)
    return jnp.where(row // block == column // block, table, 0.0)


def laplacian(padded_ref, extent, along_z_ref, along_y_ref):
    inner = padded_ref[REACH : REACH + extent]
    high, low = halves_of(inner.reshape(extent * SY, LANES))
    along_z = jnp.dot(
        jnp.concatenate([high, high, low], axis=1), along_z_ref[...],
        preferred_element_type=jnp.float32,
    )
    along_y = jnp.dot(
        along_y_ref[...], jnp.concatenate([high, low, high], axis=0),
        preferred_element_type=jnp.float32,
    )
    total = (along_z + along_y).reshape(inner.shape)
    for k in range(1, REACH + 1):
        total = total + STENCIL_WEIGHTS[k] * (
            padded_ref[REACH + k : REACH + k + extent] + padded_ref[REACH - k : REACH - k + extent]
        )
    return total


HALO_ROWS = REACH * SY


def to_rows(table):
    blocks = [table[:, at : at + LANES] for at in range(0, table.shape[1], LANES)]
    return jnp.concatenate(blocks, axis=0)


def from_rows(rows):
    blocks = [rows[at : at + ROWS] for at in range(0, rows.shape[0], ROWS)]
    return jnp.concatenate(blocks, axis=1)


def write_halos(field_ref, odd, mate_ref, cross_ref):
    extent = field_ref.shape[0]
    mate_start = (1 - odd) * (extent - REACH)
    cross_start = odd * (extent - REACH)
    for start, ref in ((mate_start, mate_ref), (cross_start, cross_ref)):
        ref[:HALO_ROWS] = field_ref[pl.ds(start, REACH)].reshape(HALO_ROWS, LANES)


def all_planes(ref):
    return [(x, ref.at[pl.ds(x * HALVES, HALVES)]) for x in range(SX)]


def field_reader(ref):
    return lambda x, half: ref[x, pl.ds(half * ROWS, ROWS), :]


def window_kernel(where_ref, field_ref, mate_ref, cross_ref, *window_refs):
    write_halos(field_ref, where_ref[0], mate_ref, cross_ref)
    for ref in window_refs:
        ref[...] = field_ref[pl.ds(where_ref[FIRST_CHUNK + 6], REACH)]


def own_planes_kernel(corner_ref, where_ref, field_ref, window_ref, low_ref, high_ref,
                      own_ref, opposite_ref):
    chunks = [low_ref, high_ref]
    here = [(where_ref[FIRST_CHUNK + h], ref) for h, ref in enumerate(chunks)]
    project(field_reader(field_ref), here, corner_ref, own_ref)
    project(field_reader(window_ref), list(enumerate(chunks)), corner_ref, opposite_ref)


def forward_kernel(corner_ref, where_ref, field_ref, own_ref, returned_ref, above_ref, below_ref,
                   flat_ref, above_out_ref, below_out_ref):
    above_out_ref[...] = above_ref[...]
    below_out_ref[...] = below_ref[...]
    flat_ref[...] = own_ref[...] + returned_ref[...]
    chunks = [(where_ref[FIRST_CHUNK + 3], above_ref), (where_ref[FIRST_CHUNK + 4], below_ref)]
    project(field_reader(field_ref), chunks, corner_ref, flat_ref, flat_ref)


def beside_kernel(corner_ref, where_ref, field_ref, start_ref, above_ref, below_ref, out_ref):
    chunks = [(where_ref[FIRST_CHUNK + 2], above_ref), (where_ref[FIRST_CHUNK + 5], below_ref)]
    project(field_reader(field_ref), chunks, corner_ref, out_ref, start_ref)


def first_sums_kernel(member_ref, energy_ref, *refs):
    flat_refs, out_ref, flat_ref = refs[:-2], refs[-2], refs[-1]
    flat_ref[...] = total_of([ref[...] for ref in flat_refs])
    sums = sum_atoms(flat_ref, member_ref)
    out_ref[...] = jnp.concatenate([to_rows(sums), to_rows(energy_ref[...])], axis=0)


def whole_kernel(corner_ref, field_ref, whole_ref, out_ref):
    project(field_reader(field_ref), all_planes(whole_ref), corner_ref, out_ref)


def step_kernel(index, chunk_count, corner_ref, where_ref, member_ref, along_z_ref, along_y_ref,
                field_ref, potential_ref, mate_ref, cross_ref, *refs):
    factors = step_factors()
    is_first, is_last = index == 0, index + 1 == len(factors)
    refs = list(refs)
    odd = where_ref[0]
    own_ref, far_ref = refs.pop(0), refs.pop(0)
    if is_first:
        table = from_rows(own_ref[...] + refs.pop(0)[...] + far_ref[...])
    else:
        table = from_rows(own_ref[HALO_ROWS:] + cross_ref[HALO_ROWS:] + far_ref[...])
    if chunk_count > 1:
        chunks = [(where_ref[FIRST_CHUNK + i], refs[i]) for i in range(chunk_count)]
    else:
        chunks = all_planes(refs[0])
    refs = refs[chunk_count:]
    energy_ref = None if is_first else refs.pop(0)
    before_ref = None if is_first else refs.pop(0)
    next_ref = refs.pop(0)
    if not is_last:
        next_mate_ref, next_cross_ref = refs.pop(0), refs.pop(0)
    if is_first:
        energy_ref = refs.pop(0)
    flat_ref, box_ref, parts_ref, padded_ref = refs
    extent = field_ref.shape[0]
    if is_first:
        atoms = table.shape[1] // 2
        energy_ref[...] = table[:, atoms:]
        table = table[:, :atoms]
    scaled = table * energy_ref[...]
    deposit(scaled, chunks, corner_ref, member_ref, flat_ref, box_ref, parts_ref)

    cells = field_ref[...]
    padded_ref[REACH : REACH + extent] = cells
    mate_at = (1 - odd) * (extent + REACH)
    cross_at = odd * (extent + REACH)
    padded_ref[pl.ds(mate_at, REACH)] = mate_ref[:HALO_ROWS].reshape(REACH, SY, LANES)
    padded_ref[pl.ds(cross_at, REACH)] = cross_ref[:HALO_ROWS].reshape(REACH, SY, LANES)
    value = -0.5 * laplacian(padded_ref, extent, along_z_ref, along_y_ref) + (potential_ref[...] - CENTRE) * cells
    for u in range(parts_ref.shape[0]):
        value = value + parts_ref[u]
    value = factors[index][0] * value
    if not is_first:
        value = value - factors[index][1] * before_ref[...]
    next_ref[...] = value
    if not is_last:
        project(field_reader(next_ref), chunks, corner_ref, flat_ref)
        sums = sum_atoms(flat_ref, member_ref)
        write_halos(next_ref, odd, next_mate_ref, next_cross_ref)
        next_mate_ref[HALO_ROWS:] = to_rows(sums)
        next_cross_ref[HALO_ROWS:] = to_rows(sums)


VMEM = pl.BlockSpec(memory_space=pltpu.VMEM)
SMEM = pl.BlockSpec(memory_space=pltpu.SMEM)
ANY = pl.BlockSpec(memory_space=pl.ANY)


def swap(values, axis, first):
    count = lax.axis_size(axis)
    pairs = []
    for i in range(first, count - 1, 2):
        pairs += [(i, i + 1), (i + 1, i)]
    return lax.ppermute(values, axis, pairs)


def turn(values, axis, step):
    count = lax.axis_size(axis)
    return lax.ppermute(values, axis, [(i, (i + step) % count) for i in range(count)])


def on_device(wave_block, potential, projectors, kb_energy, slot_atom, slot_corner):
    bands, planes, cells_y, cells_z = wave_block.shape
    assert bands == 1 and cells_y == SY and cells_z == LANES
    slots, proj_count = projectors.shape[:2]
    atom_own = kb_energy.shape[0]
    atoms = atom_own * lax.axis_size("dom")
    groups = slots // ROWS
    tiles = projectors.shape[2] // LANES
    assert proj_count == ROWS and slots % ROWS == 0
    place = lax.axis_index("dom")
    field = wave_block[0]

    def shaped(*shape):
        return jax.ShapeDtypeStruct(shape, jnp.float32)

    def call(kernel, name, out_shape, scalars, operands, scratch, after=()):
        inputs = len(scalars) + len(operands)

        def body(*refs):
            kernel(*refs[:inputs], *refs[inputs + len(after) :])

        return pl.pallas_call(
            body,
            out_shape=out_shape,
            in_specs=[SMEM] * len(scalars) + [VMEM] * len(operands) + [ANY] * len(after),
            out_specs=jax.tree.map(lambda _: VMEM, out_shape),
            scratch_shapes=[pltpu.VMEM(shape, jnp.float32) for shape in scratch],
            compiler_params=pltpu.CompilerParams(vmem_limit_bytes=16 * 2**20),
            cost_estimate=pl.CostEstimate(flops=0, bytes_accessed=0, transcendentals=0),
            name=name,
        )(*scalars, *operands, *after)

    atom_row = jnp.repeat(slot_atom, SZ)[None, :]
    own_atoms = (jnp.arange(atoms) // atom_own) == place
    energy = jnp.where(own_atoms[None, :], jnp.tile(kb_energy.T, (1, atoms // atom_own)), 0.0)
    flat = (groups, ROWS, LANES)
    boxes = (TILES, ROWS, LANES)
    parts = (COPIES, planes, SY, LANES)
    padded = (planes + 2 * REACH, SY, LANES)
    table_rows = ROWS * atoms // LANES
    sends = [shaped(HALO_ROWS + table_rows, LANES)] * 2

    def pack(first_tile, count, after=()):
        return call(
            functools.partial(pack_kernel, first_tile), "pack_projectors",
            shaped(count, groups, ROWS, ROWS, LANES), [], [projectors], [], after,
        )

    tables = call(
        table_kernel, "tables",
        [
            jax.ShapeDtypeStruct(shape, jnp.bfloat16)
            for shape in (
                (atoms, slots * SZ), (3 * LANES, LANES), (planes * SY, 3 * planes * SY)
            )
        ],
        [], [atom_row], [],
    )
    odd = (place % 2).astype(jnp.int32)
    halos = [shaped(HALO_ROWS, LANES)] * 2
    if lax.axis_size("band") == 4 and tiles == 2 * HALVES:
        at = lax.axis_index("band").astype(jnp.int32)
        owners = [at, (at + 1) % 4, (at + 3) % 4, (at + 2) % 4]
        where = jnp.stack([odd] + [2 * part + h for part in owners for h in range(2)])
        window = shaped(REACH, SY, LANES)
        low = pack(0, HALVES)
        below_low = turn(low, "band", 1)
        mate, cross, opposite = call(
            window_kernel, "cut_window", halos + [window], [where], [field], []
        )
        opposite = turn(opposite, "band", 2)
        high = pack(HALVES, HALVES, [opposite])
        above_high = turn(high, "band", -1)
        below_high = turn(high, "band", 1)
        above_low = turn(low, "band", -1)
        own, returned = call(
            own_planes_kernel, "project_own", [shaped(*flat)] * 2, [slot_corner, where],
            [field, opposite, low, high], [],
        )
        returned = turn(returned, "band", 2)
        own, above_on, below_on = call(
            forward_kernel, "project_and_forward", [shaped(*flat)] + [shaped(*low.shape)] * 2,
            [slot_corner, where], [field, own, returned, above_high, below_low], [],
        )
        far_low = turn(below_on, "band", 1)
        far_high = turn(above_on, "band", -1)
        own = call(
            beside_kernel, "project_beside", shaped(*flat), [slot_corner, where],
            [field, own, above_low, below_high], [],
        )
        flats = [own]
        chunks = [low, high, above_low, above_high, below_low, below_high, far_low, far_high]
    else:
        where = odd[None]
        mate, cross = call(window_kernel, "cut_windows", halos, [where], [field], [])
        chunks = [lax.all_gather(pack(0, tiles), "band", axis=0, tiled=True)]
        flats = [
            call(whole_kernel, "project_first", shaped(*flat), [slot_corner], [field, *chunks], [])
        ]
    mate, cross = swap(mate, "dom", 0), swap(cross, "dom", 1)
    own = call(
        first_sums_kernel, "first_sums", shaped(2 * table_rows, LANES), [],
        [tables[0], energy, *flats], [flat],
    )
    own = own + swap(own, "dom", 0)
    other = swap(own, "dom", 1)
    far = swap(other, "dom", 0)
    before = None
    for index in range(DEGREE):
        if index > 0:
            to_mate, to_cross = sent
            mate = swap(to_mate, "dom", 0)
            own = to_cross.at[HALO_ROWS:].add(mate[HALO_ROWS:])
            cross = swap(own, "dom", 1)
            far = swap(cross[HALO_ROWS:], "dom", 0)
        operands = [*tables, field, potential, mate, cross, own, far]
        if index == 0:
            operands.append(other)
        operands += chunks
        out_shape = [shaped(planes, SY, LANES)]
        if index > 0:
            operands += [energy, before]
        if index + 1 < DEGREE:
            out_shape += sends
        if index == 0:
            out_shape += [shaped(ROWS, atoms)]
        result = call(
            functools.partial(step_kernel, index, len(chunks)), f"filter_step_{index + 1}",
            out_shape, [slot_corner, where], operands, [flat, boxes, parts, padded],
        )
        before, field = field, result[0]
        sent = result[1:3]
        if index == 0:
            energy = result[3]
    return field[None]


def solution(mesh):
    placed = (
        P("band", "dom", None, None),
        P("dom", None, None),
        P("dom", None, "band"),
        P("dom", None),
        P("dom"),
        P(None, "dom"),
    )
    return jax.shard_map(
        on_device,
        mesh=mesh,
        in_specs=placed,
        out_specs=P("band", "dom", None, None),
        check_vma=False,
    )
```

```python
import functools

import jax
import jax.numpy as jnp
from jax import lax
from jax.experimental import pallas as pl
from jax.experimental.pallas import tpu as pltpu
from jax.sharding import PartitionSpec as P

SX = 8
SY = 16
SZ = 16
DEGREE = 3
LANES = 128
ROWS = 8
TILES = SX * SY * SZ // LANES
HALVES = SY // ROWS

STENCIL_WEIGHTS = (
    -5369.0 / 1800.0,
    12.0 / 7.0,
    -15.0 / 56.0,
    10.0 / 189.0,
    -1.0 / 112.0,
    2.0 / 1925.0,
    -1.0 / 16632.0,
)
REACH = len(STENCIL_WEIGHTS) - 1
LOWER_EDGE = 3.0
UPPER_EDGE = 30.0
ANCHOR_POINT = 0.5
HALF_WIDTH = (UPPER_EDGE - LOWER_EDGE) / 2.0
CENTRE = (UPPER_EDGE + LOWER_EDGE) / 2.0
SIGMA_FIRST = HALF_WIDTH / (ANCHOR_POINT - CENTRE)
COPIES = 4
FIRST_CHUNK = 1


def step_factors():
    sigma_now = SIGMA_FIRST
    factors = [(SIGMA_FIRST / HALF_WIDTH, 0.0)]
    for _ in range(2, DEGREE + 1):
        sigma_next = 1.0 / (2.0 / SIGMA_FIRST - sigma_now)
        factors.append((2.0 * sigma_next / HALF_WIDTH, sigma_now * sigma_next))
        sigma_now = sigma_next
    return factors


def iota(shape, dim):
    return lax.broadcasted_iota(jnp.int32, shape, dim)


def fold_rows(blocks):
    row = iota((ROWS, LANES), 0)
    distance = 1
    while len(blocks) > 1:
        first = (row // distance) % 2 == 0
        blocks = [
            jnp.where(first, a, b) + pltpu.roll(jnp.where(first, b, a), distance, 0)
            for a, b in zip(blocks[::2], blocks[1::2])
        ]
        distance *= 2
    return blocks[0]


def choose(masks, values):
    result = values[-1]
    for mask, value in zip(masks[:-1], values[:-1]):
        result = jnp.where(mask, value, result)
    return result


def pack_plane(first_tile, tiles, proj_ref, out_ref):
    groups = proj_ref.shape[0] // ROWS
    row = iota((ROWS, LANES), 0)
    block = iota((ROWS, LANES), 1) // SZ
    apart = (row - block + ROWS) % ROWS
    block_is = [block == b for b in range(ROWS)]
    row_is = [row == r for r in range(ROWS)]
    apart_is = [apart == d for d in range(ROWS)]

    def one(index, carry):
        tile, group = index // groups, index % groups
        cells = pl.ds(pl.multiple_of((first_tile + tile) * LANES, LANES), LANES)
        given = [proj_ref[group * ROWS + u, :, cells] for u in range(ROWS)]
        by_lane = []
        for d in range(ROWS):
            mixed = choose(block_is, [given[(b - d) % ROWS] for b in range(ROWS)])
            by_lane.append(pltpu.roll(mixed, (LANES - d * SZ) % LANES, 1) if d else mixed)
        by_row = []
        for e in range(ROWS):
            mixed = choose(apart_is, [by_lane[(d + e) % ROWS] for d in range(ROWS)])
            by_row.append(pltpu.roll(mixed, e, 0) if e else mixed)
        for p in range(ROWS):
            at = pl.ds(pl.multiple_of((index * ROWS + p) * ROWS, ROWS), ROWS)
            out_ref[at, :] = choose(row_is, [by_row[(j - p) % ROWS] for j in range(ROWS)])
        return carry

    lax.fori_loop(0, tiles * groups, one, 0)


def halves_of(value):
    high = value.astype(jnp.bfloat16)
    return high, (value - high.astype(jnp.float32)).astype(jnp.bfloat16)


def thirds_of(value):
    rest, parts = value, []
    for _ in range(3):
        high = rest.astype(jnp.bfloat16).astype(jnp.float32)
        parts.append(high)
        rest = rest - high
    return jnp.concatenate(parts, axis=0).astype(jnp.bfloat16)


def sum_thirds(value):
    return value[:ROWS] + value[ROWS : 2 * ROWS] + value[2 * ROWS :]


def table_kernel(atom_row_ref, member_ref, along_z_ref, along_y_ref):
    atoms = iota(member_ref.shape, 0)
    member_ref[...] = (atoms == atom_row_ref[...]).astype(jnp.float32).astype(jnp.bfloat16)
    high, low = halves_of(band_matrix(LANES, LANES, 3.0 * STENCIL_WEIGHTS[0]))
    along_z_ref[...] = jnp.concatenate([high, low, high], axis=0)
    high, low = halves_of(band_matrix(along_y_ref.shape[0], SY, 0.0))
    along_y_ref[...] = jnp.concatenate([high, high, low], axis=1)


def total_of(products):
    while len(products) > 1:
        pairs = [a + b for a, b in zip(products[::2], products[1::2])]
        products = pairs + products[len(pairs) * 2 :]
    return products[0]


def values_of(ref, base, groups, half, group, p):
    at = base + ((half * groups + group) * ROWS + p) * ROWS
    return ref[at : at + ROWS, :]


def project(field, chunks, corner_ref, flat_ref, start_ref=None):
    groups = flat_ref.shape[0]
    lane_block = iota((ROWS, LANES), 1) // SZ

    def one(group, carry):
        corners = [corner_ref[0, group * ROWS + u] for u in range(ROWS)]
        shifts = [
            lax.rem(LANES + u * SZ - corner_ref[2, group * ROWS + u], LANES) for u in range(ROWS)
        ]
        sums = [[] for _ in range(ROWS)]
        for plane, ref, base in chunks:
            for half in range(HALVES):
                box = None
                for u in range(ROWS):
                    turned = pltpu.roll(field(corners[u] + plane, half), shifts[u], 1)
                    box = turned if u == 0 else jnp.where(lane_block == u, turned, box)
                for p in range(ROWS):
                    sums[p].append(values_of(ref, base, groups, half, group, p) * box)
        flat = fold_rows([total_of(products) for products in sums])
        flat_ref[group] = flat if start_ref is None else flat + start_ref[group]
        return carry

    for group in range(groups):
        one(group, 0)


def sum_atoms(flat_ref, member_ref):
    flat = jnp.concatenate([flat_ref[g] for g in range(flat_ref.shape[0])], axis=1)
    return sum_thirds(
        lax.dot_general(
            thirds_of(flat), member_ref[...], (((1,), (1,)), ((), ())),
            preferred_element_type=jnp.float32,
        )
    )


def deposit(scaled, chunks, corner_ref, member_ref, flat_ref, box_ref, parts_ref):
    groups = flat_ref.shape[0]
    copies = parts_ref.shape[0]
    lane_block = iota((ROWS, LANES), 1) // SZ
    flat = sum_thirds(
        jnp.dot(thirds_of(scaled), member_ref[...], preferred_element_type=jnp.float32)
    )
    for g in range(groups):
        flat_ref[g] = flat[:, g * LANES : (g + 1) * LANES]
    parts_ref[...] = jnp.zeros(parts_ref.shape, jnp.float32)

    def one(group, carry):
        factors = [
            jnp.broadcast_to(flat_ref[group, pl.ds(p, 1), :], (ROWS, LANES)) for p in range(ROWS)
        ]
        for plane, ref, base in chunks:
            for half in range(HALVES):
                box_ref[plane * HALVES + half] = total_of(
                    [
                        values_of(ref, base, groups, half, group, p) * factors[p]
                        for p in range(ROWS)
                    ]
                )
        for u in range(ROWS):
            slot = group * ROWS + u
            planes = pl.ds(corner_ref[0, slot], SX)
            shift = lax.rem(LANES + corner_ref[2, slot] - u * SZ, LANES)
            for half in range(HALVES):
                at = (u % copies, planes, pl.ds(half * ROWS, ROWS), slice(None))
                added = [
                    pltpu.roll(
                        jnp.where(lane_block == u, box_ref[x * HALVES + half], 0.0), shift, 1
                    )
                    for x in range(SX)
                ]
                parts_ref[at] = parts_ref[at] + jnp.stack(added)
        return carry

    for group in range(groups):
        one(group, 0)


def band_matrix(size, block, centre):
    row = iota((size, size), 0)
    column = iota((size, size), 1)
    apart = jnp.abs(row - column)
    table = jnp.where(apart == 0, centre, 0.0)
    for k in range(1, REACH + 1):
        table = jnp.where(apart == k, STENCIL_WEIGHTS[k], table)
    return jnp.where(row // block == column // block, table, 0.0)


def laplacian(padded_ref, extent, along_z_ref, along_y_ref):
    inner = padded_ref[REACH : REACH + extent]
    high, low = halves_of(inner.reshape(extent * SY, LANES))
    along_z = jnp.dot(
        jnp.concatenate([high, high, low], axis=1), along_z_ref[...],
        preferred_element_type=jnp.float32,
    )
    along_y = jnp.dot(
        along_y_ref[...], jnp.concatenate([high, low, high], axis=0),
        preferred_element_type=jnp.float32,
    )
    total = (along_z + along_y).reshape(inner.shape)
    for k in range(1, REACH + 1):
        total = total + STENCIL_WEIGHTS[k] * (
            padded_ref[REACH + k : REACH + k + extent] + padded_ref[REACH - k : REACH - k + extent]
        )
    return total


HALO_ROWS = REACH * SY


def to_rows(table):
    blocks = [table[:, at : at + LANES] for at in range(0, table.shape[1], LANES)]
    return jnp.concatenate(blocks, axis=0)


def from_rows(rows):
    blocks = [rows[at : at + ROWS] for at in range(0, rows.shape[0], ROWS)]
    return jnp.concatenate(blocks, axis=1)


def write_halos(field_ref, odd, mate_ref, cross_ref):
    extent = field_ref.shape[0]
    mate_start = (1 - odd) * (extent - REACH)
    cross_start = odd * (extent - REACH)
    for start, ref in ((mate_start, mate_ref), (cross_start, cross_ref)):
        ref[:HALO_ROWS] = field_ref[pl.ds(start, REACH)].reshape(HALO_ROWS, LANES)


def all_planes(ref):
    rows = ref.shape[0] // SX
    return [(x, ref, x * rows) for x in range(SX)]


def some_planes(where_ref, first, refs):
    return [(where_ref[FIRST_CHUNK + first + i], ref, 0) for i, ref in enumerate(refs)]


def field_reader(ref):
    return lambda x, half: ref[x, pl.ds(half * ROWS, ROWS), :]


def halo_kernel(where_ref, field_ref, mate_ref, cross_ref):
    write_halos(field_ref, where_ref[0], mate_ref, cross_ref)


def low_kernel(where_ref, field_ref, proj_ref, laden_ref, mate_ref, cross_ref):
    window = field_ref[pl.ds(where_ref[FIRST_CHUNK + 2], REACH)]
    laden_ref[laden_ref.shape[0] - HALO_ROWS :] = window.reshape(HALO_ROWS, LANES)
    write_halos(field_ref, where_ref[0], mate_ref, cross_ref)
    pack_plane(0, HALVES, proj_ref, laden_ref)


def above_kernel(corner_ref, own_laden_ref, high_ref, laden_ref, flat_ref, on_ref):
    rows = on_ref.shape[0]
    on_ref[...] = laden_ref[:rows]

    def field(x, half):
        return laden_ref[pl.ds(pl.multiple_of(rows + x * SY + half * ROWS, ROWS), ROWS), :]

    project(field, [(0, own_laden_ref, 0), (1, high_ref, 0)], corner_ref, flat_ref)


def hand_on_kernel(given_ref, out_ref):
    out_ref[...] = given_ref[...]


def near_kernel(corner_ref, where_ref, field_ref, low_ref, high_ref, *refs):
    chunks = some_planes(where_ref, 0, [low_ref, high_ref]) + some_planes(where_ref, 4, refs[:-1])
    project(field_reader(field_ref), chunks, corner_ref, refs[-1])


def write_table(flat_ref, member_ref, energy_ref, out_ref):
    sums = sum_atoms(flat_ref, member_ref)
    out_ref[...] = jnp.concatenate([to_rows(sums), to_rows(energy_ref[...])], axis=0)


def last_part_kernel(corner_ref, where_ref, member_ref, energy_ref, field_ref, near_ref,
                     returned_ref, far_ref, out_ref, flat_ref):
    flat_ref[...] = near_ref[...] + returned_ref[...]
    chunks = some_planes(where_ref, 7, [far_ref])
    project(field_reader(field_ref), chunks, corner_ref, flat_ref, flat_ref)
    write_table(flat_ref, member_ref, energy_ref, out_ref)


def whole_pack_kernel(proj_ref, out_ref):
    pack_plane(0, proj_ref.shape[2] // LANES, proj_ref, out_ref)


def high_kernel(proj_ref, out_ref):
    pack_plane(HALVES, HALVES, proj_ref, out_ref)


def whole_sums_kernel(corner_ref, member_ref, energy_ref, field_ref, whole_ref, out_ref, flat_ref):
    project(field_reader(field_ref), all_planes(whole_ref), corner_ref, flat_ref)
    write_table(flat_ref, member_ref, energy_ref, out_ref)


def step_kernel(index, chunk_count, corner_ref, where_ref, member_ref, along_z_ref, along_y_ref,
                field_ref, potential_ref, mate_ref, cross_ref, *refs):
    factors = step_factors()
    is_first, is_last = index == 0, index + 1 == len(factors)
    refs = list(refs)
    odd = where_ref[0]
    own_ref, far_ref = refs.pop(0), refs.pop(0)
    if is_first:
        table = from_rows(own_ref[...] + refs.pop(0)[...] + far_ref[...])
    else:
        table = from_rows(own_ref[HALO_ROWS:] + cross_ref[HALO_ROWS:] + far_ref[...])
    if chunk_count > 1:
        chunks = some_planes(where_ref, 0, refs[:chunk_count])
    else:
        chunks = all_planes(refs[0])
    refs = refs[chunk_count:]
    energy_ref = None if is_first else refs.pop(0)
    before_ref = None if is_first else refs.pop(0)
    next_ref = refs.pop(0)
    if not is_last:
        next_mate_ref, next_cross_ref = refs.pop(0), refs.pop(0)
    if is_first:
        energy_ref = refs.pop(0)
    flat_ref, box_ref, parts_ref, padded_ref = refs
    extent = field_ref.shape[0]
    if is_first:
        atoms = table.shape[1] // 2
        energy_ref[...] = table[:, atoms:]
        table = table[:, :atoms]
    scaled = table * energy_ref[...]
    deposit(scaled, chunks, corner_ref, member_ref, flat_ref, box_ref, parts_ref)

    cells = field_ref[...]
    padded_ref[REACH : REACH + extent] = cells
    mate_at = (1 - odd) * (extent + REACH)
    cross_at = odd * (extent + REACH)
    padded_ref[pl.ds(mate_at, REACH)] = mate_ref[:HALO_ROWS].reshape(REACH, SY, LANES)
    padded_ref[pl.ds(cross_at, REACH)] = cross_ref[:HALO_ROWS].reshape(REACH, SY, LANES)
    value = -0.5 * laplacian(padded_ref, extent, along_z_ref, along_y_ref) + (potential_ref[...] - CENTRE) * cells
    for u in range(parts_ref.shape[0]):
        value = value + parts_ref[u]
    value = factors[index][0] * value
    if not is_first:
        value = value - factors[index][1] * before_ref[...]
    next_ref[...] = value
    if not is_last:
        project(field_reader(next_ref), chunks, corner_ref, flat_ref)
        sums = sum_atoms(flat_ref, member_ref)
        write_halos(next_ref, odd, next_mate_ref, next_cross_ref)
        next_mate_ref[HALO_ROWS:] = to_rows(sums)
        next_cross_ref[HALO_ROWS:] = to_rows(sums)


VMEM = pl.BlockSpec(memory_space=pltpu.VMEM)
SMEM = pl.BlockSpec(memory_space=pltpu.SMEM)
ANY = pl.BlockSpec(memory_space=pl.ANY)


def swap(values, axis, first):
    count = lax.axis_size(axis)
    pairs = []
    for i in range(first, count - 1, 2):
        pairs += [(i, i + 1), (i + 1, i)]
    return lax.ppermute(values, axis, pairs)


def turn(values, axis, step):
    count = lax.axis_size(axis)
    return lax.ppermute(values, axis, [(i, (i + step) % count) for i in range(count)])


def on_device(wave_block, potential, projectors, kb_energy, slot_atom, slot_corner):
    bands, planes, cells_y, cells_z = wave_block.shape
    assert bands == 1 and cells_y == SY and cells_z == LANES
    slots, proj_count = projectors.shape[:2]
    atom_own = kb_energy.shape[0]
    atoms = atom_own * lax.axis_size("dom")
    groups = slots // ROWS
    tiles = projectors.shape[2] // LANES
    assert proj_count == ROWS and slots % ROWS == 0
    place = lax.axis_index("dom")
    field = wave_block[0]

    def shaped(*shape):
        return jax.ShapeDtypeStruct(shape, jnp.float32)

    def call(kernel, name, out_shape, scalars, operands, scratch, after=()):
        inputs = len(scalars) + len(operands)

        def body(*refs):
            kernel(*refs[:inputs], *refs[inputs + len(after) :])

        return pl.pallas_call(
            body,
            out_shape=out_shape,
            in_specs=[SMEM] * len(scalars) + [VMEM] * len(operands) + [ANY] * len(after),
            out_specs=jax.tree.map(lambda _: VMEM, out_shape),
            scratch_shapes=[pltpu.VMEM(shape, jnp.float32) for shape in scratch],
            compiler_params=pltpu.CompilerParams(vmem_limit_bytes=16 * 2**20),
            cost_estimate=pl.CostEstimate(flops=0, bytes_accessed=0, transcendentals=0),
            name=name,
        )(*scalars, *operands, *after)

    atom_row = jnp.repeat(slot_atom, SZ)[None, :]
    own_atoms = (jnp.arange(atoms) // atom_own) == place
    energy = jnp.where(own_atoms[None, :], jnp.tile(kb_energy.T, (1, atoms // atom_own)), 0.0)
    flat = (groups, ROWS, LANES)
    boxes = (TILES, ROWS, LANES)
    parts = (COPIES, planes, SY, LANES)
    padded = (planes + 2 * REACH, SY, LANES)
    table_rows = ROWS * atoms // LANES
    sends = [shaped(HALO_ROWS + table_rows, LANES)] * 2

    flat = (groups, ROWS, LANES)
    boxes = (TILES, ROWS, LANES)
    parts = (COPIES, planes, SY, LANES)
    padded = (planes + 2 * REACH, SY, LANES)
    table_rows = ROWS * atoms // LANES
    sends = [shaped(HALO_ROWS + table_rows, LANES)] * 2

    def pack(first_tile, count, after=()):
        return call(
            functools.partial(pack_kernel, first_tile), "pack_projectors",
            shaped(count, groups, ROWS, ROWS, LANES), [], [projectors], [], after,
        )

    tables = call(
        table_kernel, "tables",
        [
            jax.ShapeDtypeStruct(shape, jnp.bfloat16)
            for shape in (
                (atoms, slots * SZ), (3 * LANES, LANES), (planes * SY, 3 * planes * SY)
            )
        ],
        [], [atom_row], [],
    )
    odd = (place % 2).astype(jnp.int32)
    halos = [shaped(HALO_ROWS, LANES)] * 2
    if lax.axis_size("band") == 4 and tiles == 2 * HALVES:
        at = lax.axis_index("band").astype(jnp.int32)
        owners = [at, (at + 1) % 4, (at + 3) % 4, (at + 2) % 4]
        where = jnp.stack([odd] + [2 * part + h for part in owners for h in range(2)])
        rows = HALVES * groups * ROWS * ROWS
        plane = shaped(rows, LANES)
        low, mate, cross = call(
            low_kernel, "pack_low", [shaped(rows + HALO_ROWS, LANES)] + halos,
            [where], [field, projectors], [],
        )
        below_low = turn(low, "band", 1)
        high = call(high_kernel, "pack_high", plane, [], [projectors], [], [low])
        below_high = turn(high, "band", 1)
        returned, on_low = call(
            above_kernel, "project_above", [shaped(*flat), plane], [slot_corner],
            [low, high, below_low], [],
        )
        returned = turn(returned, "band", -1)
        far_low = turn(on_low, "band", 1)

        def hand_on(values, *after):
            return call(hand_on_kernel, "hand_on", plane, [], [values], [], after)

        on_high = hand_on(below_high, on_low, returned)
        far_high = turn(on_high, "band", 1)
        on_far_low = hand_on(far_low, on_high)
        above_low = turn(on_far_low, "band", 1)
        near = call(
            near_kernel, "project_near", shaped(*flat), [slot_corner, where],
            [field, low, high, below_low, below_high, far_low], [],
        )
        on_far_high = hand_on(far_high, on_far_low, near, tables[0], energy)
        above_high = turn(on_far_high, "band", 1)
        own = call(
            last_part_kernel, "first_sums", shaped(2 * table_rows, LANES), [slot_corner, where],
            [tables[0], energy, field, near, returned, far_high], [flat],
        )
        chunks = [low, high, above_low, above_high, below_low, below_high, far_low, far_high]
    else:
        where = odd[None]
        mate, cross = call(halo_kernel, "cut_halos", halos, [where], [field], [])
        packed = call(
            whole_pack_kernel, "pack_projectors", shaped(tiles * groups * ROWS * ROWS, LANES),
            [], [projectors], [],
        )
        chunks = [lax.all_gather(packed, "band", axis=0, tiled=True)]
        own = call(
            whole_sums_kernel, "first_sums", shaped(2 * table_rows, LANES), [slot_corner],
            [tables[0], energy, field, *chunks], [flat],
        )
    mate, cross = swap(mate, "dom", 0), swap(cross, "dom", 1)
    own = own + swap(own, "dom", 0)
    other = swap(own, "dom", 1)
    far = swap(other, "dom", 0)
    before = None
    for index in range(DEGREE):
        if index > 0:
            to_mate, to_cross = sent
            mate = swap(to_mate, "dom", 0)
            own = to_cross.at[HALO_ROWS:].add(mate[HALO_ROWS:])
            cross = swap(own, "dom", 1)
            far = swap(cross[HALO_ROWS:], "dom", 0)
        operands = [*tables, field, potential, mate, cross, own, far]
        if index == 0:
            operands.append(other)
        operands += chunks
        out_shape = [shaped(planes, SY, LANES)]
        if index > 0:
            operands += [energy, before]
        if index + 1 < DEGREE:
            out_shape += sends
        if index == 0:
            out_shape += [shaped(ROWS, atoms)]
        result = call(
            functools.partial(step_kernel, index, len(chunks)), f"filter_step_{index + 1}",
            out_shape, [slot_corner, where], operands, [flat, boxes, parts, padded],
        )
        before, field = field, result[0]
        sent = result[1:3]
        if index == 0:
            energy = result[3]
    return field[None]


def solution(mesh):
    placed = (
        P("band", "dom", None, None),
        P("dom", None, None),
        P("dom", None, "band"),
        P("dom", None),
        P("dom"),
        P(None, "dom"),
    )
    return jax.shard_map(
        on_device,
        mesh=mesh,
        in_specs=placed,
        out_specs=P("band", "dom", None, None),
        check_vma=False,
    )
```

```python
import functools

import jax
import jax.numpy as jnp
from jax import lax
from jax.experimental import pallas as pl
from jax.experimental.pallas import tpu as pltpu
from jax.sharding import PartitionSpec as P

SX = 8
SY = 16
SZ = 16
DEGREE = 3
LANES = 128
ROWS = 8
TILES = SX * SY * SZ // LANES
HALVES = SY // ROWS

STENCIL_WEIGHTS = (
    -5369.0 / 1800.0,
    12.0 / 7.0,
    -15.0 / 56.0,
    10.0 / 189.0,
    -1.0 / 112.0,
    2.0 / 1925.0,
    -1.0 / 16632.0,
)
REACH = len(STENCIL_WEIGHTS) - 1
LOWER_EDGE = 3.0
UPPER_EDGE = 30.0
ANCHOR_POINT = 0.5
HALF_WIDTH = (UPPER_EDGE - LOWER_EDGE) / 2.0
CENTRE = (UPPER_EDGE + LOWER_EDGE) / 2.0
SIGMA_FIRST = HALF_WIDTH / (ANCHOR_POINT - CENTRE)
COPIES = 4
FIRST_CHUNK = 1


def step_factors():
    sigma_now = SIGMA_FIRST
    factors = [(SIGMA_FIRST / HALF_WIDTH, 0.0)]
    for _ in range(2, DEGREE + 1):
        sigma_next = 1.0 / (2.0 / SIGMA_FIRST - sigma_now)
        factors.append((2.0 * sigma_next / HALF_WIDTH, sigma_now * sigma_next))
        sigma_now = sigma_next
    return factors


def iota(shape, dim):
    return lax.broadcasted_iota(jnp.int32, shape, dim)


def fold_rows(blocks):
    row = iota((ROWS, LANES), 0)
    distance = 1
    while len(blocks) > 1:
        first = (row // distance) % 2 == 0
        blocks = [
            jnp.where(first, a, b) + pltpu.roll(jnp.where(first, b, a), distance, 0)
            for a, b in zip(blocks[::2], blocks[1::2])
        ]
        distance *= 2
    return blocks[0]


def choose(masks, values):
    result = values[-1]
    for mask, value in zip(masks[:-1], values[:-1]):
        result = jnp.where(mask, value, result)
    return result


def pack_plane(first_tile, tiles, proj_ref, out_ref):
    groups = proj_ref.shape[0] // ROWS
    row = iota((ROWS, LANES), 0)
    block = iota((ROWS, LANES), 1) // SZ
    apart = (row - block + ROWS) % ROWS
    block_is = [block == b for b in range(ROWS)]
    row_is = [row == r for r in range(ROWS)]
    apart_is = [apart == d for d in range(ROWS)]

    def one(index, carry):
        tile, group = index // groups, index % groups
        cells = pl.ds(pl.multiple_of((first_tile + tile) * LANES, LANES), LANES)
        given = [proj_ref[group * ROWS + u, :, cells] for u in range(ROWS)]
        by_lane = []
        for d in range(ROWS):
            mixed = choose(block_is, [given[(b - d) % ROWS] for b in range(ROWS)])
            by_lane.append(pltpu.roll(mixed, (LANES - d * SZ) % LANES, 1) if d else mixed)
        by_row = []
        for e in range(ROWS):
            mixed = choose(apart_is, [by_lane[(d + e) % ROWS] for d in range(ROWS)])
            by_row.append(pltpu.roll(mixed, e, 0) if e else mixed)
        for p in range(ROWS):
            at = pl.ds(pl.multiple_of((index * ROWS + p) * ROWS, ROWS), ROWS)
            out_ref[at, :] = choose(row_is, [by_row[(j - p) % ROWS] for j in range(ROWS)])
        return carry

    lax.fori_loop(0, tiles * groups, one, 0)


def halves_of(value):
    high = value.astype(jnp.bfloat16)
    return high, (value - high.astype(jnp.float32)).astype(jnp.bfloat16)


def thirds_of(value):
    rest, parts = value, []
    for _ in range(3):
        high = rest.astype(jnp.bfloat16).astype(jnp.float32)
        parts.append(high)
        rest = rest - high
    return jnp.concatenate(parts, axis=0).astype(jnp.bfloat16)


def sum_thirds(value):
    return value[:ROWS] + value[ROWS : 2 * ROWS] + value[2 * ROWS :]


def table_kernel(atom_row_ref, member_ref, along_z_ref, along_y_ref):
    atoms = iota(member_ref.shape, 0)
    member_ref[...] = (atoms == atom_row_ref[...]).astype(jnp.float32).astype(jnp.bfloat16)
    high, low = halves_of(band_matrix(LANES, LANES, 3.0 * STENCIL_WEIGHTS[0]))
    along_z_ref[...] = jnp.concatenate([high, low, high], axis=0)
    high, low = halves_of(band_matrix(along_y_ref.shape[0], SY, 0.0))
    along_y_ref[...] = jnp.concatenate([high, high, low], axis=1)


def total_of(products):
    while len(products) > 1:
        pairs = [a + b for a, b in zip(products[::2], products[1::2])]
        products = pairs + products[len(pairs) * 2 :]
    return products[0]


def values_of(ref, base, groups, half, group, p):
    at = base + ((half * groups + group) * ROWS + p) * ROWS
    return ref[at : at + ROWS, :]


def project(field, chunks, corner_ref, flat_ref, start_ref=None):
    groups = flat_ref.shape[0]
    lane_block = iota((ROWS, LANES), 1) // SZ

    def one(group, carry):
        corners = [corner_ref[0, group * ROWS + u] for u in range(ROWS)]
        shifts = [
            lax.rem(LANES + u * SZ - corner_ref[2, group * ROWS + u], LANES) for u in range(ROWS)
        ]
        sums = [[] for _ in range(ROWS)]
        for plane, ref, base in chunks:
            for half in range(HALVES):
                box = None
                for u in range(ROWS):
                    turned = pltpu.roll(field(corners[u] + plane, half), shifts[u], 1)
                    box = turned if u == 0 else jnp.where(lane_block == u, turned, box)
                for p in range(ROWS):
                    sums[p].append(values_of(ref, base, groups, half, group, p) * box)
        flat = fold_rows([total_of(products) for products in sums])
        flat_ref[group] = flat if start_ref is None else flat + start_ref[group]
        return carry

    for group in range(groups):
        one(group, 0)


def sum_atoms(flat_ref, member_ref):
    flat = jnp.concatenate([flat_ref[g] for g in range(flat_ref.shape[0])], axis=1)
    return sum_thirds(
        lax.dot_general(
            thirds_of(flat), member_ref[...], (((1,), (1,)), ((), ())),
            preferred_element_type=jnp.float32,
        )
    )


def deposit(scaled, chunks, corner_ref, member_ref, flat_ref, box_ref, parts_ref):
    groups = flat_ref.shape[0]
    copies = parts_ref.shape[0]
    lane_block = iota((ROWS, LANES), 1) // SZ
    flat = sum_thirds(
        jnp.dot(thirds_of(scaled), member_ref[...], preferred_element_type=jnp.float32)
    )
    for g in range(groups):
        flat_ref[g] = flat[:, g * LANES : (g + 1) * LANES]
    parts_ref[...] = jnp.zeros(parts_ref.shape, jnp.float32)

    def one(group, carry):
        factors = [
            jnp.broadcast_to(flat_ref[group, pl.ds(p, 1), :], (ROWS, LANES)) for p in range(ROWS)
        ]
        for plane, ref, base in chunks:
            for half in range(HALVES):
                box_ref[plane * HALVES + half] = total_of(
                    [
                        values_of(ref, base, groups, half, group, p) * factors[p]
                        for p in range(ROWS)
                    ]
                )
        for u in range(ROWS):
            slot = group * ROWS + u
            planes = pl.ds(corner_ref[0, slot], SX)
            shift = lax.rem(LANES + corner_ref[2, slot] - u * SZ, LANES)
            for half in range(HALVES):
                at = (u % copies, planes, pl.ds(half * ROWS, ROWS), slice(None))
                added = [
                    pltpu.roll(
                        jnp.where(lane_block == u, box_ref[x * HALVES + half], 0.0), shift, 1
                    )
                    for x in range(SX)
                ]
                parts_ref[at] = parts_ref[at] + jnp.stack(added)
        return carry

    for group in range(groups):
        one(group, 0)


def band_matrix(size, block, centre):
    row = iota((size, size), 0)
    column = iota((size, size), 1)
    apart = jnp.abs(row - column)
    table = jnp.where(apart == 0, centre, 0.0)
    for k in range(1, REACH + 1):
        table = jnp.where(apart == k, STENCIL_WEIGHTS[k], table)
    return jnp.where(row // block == column // block, table, 0.0)


def laplacian(padded_ref, extent, along_z_ref, along_y_ref):
    inner = padded_ref[REACH : REACH + extent]
    high, low = halves_of(inner.reshape(extent * SY, LANES))
    along_z = jnp.dot(
        jnp.concatenate([high, high, low], axis=1), along_z_ref[...],
        preferred_element_type=jnp.float32,
    )
    along_y = jnp.dot(
        along_y_ref[...], jnp.concatenate([high, low, high], axis=0),
        preferred_element_type=jnp.float32,
    )
    total = (along_z + along_y).reshape(inner.shape)
    for k in range(1, REACH + 1):
        total = total + STENCIL_WEIGHTS[k] * (
            padded_ref[REACH + k : REACH + k + extent] + padded_ref[REACH - k : REACH - k + extent]
        )
    return total


HALO_ROWS = REACH * SY


def to_rows(table):
    blocks = [table[:, at : at + LANES] for at in range(0, table.shape[1], LANES)]
    return jnp.concatenate(blocks, axis=0)


def from_rows(rows):
    blocks = [rows[at : at + ROWS] for at in range(0, rows.shape[0], ROWS)]
    return jnp.concatenate(blocks, axis=1)


def write_halos(field_ref, odd, mate_ref, cross_ref):
    extent = field_ref.shape[0]
    mate_start = (1 - odd) * (extent - REACH)
    cross_start = odd * (extent - REACH)
    for start, ref in ((mate_start, mate_ref), (cross_start, cross_ref)):
        ref[:HALO_ROWS] = field_ref[pl.ds(start, REACH)].reshape(HALO_ROWS, LANES)


def all_planes(ref):
    rows = ref.shape[0] // SX
    return [(x, ref, x * rows) for x in range(SX)]


def some_planes(where_ref, first, refs):
    return [(where_ref[FIRST_CHUNK + first + i], ref, 0) for i, ref in enumerate(refs)]


def field_reader(ref):
    return lambda x, half: ref[x, pl.ds(half * ROWS, ROWS), :]


def halo_kernel(where_ref, field_ref, mate_ref, cross_ref):
    write_halos(field_ref, where_ref[0], mate_ref, cross_ref)


def low_kernel(where_ref, field_hbm, proj_hbm, laden_ref, mate_ref, cross_ref,
               field_ref, proj_ref, field_sem, proj_sem):
    cells = pl.ds(0, proj_ref.shape[2])
    proj_copy = pltpu.make_async_copy(proj_hbm.at[:, :, cells], proj_ref, proj_sem)
    field_copy = pltpu.make_async_copy(field_hbm, field_ref, field_sem)
    proj_copy.start()
    field_copy.start()
    field_copy.wait()
    window = field_ref[pl.ds(where_ref[FIRST_CHUNK + 2], REACH)]
    laden_ref[laden_ref.shape[0] - HALO_ROWS :] = window.reshape(HALO_ROWS, LANES)
    write_halos(field_ref, where_ref[0], mate_ref, cross_ref)
    proj_copy.wait()
    pack_plane(0, HALVES, proj_ref, laden_ref)


def above_kernel(corner_ref, own_laden_ref, high_ref, laden_ref, flat_ref, on_ref):
    rows = on_ref.shape[0]
    on_ref[...] = laden_ref[:rows]

    def field(x, half):
        return laden_ref[pl.ds(pl.multiple_of(rows + x * SY + half * ROWS, ROWS), ROWS), :]

    project(field, [(0, own_laden_ref, 0), (1, high_ref, 0)], corner_ref, flat_ref)


def hand_on_kernel(given_ref, out_ref):
    out_ref[...] = given_ref[...]


def near_kernel(corner_ref, where_ref, field_ref, low_ref, high_ref, *refs):
    chunks = some_planes(where_ref, 0, [low_ref, high_ref]) + some_planes(where_ref, 4, refs[:-1])
    project(field_reader(field_ref), chunks, corner_ref, refs[-1])


def write_table(flat_ref, member_ref, energy_ref, out_ref):
    sums = sum_atoms(flat_ref, member_ref)
    out_ref[...] = jnp.concatenate([to_rows(sums), to_rows(energy_ref[...])], axis=0)


def last_part_kernel(corner_ref, where_ref, member_ref, energy_ref, field_ref, near_ref,
                     returned_ref, far_ref, out_ref, flat_ref):
    flat_ref[...] = near_ref[...] + returned_ref[...]
    chunks = some_planes(where_ref, 7, [far_ref])
    project(field_reader(field_ref), chunks, corner_ref, flat_ref, flat_ref)
    write_table(flat_ref, member_ref, energy_ref, out_ref)


def whole_pack_kernel(proj_ref, out_ref):
    pack_plane(0, proj_ref.shape[2] // LANES, proj_ref, out_ref)


def high_kernel(proj_ref, out_ref):
    pack_plane(HALVES, HALVES, proj_ref, out_ref)


def whole_sums_kernel(corner_ref, member_ref, energy_ref, field_ref, whole_ref, out_ref, flat_ref):
    project(field_reader(field_ref), all_planes(whole_ref), corner_ref, flat_ref)
    write_table(flat_ref, member_ref, energy_ref, out_ref)


def step_kernel(index, chunk_count, corner_ref, where_ref, member_ref, along_z_ref, along_y_ref,
                field_ref, potential_ref, mate_ref, cross_ref, *refs):
    factors = step_factors()
    is_first, is_last = index == 0, index + 1 == len(factors)
    refs = list(refs)
    odd = where_ref[0]
    own_ref, far_ref = refs.pop(0), refs.pop(0)
    if is_first:
        table = from_rows(own_ref[...] + refs.pop(0)[...] + far_ref[...])
    else:
        table = from_rows(own_ref[HALO_ROWS:] + cross_ref[HALO_ROWS:] + far_ref[...])
    if chunk_count > 1:
        chunks = some_planes(where_ref, 0, refs[:chunk_count])
    else:
        chunks = all_planes(refs[0])
    refs = refs[chunk_count:]
    energy_ref = None if is_first else refs.pop(0)
    before_ref = None if is_first else refs.pop(0)
    next_ref = refs.pop(0)
    if not is_last:
        next_mate_ref, next_cross_ref = refs.pop(0), refs.pop(0)
    if is_first:
        energy_ref = refs.pop(0)
    flat_ref, box_ref, parts_ref, padded_ref = refs
    extent = field_ref.shape[0]
    if is_first:
        atoms = table.shape[1] // 2
        energy_ref[...] = table[:, atoms:]
        table = table[:, :atoms]
    scaled = table * energy_ref[...]
    deposit(scaled, chunks, corner_ref, member_ref, flat_ref, box_ref, parts_ref)

    cells = field_ref[...]
    padded_ref[REACH : REACH + extent] = cells
    mate_at = (1 - odd) * (extent + REACH)
    cross_at = odd * (extent + REACH)
    padded_ref[pl.ds(mate_at, REACH)] = mate_ref[:HALO_ROWS].reshape(REACH, SY, LANES)
    padded_ref[pl.ds(cross_at, REACH)] = cross_ref[:HALO_ROWS].reshape(REACH, SY, LANES)
    value = -0.5 * laplacian(padded_ref, extent, along_z_ref, along_y_ref) + (potential_ref[...] - CENTRE) * cells
    for u in range(parts_ref.shape[0]):
        value = value + parts_ref[u]
    value = factors[index][0] * value
    if not is_first:
        value = value - factors[index][1] * before_ref[...]
    next_ref[...] = value
    if not is_last:
        project(field_reader(next_ref), chunks, corner_ref, flat_ref)
        sums = sum_atoms(flat_ref, member_ref)
        write_halos(next_ref, odd, next_mate_ref, next_cross_ref)
        next_mate_ref[HALO_ROWS:] = to_rows(sums)
        next_cross_ref[HALO_ROWS:] = to_rows(sums)


VMEM = pl.BlockSpec(memory_space=pltpu.VMEM)
SMEM = pl.BlockSpec(memory_space=pltpu.SMEM)
ANY = pl.BlockSpec(memory_space=pl.ANY)
HBM = pl.BlockSpec(memory_space=pltpu.HBM)


def swap(values, axis, first):
    count = lax.axis_size(axis)
    pairs = []
    for i in range(first, count - 1, 2):
        pairs += [(i, i + 1), (i + 1, i)]
    return lax.ppermute(values, axis, pairs)


def turn(values, axis, step):
    count = lax.axis_size(axis)
    return lax.ppermute(values, axis, [(i, (i + step) % count) for i in range(count)])


def on_device(wave_block, potential, projectors, kb_energy, slot_atom, slot_corner):
    bands, planes, cells_y, cells_z = wave_block.shape
    assert bands == 1 and cells_y == SY and cells_z == LANES
    slots, proj_count = projectors.shape[:2]
    atom_own = kb_energy.shape[0]
    atoms = atom_own * lax.axis_size("dom")
    groups = slots // ROWS
    tiles = projectors.shape[2] // LANES
    assert proj_count == ROWS and slots % ROWS == 0
    place = lax.axis_index("dom")
    field = wave_block[0]

    def shaped(*shape):
        return jax.ShapeDtypeStruct(shape, jnp.float32)

    def call(kernel, name, out_shape, scalars, operands, scratch, after=()):
        inputs = len(scalars) + len(operands)

        def body(*refs):
            kernel(*refs[:inputs], *refs[inputs + len(after) :])

        return pl.pallas_call(
            body,
            out_shape=out_shape,
            in_specs=[SMEM] * len(scalars) + [VMEM] * len(operands) + [ANY] * len(after),
            out_specs=jax.tree.map(lambda _: VMEM, out_shape),
            scratch_shapes=[pltpu.VMEM(shape, jnp.float32) for shape in scratch],
            compiler_params=pltpu.CompilerParams(vmem_limit_bytes=16 * 2**20),
            cost_estimate=pl.CostEstimate(flops=0, bytes_accessed=0, transcendentals=0),
            name=name,
        )(*scalars, *operands, *after)

    atom_row = jnp.repeat(slot_atom, SZ)[None, :]
    own_atoms = (jnp.arange(atoms) // atom_own) == place
    energy = jnp.where(own_atoms[None, :], jnp.tile(kb_energy.T, (1, atoms // atom_own)), 0.0)
    flat = (groups, ROWS, LANES)
    boxes = (TILES, ROWS, LANES)
    parts = (COPIES, planes, SY, LANES)
    padded = (planes + 2 * REACH, SY, LANES)
    table_rows = ROWS * atoms // LANES
    sends = [shaped(HALO_ROWS + table_rows, LANES)] * 2

    flat = (groups, ROWS, LANES)
    boxes = (TILES, ROWS, LANES)
    parts = (COPIES, planes, SY, LANES)
    padded = (planes + 2 * REACH, SY, LANES)
    table_rows = ROWS * atoms // LANES
    sends = [shaped(HALO_ROWS + table_rows, LANES)] * 2

    def pack(first_tile, count, after=()):
        return call(
            functools.partial(pack_kernel, first_tile), "pack_projectors",
            shaped(count, groups, ROWS, ROWS, LANES), [], [projectors], [], after,
        )

    tables = call(
        table_kernel, "tables",
        [
            jax.ShapeDtypeStruct(shape, jnp.bfloat16)
            for shape in (
                (atoms, slots * SZ), (3 * LANES, LANES), (planes * SY, 3 * planes * SY)
            )
        ],
        [], [atom_row], [],
    )
    odd = (place % 2).astype(jnp.int32)
    halos = [shaped(HALO_ROWS, LANES)] * 2
    if lax.axis_size("band") == 4 and tiles == 2 * HALVES:
        at = lax.axis_index("band").astype(jnp.int32)
        owners = [at, (at + 1) % 4, (at + 3) % 4, (at + 2) % 4]
        where = jnp.stack([odd] + [2 * part + h for part in owners for h in range(2)])
        rows = HALVES * groups * ROWS * ROWS
        plane = shaped(rows, LANES)
        low, mate, cross = pl.pallas_call(
            low_kernel,
            out_shape=[shaped(rows + HALO_ROWS, LANES)] + halos,
            in_specs=[SMEM, HBM, HBM],
            out_specs=[VMEM] * 3,
            scratch_shapes=[
                pltpu.VMEM(field.shape, jnp.float32),
                pltpu.VMEM((slots, ROWS, HALVES * LANES), jnp.float32),
                pltpu.SemaphoreType.DMA,
                pltpu.SemaphoreType.DMA,
            ],
            compiler_params=pltpu.CompilerParams(vmem_limit_bytes=62 * 2**20),
            cost_estimate=pl.CostEstimate(flops=0, bytes_accessed=0, transcendentals=0),
            name="pack_low",
        )(where, field, projectors)
        mate, cross = swap(mate, "dom", 0), swap(cross, "dom", 1)
        below_low = turn(low, "band", 1)
        high = call(high_kernel, "pack_high", plane, [], [projectors], [], [low])
        below_high = turn(high, "band", 1)
        returned, on_low = call(
            above_kernel, "project_above", [shaped(*flat), plane], [slot_corner],
            [low, high, below_low], [],
        )
        returned = turn(returned, "band", -1)
        far_low = turn(on_low, "band", 1)

        def hand_on(values, *after):
            return call(hand_on_kernel, "hand_on", plane, [], [values], [], after)

        on_high = hand_on(below_high, on_low, returned)
        far_high = turn(on_high, "band", 1)
        on_far_low = hand_on(far_low, on_high)
        above_low = turn(on_far_low, "band", 1)
        near = call(
            near_kernel, "project_near", shaped(*flat), [slot_corner, where],
            [field, low, high, below_low, below_high, far_low], [], [mate, cross],
        )
        on_far_high = hand_on(far_high, on_far_low, near, tables[0], energy)
        above_high = turn(on_far_high, "band", 1)
        own = call(
            last_part_kernel, "first_sums", shaped(2 * table_rows, LANES), [slot_corner, where],
            [tables[0], energy, field, near, returned, far_high], [flat],
        )
        own = own + swap(own, "dom", 0)
        chunks = [low, high, above_low, above_high, below_low, below_high, far_low, far_high]
    else:
        where = odd[None]
        mate, cross = call(halo_kernel, "cut_halos", halos, [where], [field], [])
        packed = call(
            whole_pack_kernel, "pack_projectors", shaped(tiles * groups * ROWS * ROWS, LANES),
            [], [projectors], [],
        )
        chunks = [lax.all_gather(packed, "band", axis=0, tiled=True)]
        own = call(
            whole_sums_kernel, "first_sums", shaped(2 * table_rows, LANES), [slot_corner],
            [tables[0], energy, field, *chunks], [flat],
        )
        mate, cross = swap(mate, "dom", 0), swap(cross, "dom", 1)
        own = own + swap(own, "dom", 0)
    other = swap(own, "dom", 1)
    far = swap(other, "dom", 0)
    before = None
    for index in range(DEGREE):
        if index > 0:
            to_mate, to_cross = sent
            mate = swap(to_mate, "dom", 0)
            own = to_cross.at[HALO_ROWS:].add(mate[HALO_ROWS:])
            cross = swap(own, "dom", 1)
            far = swap(cross[HALO_ROWS:], "dom", 0)
        operands = [*tables, field, potential, mate, cross, own, far]
        if index == 0:
            operands.append(other)
        operands += chunks
        out_shape = [shaped(planes, SY, LANES)]
        if index > 0:
            operands += [energy, before]
        if index + 1 < DEGREE:
            out_shape += sends
        if index == 0:
            out_shape += [shaped(ROWS, atoms)]
        result = call(
            functools.partial(step_kernel, index, len(chunks)), f"filter_step_{index + 1}",
            out_shape, [slot_corner, where], operands, [flat, boxes, parts, padded],
        )
        before, field = field, result[0]
        sent = result[1:3]
        if index == 0:
            energy = result[3]
    return field[None]


def solution(mesh):
    placed = (
        P("band", "dom", None, None),
        P("dom", None, None),
        P("dom", None, "band"),
        P("dom", None),
        P("dom"),
        P(None, "dom"),
    )
    return jax.shard_map(
        on_device,
        mesh=mesh,
        in_specs=placed,
        out_specs=P("band", "dom", None, None),
        check_vma=False,
    )
```

```python
import functools

import jax
import jax.numpy as jnp
from jax import lax
from jax.experimental import pallas as pl
from jax.experimental.pallas import tpu as pltpu
from jax.sharding import PartitionSpec as P

SX = 8
SY = 16
SZ = 16
DEGREE = 3
LANES = 128
ROWS = 8
TILES = SX * SY * SZ // LANES
HALVES = SY // ROWS

STENCIL_WEIGHTS = (
    -5369.0 / 1800.0,
    12.0 / 7.0,
    -15.0 / 56.0,
    10.0 / 189.0,
    -1.0 / 112.0,
    2.0 / 1925.0,
    -1.0 / 16632.0,
)
REACH = len(STENCIL_WEIGHTS) - 1
LOWER_EDGE = 3.0
UPPER_EDGE = 30.0
ANCHOR_POINT = 0.5
HALF_WIDTH = (UPPER_EDGE - LOWER_EDGE) / 2.0
CENTRE = (UPPER_EDGE + LOWER_EDGE) / 2.0
SIGMA_FIRST = HALF_WIDTH / (ANCHOR_POINT - CENTRE)
COPIES = 4
FIRST_CHUNK = 1


def step_factors():
    sigma_now = SIGMA_FIRST
    factors = [(SIGMA_FIRST / HALF_WIDTH, 0.0)]
    for _ in range(2, DEGREE + 1):
        sigma_next = 1.0 / (2.0 / SIGMA_FIRST - sigma_now)
        factors.append((2.0 * sigma_next / HALF_WIDTH, sigma_now * sigma_next))
        sigma_now = sigma_next
    return factors


def iota(shape, dim):
    return lax.broadcasted_iota(jnp.int32, shape, dim)


def fold_rows(blocks):
    row = iota((ROWS, LANES), 0)
    distance = 1
    while len(blocks) > 1:
        first = (row // distance) % 2 == 0
        blocks = [
            jnp.where(first, a, b) + pltpu.roll(jnp.where(first, b, a), distance, 0)
            for a, b in zip(blocks[::2], blocks[1::2])
        ]
        distance *= 2
    return blocks[0]


def choose(masks, values):
    result = values[-1]
    for mask, value in zip(masks[:-1], values[:-1]):
        result = jnp.where(mask, value, result)
    return result


def pack_plane(first_tile, tiles, proj_ref, out_ref):
    groups = proj_ref.shape[0] // ROWS
    row = iota((ROWS, LANES), 0)
    block = iota((ROWS, LANES), 1) // SZ
    apart = (row - block + ROWS) % ROWS
    block_is = [block == b for b in range(ROWS)]
    row_is = [row == r for r in range(ROWS)]
    apart_is = [apart == d for d in range(ROWS)]

    def one(index, carry):
        tile, group = index // groups, index % groups
        cells = pl.ds(pl.multiple_of((first_tile + tile) * LANES, LANES), LANES)
        given = [proj_ref[group * ROWS + u, :, cells] for u in range(ROWS)]
        by_lane = []
        for d in range(ROWS):
            mixed = choose(block_is, [given[(b - d) % ROWS] for b in range(ROWS)])
            by_lane.append(pltpu.roll(mixed, (LANES - d * SZ) % LANES, 1) if d else mixed)
        by_row = []
        for e in range(ROWS):
            mixed = choose(apart_is, [by_lane[(d + e) % ROWS] for d in range(ROWS)])
            by_row.append(pltpu.roll(mixed, e, 0) if e else mixed)
        for p in range(ROWS):
            at = pl.ds(pl.multiple_of((index * ROWS + p) * ROWS, ROWS), ROWS)
            out_ref[at, :] = choose(row_is, [by_row[(j - p) % ROWS] for j in range(ROWS)])
        return carry

    lax.fori_loop(0, tiles * groups, one, 0)


def halves_of(value):
    high = value.astype(jnp.bfloat16)
    return high, (value - high.astype(jnp.float32)).astype(jnp.bfloat16)


def thirds_of(value):
    rest, parts = value, []
    for _ in range(3):
        high = rest.astype(jnp.bfloat16).astype(jnp.float32)
        parts.append(high)
        rest = rest - high
    return jnp.concatenate(parts, axis=0).astype(jnp.bfloat16)


def sum_thirds(value):
    return value[:ROWS] + value[ROWS : 2 * ROWS] + value[2 * ROWS :]


def table_kernel(atom_row_ref, member_ref, along_z_ref, along_y_ref):
    atoms = iota(member_ref.shape, 0)
    member_ref[...] = (atoms == atom_row_ref[...]).astype(jnp.float32).astype(jnp.bfloat16)
    high, low = halves_of(band_matrix(LANES, LANES, 3.0 * STENCIL_WEIGHTS[0]))
    along_z_ref[...] = jnp.concatenate([high, low, high], axis=0)
    high, low = halves_of(band_matrix(along_y_ref.shape[0], SY, 0.0))
    along_y_ref[...] = jnp.concatenate([high, high, low], axis=1)


def total_of(products):
    while len(products) > 1:
        pairs = [a + b for a, b in zip(products[::2], products[1::2])]
        products = pairs + products[len(pairs) * 2 :]
    return products[0]


def values_of(ref, base, groups, half, group, p):
    at = base + ((half * groups + group) * ROWS + p) * ROWS
    return ref[at : at + ROWS, :]


def project(field, chunks, corner_ref, flat_ref, start_ref=None):
    groups = flat_ref.shape[0]
    lane_block = iota((ROWS, LANES), 1) // SZ

    def one(group, carry):
        corners = [corner_ref[0, group * ROWS + u] for u in range(ROWS)]
        shifts = [
            lax.rem(LANES + u * SZ - corner_ref[2, group * ROWS + u], LANES) for u in range(ROWS)
        ]
        sums = [[] for _ in range(ROWS)]
        for plane, ref, base in chunks:
            for half in range(HALVES):
                box = None
                for u in range(ROWS):
                    turned = pltpu.roll(field(corners[u] + plane, half), shifts[u], 1)
                    box = turned if u == 0 else jnp.where(lane_block == u, turned, box)
                for p in range(ROWS):
                    sums[p].append(values_of(ref, base, groups, half, group, p) * box)
        flat = fold_rows([total_of(products) for products in sums])
        flat_ref[group] = flat if start_ref is None else flat + start_ref[group]
        return carry

    for group in range(groups):
        one(group, 0)


def sum_atoms(flat_ref, member_ref):
    flat = jnp.concatenate([flat_ref[g] for g in range(flat_ref.shape[0])], axis=1)
    return sum_thirds(
        lax.dot_general(
            thirds_of(flat), member_ref[...], (((1,), (1,)), ((), ())),
            preferred_element_type=jnp.float32,
        )
    )


def deposit(scaled, chunks, corner_ref, member_ref, flat_ref, box_ref, parts_ref):
    groups = flat_ref.shape[0]
    copies = parts_ref.shape[0]
    lane_block = iota((ROWS, LANES), 1) // SZ
    flat = sum_thirds(
        jnp.dot(thirds_of(scaled), member_ref[...], preferred_element_type=jnp.float32)
    )
    for g in range(groups):
        flat_ref[g] = flat[:, g * LANES : (g + 1) * LANES]
    parts_ref[...] = jnp.zeros(parts_ref.shape, jnp.float32)

    def one(group, carry):
        factors = [
            jnp.broadcast_to(flat_ref[group, pl.ds(p, 1), :], (ROWS, LANES)) for p in range(ROWS)
        ]
        for plane, ref, base in chunks:
            for half in range(HALVES):
                box_ref[plane * HALVES + half] = total_of(
                    [
                        values_of(ref, base, groups, half, group, p) * factors[p]
                        for p in range(ROWS)
                    ]
                )
        for u in range(ROWS):
            slot = group * ROWS + u
            planes = pl.ds(corner_ref[0, slot], SX)
            shift = lax.rem(LANES + corner_ref[2, slot] - u * SZ, LANES)
            for half in range(HALVES):
                at = (u % copies, planes, pl.ds(half * ROWS, ROWS), slice(None))
                added = [
                    pltpu.roll(
                        jnp.where(lane_block == u, box_ref[x * HALVES + half], 0.0), shift, 1
                    )
                    for x in range(SX)
                ]
                parts_ref[at] = parts_ref[at] + jnp.stack(added)
        return carry

    for group in range(groups):
        one(group, 0)


def band_matrix(size, block, centre):
    row = iota((size, size), 0)
    column = iota((size, size), 1)
    apart = jnp.abs(row - column)
    table = jnp.where(apart == 0, centre, 0.0)
    for k in range(1, REACH + 1):
        table = jnp.where(apart == k, STENCIL_WEIGHTS[k], table)
    return jnp.where(row // block == column // block, table, 0.0)


def laplacian(padded_ref, extent, along_z_ref, along_y_ref):
    inner = padded_ref[REACH : REACH + extent]
    high, low = halves_of(inner.reshape(extent * SY, LANES))
    along_z = jnp.dot(
        jnp.concatenate([high, high, low], axis=1), along_z_ref[...],
        preferred_element_type=jnp.float32,
    )
    along_y = jnp.dot(
        along_y_ref[...], jnp.concatenate([high, low, high], axis=0),
        preferred_element_type=jnp.float32,
    )
    total = (along_z + along_y).reshape(inner.shape)
    for k in range(1, REACH + 1):
        total = total + STENCIL_WEIGHTS[k] * (
            padded_ref[REACH + k : REACH + k + extent] + padded_ref[REACH - k : REACH - k + extent]
        )
    return total


HALO_ROWS = REACH * SY


def to_rows(table):
    blocks = [table[:, at : at + LANES] for at in range(0, table.shape[1], LANES)]
    return jnp.concatenate(blocks, axis=0)


def from_rows(rows):
    blocks = [rows[at : at + ROWS] for at in range(0, rows.shape[0], ROWS)]
    return jnp.concatenate(blocks, axis=1)


def write_halos(field_ref, odd, mate_ref, cross_ref):
    extent = field_ref.shape[0]
    mate_start = (1 - odd) * (extent - REACH)
    cross_start = odd * (extent - REACH)
    for start, ref in ((mate_start, mate_ref), (cross_start, cross_ref)):
        ref[:HALO_ROWS] = field_ref[pl.ds(start, REACH)].reshape(HALO_ROWS, LANES)


def all_planes(ref):
    rows = ref.shape[0] // SX
    return [(x, ref, x * rows) for x in range(SX)]


def some_planes(where_ref, first, refs):
    return [(where_ref[FIRST_CHUNK + first + i], ref, 0) for i, ref in enumerate(refs)]


def field_reader(ref):
    return lambda x, half: ref[x, pl.ds(half * ROWS, ROWS), :]


def halo_kernel(where_ref, field_ref, mate_ref, cross_ref):
    write_halos(field_ref, where_ref[0], mate_ref, cross_ref)


def low_kernel(where_ref, field_ref, proj_ref, laden_ref, mate_ref, cross_ref):
    window = field_ref[pl.ds(where_ref[FIRST_CHUNK + 2], REACH)]
    laden_ref[laden_ref.shape[0] - HALO_ROWS :] = window.reshape(HALO_ROWS, LANES)
    write_halos(field_ref, where_ref[0], mate_ref, cross_ref)
    pack_plane(0, HALVES, proj_ref, laden_ref)


def above_kernel(corner_ref, own_laden_ref, high_ref, laden_ref, flat_ref, on_ref):
    rows = on_ref.shape[0]
    on_ref[...] = laden_ref[:rows]

    def field(x, half):
        return laden_ref[pl.ds(pl.multiple_of(rows + x * SY + half * ROWS, ROWS), ROWS), :]

    project(field, [(0, own_laden_ref, 0), (1, high_ref, 0)], corner_ref, flat_ref)


def hand_on_kernel(given_ref, out_ref):
    out_ref[...] = given_ref[...]


def near_kernel(corner_ref, where_ref, field_ref, low_ref, high_ref, *refs):
    chunks = some_planes(where_ref, 0, [low_ref, high_ref]) + some_planes(where_ref, 4, refs[:-1])
    project(field_reader(field_ref), chunks, corner_ref, refs[-1])


def write_table(flat_ref, member_ref, energy_ref, out_ref):
    sums = sum_atoms(flat_ref, member_ref)
    out_ref[...] = jnp.concatenate([to_rows(sums), to_rows(energy_ref[...])], axis=0)


def last_part_kernel(corner_ref, where_ref, member_ref, energy_ref, field_ref, near_ref,
                     returned_ref, far_ref, out_ref, flat_ref):
    flat_ref[...] = near_ref[...] + returned_ref[...]
    chunks = some_planes(where_ref, 7, [far_ref])
    project(field_reader(field_ref), chunks, corner_ref, flat_ref, flat_ref)
    write_table(flat_ref, member_ref, energy_ref, out_ref)


def whole_pack_kernel(proj_ref, out_ref):
    pack_plane(0, proj_ref.shape[2] // LANES, proj_ref, out_ref)


def high_kernel(proj_ref, out_ref):
    pack_plane(HALVES, HALVES, proj_ref, out_ref)


def whole_sums_kernel(corner_ref, member_ref, energy_ref, field_ref, whole_ref, out_ref, flat_ref):
    project(field_reader(field_ref), all_planes(whole_ref), corner_ref, flat_ref)
    write_table(flat_ref, member_ref, energy_ref, out_ref)


def step_kernel(index, chunk_count, corner_ref, where_ref, member_ref, along_z_ref, along_y_ref,
                field_ref, potential_ref, mate_ref, cross_ref, *refs):
    factors = step_factors()
    is_first, is_last = index == 0, index + 1 == len(factors)
    refs = list(refs)
    odd = where_ref[0]
    own_ref, far_ref = refs.pop(0), refs.pop(0)
    if is_first:
        table = from_rows(own_ref[...] + refs.pop(0)[...] + far_ref[...])
    else:
        table = from_rows(own_ref[HALO_ROWS:] + cross_ref[HALO_ROWS:] + far_ref[...])
    if chunk_count > 1:
        chunks = some_planes(where_ref, 0, refs[:chunk_count])
    else:
        chunks = all_planes(refs[0])
    refs = refs[chunk_count:]
    energy_ref = None if is_first else refs.pop(0)
    before_ref = None if is_first else refs.pop(0)
    next_ref = refs.pop(0)
    if not is_last:
        next_mate_ref, next_cross_ref = refs.pop(0), refs.pop(0)
    if is_first:
        energy_ref = refs.pop(0)
    flat_ref, box_ref, parts_ref, padded_ref = refs
    extent = field_ref.shape[0]
    if is_first:
        atoms = table.shape[1] // 2
        energy_ref[...] = table[:, atoms:]
        table = table[:, :atoms]
    scaled = table * energy_ref[...]
    deposit(scaled, chunks, corner_ref, member_ref, flat_ref, box_ref, parts_ref)

    cells = field_ref[...]
    padded_ref[REACH : REACH + extent] = cells
    mate_at = (1 - odd) * (extent + REACH)
    cross_at = odd * (extent + REACH)
    padded_ref[pl.ds(mate_at, REACH)] = mate_ref[:HALO_ROWS].reshape(REACH, SY, LANES)
    padded_ref[pl.ds(cross_at, REACH)] = cross_ref[:HALO_ROWS].reshape(REACH, SY, LANES)
    value = -0.5 * laplacian(padded_ref, extent, along_z_ref, along_y_ref) + (potential_ref[...] - CENTRE) * cells
    for u in range(parts_ref.shape[0]):
        value = value + parts_ref[u]
    value = factors[index][0] * value
    if not is_first:
        value = value - factors[index][1] * before_ref[...]
    next_ref[...] = value
    if not is_last:
        project(field_reader(next_ref), chunks, corner_ref, flat_ref)
        sums = sum_atoms(flat_ref, member_ref)
        write_halos(next_ref, odd, next_mate_ref, next_cross_ref)
        next_mate_ref[HALO_ROWS:] = to_rows(sums)
        next_cross_ref[HALO_ROWS:] = to_rows(sums)


VMEM = pl.BlockSpec(memory_space=pltpu.VMEM)
SMEM = pl.BlockSpec(memory_space=pltpu.SMEM)
ANY = pl.BlockSpec(memory_space=pl.ANY)


def swap(values, axis, first):
    count = lax.axis_size(axis)
    pairs = []
    for i in range(first, count - 1, 2):
        pairs += [(i, i + 1), (i + 1, i)]
    return lax.ppermute(values, axis, pairs)


def turn(values, axis, step):
    count = lax.axis_size(axis)
    return lax.ppermute(values, axis, [(i, (i + step) % count) for i in range(count)])


def on_device(wave_block, potential, projectors, kb_energy, slot_atom, slot_corner):
    bands, planes, cells_y, cells_z = wave_block.shape
    assert bands == 1 and cells_y == SY and cells_z == LANES
    slots, proj_count = projectors.shape[:2]
    atom_own = kb_energy.shape[0]
    atoms = atom_own * lax.axis_size("dom")
    groups = slots // ROWS
    tiles = projectors.shape[2] // LANES
    assert proj_count == ROWS and slots % ROWS == 0
    place = lax.axis_index("dom")
    field = wave_block[0]

    def shaped(*shape):
        return jax.ShapeDtypeStruct(shape, jnp.float32)

    def call(kernel, name, out_shape, scalars, operands, scratch, after=()):
        inputs = len(scalars) + len(operands)

        def body(*refs):
            kernel(*refs[:inputs], *refs[inputs + len(after) :])

        return pl.pallas_call(
            body,
            out_shape=out_shape,
            in_specs=[SMEM] * len(scalars) + [VMEM] * len(operands) + [ANY] * len(after),
            out_specs=jax.tree.map(lambda _: VMEM, out_shape),
            scratch_shapes=[pltpu.VMEM(shape, jnp.float32) for shape in scratch],
            compiler_params=pltpu.CompilerParams(vmem_limit_bytes=16 * 2**20),
            cost_estimate=pl.CostEstimate(flops=0, bytes_accessed=0, transcendentals=0),
            name=name,
        )(*scalars, *operands, *after)

    atom_row = jnp.repeat(slot_atom, SZ)[None, :]
    own_atoms = (jnp.arange(atoms) // atom_own) == place
    energy = jnp.where(own_atoms[None, :], jnp.tile(kb_energy.T, (1, atoms // atom_own)), 0.0)
    flat = (groups, ROWS, LANES)
    boxes = (TILES, ROWS, LANES)
    parts = (COPIES, planes, SY, LANES)
    padded = (planes + 2 * REACH, SY, LANES)
    table_rows = ROWS * atoms // LANES
    sends = [shaped(HALO_ROWS + table_rows, LANES)] * 2

    flat = (groups, ROWS, LANES)
    boxes = (TILES, ROWS, LANES)
    parts = (COPIES, planes, SY, LANES)
    padded = (planes + 2 * REACH, SY, LANES)
    table_rows = ROWS * atoms // LANES
    sends = [shaped(HALO_ROWS + table_rows, LANES)] * 2

    def pack(first_tile, count, after=()):
        return call(
            functools.partial(pack_kernel, first_tile), "pack_projectors",
            shaped(count, groups, ROWS, ROWS, LANES), [], [projectors], [], after,
        )

    tables = call(
        table_kernel, "tables",
        [
            jax.ShapeDtypeStruct(shape, jnp.bfloat16)
            for shape in (
                (atoms, slots * SZ), (3 * LANES, LANES), (planes * SY, 3 * planes * SY)
            )
        ],
        [], [atom_row], [],
    )
    odd = (place % 2).astype(jnp.int32)
    halos = [shaped(HALO_ROWS, LANES)] * 2
    if lax.axis_size("band") == 4 and tiles == 2 * HALVES:
        at = lax.axis_index("band").astype(jnp.int32)
        owners = [at, (at + 1) % 4, (at + 3) % 4, (at + 2) % 4]
        where = jnp.stack([odd] + [2 * part + h for part in owners for h in range(2)])
        rows = HALVES * groups * ROWS * ROWS
        plane = shaped(rows, LANES)
        low, mate, cross = call(
            low_kernel, "pack_low", [shaped(rows + HALO_ROWS, LANES)] + halos,
            [where], [field, projectors], [],
        )
        mate, cross = swap(mate, "dom", 0), swap(cross, "dom", 1)
        below_low = turn(low, "band", 1)
        high = call(high_kernel, "pack_high", plane, [], [projectors], [], [low])
        below_high = turn(high, "band", 1)
        returned, on_low = call(
            above_kernel, "project_above", [shaped(*flat), plane], [slot_corner],
            [low, high, below_low], [],
        )
        returned = turn(returned, "band", -1)
        far_low = turn(on_low, "band", 1)

        def hand_on(values, *after):
            return call(hand_on_kernel, "hand_on", plane, [], [values], [], after)

        on_high = hand_on(below_high, on_low, returned)
        far_high = turn(on_high, "band", 1)
        on_far_low = hand_on(far_low, on_high, tables[0], energy)
        above_low = turn(on_far_low, "band", 1)
        near = call(
            near_kernel, "project_near", shaped(*flat), [slot_corner, where],
            [field, low, high, below_low, below_high, far_low], [], [mate, cross],
        )
        own = call(
            last_part_kernel, "first_sums", shaped(2 * table_rows, LANES), [slot_corner, where],
            [tables[0], energy, field, near, returned, far_high], [flat],
        )
        own = own + swap(own, "dom", 0)
        on_far_high = hand_on(far_high, own)
        above_high = turn(on_far_high, "band", 1)
        own = call(
            hand_on_kernel, "hold", shaped(*own.shape), [], [own], [], [above_low]
        )
        chunks = [low, high, above_low, above_high, below_low, below_high, far_low, far_high]
    else:
        where = odd[None]
        mate, cross = call(halo_kernel, "cut_halos", halos, [where], [field], [])
        packed = call(
            whole_pack_kernel, "pack_projectors", shaped(tiles * groups * ROWS * ROWS, LANES),
            [], [projectors], [],
        )
        chunks = [lax.all_gather(packed, "band", axis=0, tiled=True)]
        own = call(
            whole_sums_kernel, "first_sums", shaped(2 * table_rows, LANES), [slot_corner],
            [tables[0], energy, field, *chunks], [flat],
        )
        mate, cross = swap(mate, "dom", 0), swap(cross, "dom", 1)
        own = own + swap(own, "dom", 0)
    other = swap(own, "dom", 1)
    far = swap(other, "dom", 0)
    before = None
    for index in range(DEGREE):
        if index > 0:
            to_mate, to_cross = sent
            mate = swap(to_mate, "dom", 0)
            own = to_cross.at[HALO_ROWS:].add(mate[HALO_ROWS:])
            cross = swap(own, "dom", 1)
            far = swap(cross[HALO_ROWS:], "dom", 0)
        operands = [*tables, field, potential, mate, cross, own, far]
        if index == 0:
            operands.append(other)
        operands += chunks
        out_shape = [shaped(planes, SY, LANES)]
        if index > 0:
            operands += [energy, before]
        if index + 1 < DEGREE:
            out_shape += sends
        if index == 0:
            out_shape += [shaped(ROWS, atoms)]
        result = call(
            functools.partial(step_kernel, index, len(chunks)), f"filter_step_{index + 1}",
            out_shape, [slot_corner, where], operands, [flat, boxes, parts, padded],
        )
        before, field = field, result[0]
        sent = result[1:3]
        if index == 0:
            energy = result[3]
    return field[None]


def solution(mesh):
    placed = (
        P("band", "dom", None, None),
        P("dom", None, None),
        P("dom", None, "band"),
        P("dom", None),
        P("dom"),
        P(None, "dom"),
    )
    return jax.shard_map(
        on_device,
        mesh=mesh,
        in_specs=placed,
        out_specs=P("band", "dom", None, None),
        check_vma=False,
    )
```

```python
import functools

import jax
import jax.numpy as jnp
from jax import lax
from jax.experimental import pallas as pl
from jax.experimental.pallas import tpu as pltpu
from jax.sharding import PartitionSpec as P

SX = 8
SY = 16
SZ = 16
DEGREE = 3
LANES = 128
ROWS = 8
TILES = SX * SY * SZ // LANES
HALVES = SY // ROWS

STENCIL_WEIGHTS = (
    -5369.0 / 1800.0,
    12.0 / 7.0,
    -15.0 / 56.0,
    10.0 / 189.0,
    -1.0 / 112.0,
    2.0 / 1925.0,
    -1.0 / 16632.0,
)
REACH = len(STENCIL_WEIGHTS) - 1
LOWER_EDGE = 3.0
UPPER_EDGE = 30.0
ANCHOR_POINT = 0.5
HALF_WIDTH = (UPPER_EDGE - LOWER_EDGE) / 2.0
CENTRE = (UPPER_EDGE + LOWER_EDGE) / 2.0
SIGMA_FIRST = HALF_WIDTH / (ANCHOR_POINT - CENTRE)
COPIES = 4
FIRST_CHUNK = 1


def step_factors():
    sigma_now = SIGMA_FIRST
    factors = [(SIGMA_FIRST / HALF_WIDTH, 0.0)]
    for _ in range(2, DEGREE + 1):
        sigma_next = 1.0 / (2.0 / SIGMA_FIRST - sigma_now)
        factors.append((2.0 * sigma_next / HALF_WIDTH, sigma_now * sigma_next))
        sigma_now = sigma_next
    return factors


def iota(shape, dim):
    return lax.broadcasted_iota(jnp.int32, shape, dim)


def fold_rows(blocks):
    row = iota((ROWS, LANES), 0)
    distance = 1
    while len(blocks) > 1:
        first = (row // distance) % 2 == 0
        blocks = [
            jnp.where(first, a, b) + pltpu.roll(jnp.where(first, b, a), distance, 0)
            for a, b in zip(blocks[::2], blocks[1::2])
        ]
        distance *= 2
    return blocks[0]


def choose(masks, values):
    result = values[-1]
    for mask, value in zip(masks[:-1], values[:-1]):
        result = jnp.where(mask, value, result)
    return result


def pack_plane(first_tile, tiles, proj_ref, out_ref):
    groups = proj_ref.shape[0] // ROWS
    row = iota((ROWS, LANES), 0)
    block = iota((ROWS, LANES), 1) // SZ
    apart = (row - block + ROWS) % ROWS
    block_is = [block == b for b in range(ROWS)]
    row_is = [row == r for r in range(ROWS)]
    apart_is = [apart == d for d in range(ROWS)]

    def one(index, carry):
        tile, group = index // groups, index % groups
        cells = pl.ds(pl.multiple_of((first_tile + tile) * LANES, LANES), LANES)
        given = [proj_ref[group * ROWS + u, :, cells] for u in range(ROWS)]
        by_lane = []
        for d in range(ROWS):
            mixed = choose(block_is, [given[(b - d) % ROWS] for b in range(ROWS)])
            by_lane.append(pltpu.roll(mixed, (LANES - d * SZ) % LANES, 1) if d else mixed)
        by_row = []
        for e in range(ROWS):
            mixed = choose(apart_is, [by_lane[(d + e) % ROWS] for d in range(ROWS)])
            by_row.append(pltpu.roll(mixed, e, 0) if e else mixed)
        for p in range(ROWS):
            at = pl.ds(pl.multiple_of((index * ROWS + p) * ROWS, ROWS), ROWS)
            out_ref[at, :] = choose(row_is, [by_row[(j - p) % ROWS] for j in range(ROWS)])
        return carry

    lax.fori_loop(0, tiles * groups, one, 0)


def halves_of(value):
    high = value.astype(jnp.bfloat16)
    return high, (value - high.astype(jnp.float32)).astype(jnp.bfloat16)


def thirds_of(value):
    rest, parts = value, []
    for _ in range(3):
        high = rest.astype(jnp.bfloat16).astype(jnp.float32)
        parts.append(high)
        rest = rest - high
    return jnp.concatenate(parts, axis=0).astype(jnp.bfloat16)


def sum_thirds(value):
    return value[:ROWS] + value[ROWS : 2 * ROWS] + value[2 * ROWS :]


def table_kernel(atom_row_ref, member_ref, along_z_ref, along_y_ref):
    atoms = iota(member_ref.shape, 0)
    member_ref[...] = (atoms == atom_row_ref[...]).astype(jnp.float32).astype(jnp.bfloat16)
    high, low = halves_of(band_matrix(LANES, LANES, 3.0 * STENCIL_WEIGHTS[0]))
    along_z_ref[...] = jnp.concatenate([high, low, high], axis=0)
    high, low = halves_of(band_matrix(along_y_ref.shape[0], SY, 0.0))
    along_y_ref[...] = jnp.concatenate([high, high, low], axis=1)


def total_of(products):
    while len(products) > 1:
        pairs = [a + b for a, b in zip(products[::2], products[1::2])]
        products = pairs + products[len(pairs) * 2 :]
    return products[0]


def values_of(ref, base, groups, half, group, p):
    at = base + ((half * groups + group) * ROWS + p) * ROWS
    return ref[at : at + ROWS, :]


def project(field, chunks, corner_ref, flat_ref, start_ref=None):
    groups = flat_ref.shape[0]
    lane_block = iota((ROWS, LANES), 1) // SZ

    def one(group, carry):
        corners = [corner_ref[0, group * ROWS + u] for u in range(ROWS)]
        shifts = [
            lax.rem(LANES + u * SZ - corner_ref[2, group * ROWS + u], LANES) for u in range(ROWS)
        ]
        sums = [[] for _ in range(ROWS)]
        for plane, ref, base in chunks:
            for half in range(HALVES):
                box = None
                for u in range(ROWS):
                    turned = pltpu.roll(field(corners[u] + plane, half), shifts[u], 1)
                    box = turned if u == 0 else jnp.where(lane_block == u, turned, box)
                for p in range(ROWS):
                    sums[p].append(values_of(ref, base, groups, half, group, p) * box)
        flat = fold_rows([total_of(products) for products in sums])
        flat_ref[group] = flat if start_ref is None else flat + start_ref[group]
        return carry

    for group in range(groups):
        one(group, 0)


def sum_atoms(flat_ref, member_ref):
    flat = jnp.concatenate([flat_ref[g] for g in range(flat_ref.shape[0])], axis=1)
    return sum_thirds(
        lax.dot_general(
            thirds_of(flat), member_ref[...], (((1,), (1,)), ((), ())),
            preferred_element_type=jnp.float32,
        )
    )


def deposit(scaled, chunks, corner_ref, member_ref, flat_ref, box_ref, parts_ref):
    groups = flat_ref.shape[0]
    copies = parts_ref.shape[0]
    lane_block = iota((ROWS, LANES), 1) // SZ
    flat = sum_thirds(
        jnp.dot(thirds_of(scaled), member_ref[...], preferred_element_type=jnp.float32)
    )
    for g in range(groups):
        flat_ref[g] = flat[:, g * LANES : (g + 1) * LANES]
    parts_ref[...] = jnp.zeros(parts_ref.shape, jnp.float32)

    def one(group, carry):
        factors = [
            jnp.broadcast_to(flat_ref[group, pl.ds(p, 1), :], (ROWS, LANES)) for p in range(ROWS)
        ]
        for plane, ref, base in chunks:
            for half in range(HALVES):
                box_ref[plane * HALVES + half] = total_of(
                    [
                        values_of(ref, base, groups, half, group, p) * factors[p]
                        for p in range(ROWS)
                    ]
                )
        for u in range(ROWS):
            slot = group * ROWS + u
            planes = pl.ds(corner_ref[0, slot], SX)
            shift = lax.rem(LANES + corner_ref[2, slot] - u * SZ, LANES)
            for half in range(HALVES):
                at = (u % copies, planes, pl.ds(half * ROWS, ROWS), slice(None))
                added = [
                    pltpu.roll(
                        jnp.where(lane_block == u, box_ref[x * HALVES + half], 0.0), shift, 1
                    )
                    for x in range(SX)
                ]
                parts_ref[at] = parts_ref[at] + jnp.stack(added)
        return carry

    for group in range(groups):
        one(group, 0)


def band_matrix(size, block, centre):
    row = iota((size, size), 0)
    column = iota((size, size), 1)
    apart = jnp.abs(row - column)
    table = jnp.where(apart == 0, centre, 0.0)
    for k in range(1, REACH + 1):
        table = jnp.where(apart == k, STENCIL_WEIGHTS[k], table)
    return jnp.where(row // block == column // block, table, 0.0)


def laplacian(padded_ref, extent, along_z_ref, along_y_ref):
    inner = padded_ref[REACH : REACH + extent]
    high, low = halves_of(inner.reshape(extent * SY, LANES))
    along_z = jnp.dot(
        jnp.concatenate([high, high, low], axis=1), along_z_ref[...],
        preferred_element_type=jnp.float32,
    )
    along_y = jnp.dot(
        along_y_ref[...], jnp.concatenate([high, low, high], axis=0),
        preferred_element_type=jnp.float32,
    )
    total = (along_z + along_y).reshape(inner.shape)
    for k in range(1, REACH + 1):
        total = total + STENCIL_WEIGHTS[k] * (
            padded_ref[REACH + k : REACH + k + extent] + padded_ref[REACH - k : REACH - k + extent]
        )
    return total


HALO_ROWS = REACH * SY


def to_rows(table):
    blocks = [table[:, at : at + LANES] for at in range(0, table.shape[1], LANES)]
    return jnp.concatenate(blocks, axis=0)


def from_rows(rows):
    blocks = [rows[at : at + ROWS] for at in range(0, rows.shape[0], ROWS)]
    return jnp.concatenate(blocks, axis=1)


def write_halos(field_ref, odd, mate_ref, cross_ref):
    extent = field_ref.shape[0]
    mate_start = (1 - odd) * (extent - REACH)
    cross_start = odd * (extent - REACH)
    for start, ref in ((mate_start, mate_ref), (cross_start, cross_ref)):
        ref[:HALO_ROWS] = field_ref[pl.ds(start, REACH)].reshape(HALO_ROWS, LANES)


def all_planes(ref):
    rows = ref.shape[0] // SX
    return [(x, ref, x * rows) for x in range(SX)]


def some_planes(where_ref, first, refs):
    return [(where_ref[FIRST_CHUNK + first + i], ref, 0) for i, ref in enumerate(refs)]


def field_reader(ref):
    return lambda x, half: ref[x, pl.ds(half * ROWS, ROWS), :]


def halo_kernel(where_ref, field_ref, mate_ref, cross_ref):
    write_halos(field_ref, where_ref[0], mate_ref, cross_ref)


def low_kernel(proj_ref, laden_ref):
    pack_plane(0, HALVES, proj_ref, laden_ref)


def window_kernel(where_ref, field_ref, laden_ref, out_ref):
    window = field_ref[pl.ds(where_ref[FIRST_CHUNK + 2], REACH)]
    out_ref[out_ref.shape[0] - HALO_ROWS :] = window.reshape(HALO_ROWS, LANES)


def above_kernel(corner_ref, own_laden_ref, high_ref, laden_ref, flat_ref, on_ref):
    rows = on_ref.shape[0]
    on_ref[...] = laden_ref[:rows]

    def field(x, half):
        return laden_ref[pl.ds(pl.multiple_of(rows + x * SY + half * ROWS, ROWS), ROWS), :]

    project(field, [(0, own_laden_ref, 0), (1, high_ref, 0)], corner_ref, flat_ref)


def hand_on_kernel(given_ref, out_ref):
    out_ref[...] = given_ref[...]


def near_kernel(corner_ref, where_ref, field_ref, low_ref, high_ref, *refs):
    chunks = some_planes(where_ref, 0, [low_ref, high_ref]) + some_planes(where_ref, 4, refs[:-1])
    project(field_reader(field_ref), chunks, corner_ref, refs[-1])


def write_table(flat_ref, member_ref, energy_ref, out_ref):
    sums = sum_atoms(flat_ref, member_ref)
    out_ref[...] = jnp.concatenate([to_rows(sums), to_rows(energy_ref[...])], axis=0)


def last_part_kernel(corner_ref, where_ref, member_ref, energy_ref, field_ref, near_ref,
                     returned_ref, far_ref, out_ref, flat_ref):
    flat_ref[...] = near_ref[...] + returned_ref[...]
    chunks = some_planes(where_ref, 7, [far_ref])
    project(field_reader(field_ref), chunks, corner_ref, flat_ref, flat_ref)
    write_table(flat_ref, member_ref, energy_ref, out_ref)


def whole_pack_kernel(proj_ref, out_ref):
    pack_plane(0, proj_ref.shape[2] // LANES, proj_ref, out_ref)


def high_kernel(proj_ref, out_ref):
    pack_plane(HALVES, HALVES, proj_ref, out_ref)


def whole_sums_kernel(corner_ref, member_ref, energy_ref, field_ref, whole_ref, out_ref, flat_ref):
    project(field_reader(field_ref), all_planes(whole_ref), corner_ref, flat_ref)
    write_table(flat_ref, member_ref, energy_ref, out_ref)


def step_kernel(index, chunk_count, corner_ref, where_ref, member_ref, along_z_ref, along_y_ref,
                field_ref, potential_ref, mate_ref, cross_ref, *refs):
    factors = step_factors()
    is_first, is_last = index == 0, index + 1 == len(factors)
    refs = list(refs)
    odd = where_ref[0]
    own_ref, far_ref = refs.pop(0), refs.pop(0)
    if is_first:
        table = from_rows(own_ref[...] + refs.pop(0)[...] + far_ref[...])
    else:
        table = from_rows(own_ref[HALO_ROWS:] + cross_ref[HALO_ROWS:] + far_ref[...])
    if chunk_count > 1:
        chunks = some_planes(where_ref, 0, refs[:chunk_count])
    else:
        chunks = all_planes(refs[0])
    refs = refs[chunk_count:]
    energy_ref = None if is_first else refs.pop(0)
    before_ref = None if is_first else refs.pop(0)
    next_ref = refs.pop(0)
    if not is_last:
        next_mate_ref, next_cross_ref = refs.pop(0), refs.pop(0)
    if is_first:
        energy_ref = refs.pop(0)
    flat_ref, box_ref, parts_ref, padded_ref = refs
    extent = field_ref.shape[0]
    if is_first:
        atoms = table.shape[1] // 2
        energy_ref[...] = table[:, atoms:]
        table = table[:, :atoms]
    scaled = table * energy_ref[...]
    deposit(scaled, chunks, corner_ref, member_ref, flat_ref, box_ref, parts_ref)

    cells = field_ref[...]
    padded_ref[REACH : REACH + extent] = cells
    mate_at = (1 - odd) * (extent + REACH)
    cross_at = odd * (extent + REACH)
    padded_ref[pl.ds(mate_at, REACH)] = mate_ref[:HALO_ROWS].reshape(REACH, SY, LANES)
    padded_ref[pl.ds(cross_at, REACH)] = cross_ref[:HALO_ROWS].reshape(REACH, SY, LANES)
    value = -0.5 * laplacian(padded_ref, extent, along_z_ref, along_y_ref) + (potential_ref[...] - CENTRE) * cells
    for u in range(parts_ref.shape[0]):
        value = value + parts_ref[u]
    value = factors[index][0] * value
    if not is_first:
        value = value - factors[index][1] * before_ref[...]
    next_ref[...] = value
    if not is_last:
        project(field_reader(next_ref), chunks, corner_ref, flat_ref)
        sums = sum_atoms(flat_ref, member_ref)
        write_halos(next_ref, odd, next_mate_ref, next_cross_ref)
        next_mate_ref[HALO_ROWS:] = to_rows(sums)
        next_cross_ref[HALO_ROWS:] = to_rows(sums)


VMEM = pl.BlockSpec(memory_space=pltpu.VMEM)
SMEM = pl.BlockSpec(memory_space=pltpu.SMEM)
ANY = pl.BlockSpec(memory_space=pl.ANY)


def swap(values, axis, first):
    count = lax.axis_size(axis)
    pairs = []
    for i in range(first, count - 1, 2):
        pairs += [(i, i + 1), (i + 1, i)]
    return lax.ppermute(values, axis, pairs)


def turn(values, axis, step):
    count = lax.axis_size(axis)
    return lax.ppermute(values, axis, [(i, (i + step) % count) for i in range(count)])


def on_device(wave_block, potential, projectors, kb_energy, slot_atom, slot_corner):
    bands, planes, cells_y, cells_z = wave_block.shape
    assert bands == 1 and cells_y == SY and cells_z == LANES
    slots, proj_count = projectors.shape[:2]
    atom_own = kb_energy.shape[0]
    atoms = atom_own * lax.axis_size("dom")
    groups = slots // ROWS
    tiles = projectors.shape[2] // LANES
    assert proj_count == ROWS and slots % ROWS == 0
    place = lax.axis_index("dom")
    field = wave_block[0]

    def shaped(*shape):
        return jax.ShapeDtypeStruct(shape, jnp.float32)

    def call(kernel, name, out_shape, scalars, operands, scratch, after=(), in_place={}):
        inputs = len(scalars) + len(operands)

        def body(*refs):
            kernel(*refs[:inputs], *refs[inputs + len(after) :])

        return pl.pallas_call(
            body,
            out_shape=out_shape,
            in_specs=[SMEM] * len(scalars) + [VMEM] * len(operands) + [ANY] * len(after),
            out_specs=jax.tree.map(lambda _: VMEM, out_shape),
            scratch_shapes=[pltpu.VMEM(shape, jnp.float32) for shape in scratch],
            compiler_params=pltpu.CompilerParams(vmem_limit_bytes=16 * 2**20),
            input_output_aliases=in_place,
            cost_estimate=pl.CostEstimate(flops=0, bytes_accessed=0, transcendentals=0),
            name=name,
        )(*scalars, *operands, *after)

    atom_row = jnp.repeat(slot_atom, SZ)[None, :]
    own_atoms = (jnp.arange(atoms) // atom_own) == place
    energy = jnp.where(own_atoms[None, :], jnp.tile(kb_energy.T, (1, atoms // atom_own)), 0.0)
    flat = (groups, ROWS, LANES)
    boxes = (TILES, ROWS, LANES)
    parts = (COPIES, planes, SY, LANES)
    padded = (planes + 2 * REACH, SY, LANES)
    table_rows = ROWS * atoms // LANES
    sends = [shaped(HALO_ROWS + table_rows, LANES)] * 2

    flat = (groups, ROWS, LANES)
    boxes = (TILES, ROWS, LANES)
    parts = (COPIES, planes, SY, LANES)
    padded = (planes + 2 * REACH, SY, LANES)
    table_rows = ROWS * atoms // LANES
    sends = [shaped(HALO_ROWS + table_rows, LANES)] * 2

    def pack(first_tile, count, after=()):
        return call(
            functools.partial(pack_kernel, first_tile), "pack_projectors",
            shaped(count, groups, ROWS, ROWS, LANES), [], [projectors], [], after,
        )

    tables = call(
        table_kernel, "tables",
        [
            jax.ShapeDtypeStruct(shape, jnp.bfloat16)
            for shape in (
                (atoms, slots * SZ), (3 * LANES, LANES), (planes * SY, 3 * planes * SY)
            )
        ],
        [], [atom_row], [],
    )
    odd = (place % 2).astype(jnp.int32)
    halos = [shaped(HALO_ROWS, LANES)] * 2
    if lax.axis_size("band") == 4 and tiles == 2 * HALVES:
        at = lax.axis_index("band").astype(jnp.int32)
        owners = [at, (at + 1) % 4, (at + 3) % 4, (at + 2) % 4]
        where = jnp.stack([odd] + [2 * part + h for part in owners for h in range(2)])
        rows = HALVES * groups * ROWS * ROWS
        plane = shaped(rows, LANES)
        laden = shaped(rows + HALO_ROWS, LANES)
        low = call(low_kernel, "pack_low", laden, [], [projectors], [])
        low = call(
            window_kernel, "add_window", laden, [where], [field, low], [], (), {2: 0}
        )
        below_low = turn(low, "band", 1)
        high = call(high_kernel, "pack_high", plane, [], [projectors], [], [low])
        below_high = turn(high, "band", 1)
        returned, on_low = call(
            above_kernel, "project_above", [shaped(*flat), plane], [slot_corner],
            [low, high, below_low], [],
        )
        returned = turn(returned, "band", -1)
        far_low = turn(on_low, "band", 1)

        def hand_on(values, *after):
            return call(hand_on_kernel, "hand_on", plane, [], [values], [], after)

        on_high = hand_on(below_high, on_low, returned)
        far_high = turn(on_high, "band", 1)
        on_far_low = hand_on(far_low, on_high, tables[0], energy)
        above_low = turn(on_far_low, "band", 1)
        mate, cross = call(
            halo_kernel, "cut_halos", halos, [where], [field], [], [on_far_low]
        )
        mate, cross = swap(mate, "dom", 0), swap(cross, "dom", 1)
        near = call(
            near_kernel, "project_near", shaped(*flat), [slot_corner, where],
            [field, low, high, below_low, below_high, far_low], [],
        )
        on_far_high = hand_on(far_high, near, tables[0], energy, mate, cross)
        above_high = turn(on_far_high, "band", 1)
        own = call(
            last_part_kernel, "first_sums", shaped(2 * table_rows, LANES), [slot_corner, where],
            [tables[0], energy, field, near, returned, far_high], [flat],
        )
        chunks = [low, high, above_low, above_high, below_low, below_high, far_low, far_high]
    else:
        where = odd[None]
        mate, cross = call(halo_kernel, "cut_halos", halos, [where], [field], [])
        packed = call(
            whole_pack_kernel, "pack_projectors", shaped(tiles * groups * ROWS * ROWS, LANES),
            [], [projectors], [],
        )
        chunks = [lax.all_gather(packed, "band", axis=0, tiled=True)]
        own = call(
            whole_sums_kernel, "first_sums", shaped(2 * table_rows, LANES), [slot_corner],
            [tables[0], energy, field, *chunks], [flat],
        )
        mate, cross = swap(mate, "dom", 0), swap(cross, "dom", 1)
    own = own + swap(own, "dom", 0)
    other = swap(own, "dom", 1)
    far = swap(other, "dom", 0)
    before = None
    for index in range(DEGREE):
        if index > 0:
            to_mate, to_cross = sent
            mate = swap(to_mate, "dom", 0)
            own = to_cross.at[HALO_ROWS:].add(mate[HALO_ROWS:])
            cross = swap(own, "dom", 1)
            far = swap(cross[HALO_ROWS:], "dom", 0)
        operands = [*tables, field, potential, mate, cross, own, far]
        if index == 0:
            operands.append(other)
        operands += chunks
        out_shape = [shaped(planes, SY, LANES)]
        if index > 0:
            operands += [energy, before]
        if index + 1 < DEGREE:
            out_shape += sends
        if index == 0:
            out_shape += [shaped(ROWS, atoms)]
        result = call(
            functools.partial(step_kernel, index, len(chunks)), f"filter_step_{index + 1}",
            out_shape, [slot_corner, where], operands, [flat, boxes, parts, padded],
        )
        before, field = field, result[0]
        sent = result[1:3]
        if index == 0:
            energy = result[3]
    return field[None]


def solution(mesh):
    placed = (
        P("band", "dom", None, None),
        P("dom", None, None),
        P("dom", None, "band"),
        P("dom", None),
        P("dom"),
        P(None, "dom"),
    )
    return jax.shard_map(
        on_device,
        mesh=mesh,
        in_specs=placed,
        out_specs=P("band", "dom", None, None),
        check_vma=False,
    )
```

```python
import functools

import jax
import jax.numpy as jnp
from jax import lax
from jax.experimental import pallas as pl
from jax.experimental.pallas import tpu as pltpu
from jax.sharding import PartitionSpec as P

SX = 8
SY = 16
SZ = 16
DEGREE = 3
LANES = 128
ROWS = 8
TILES = SX * SY * SZ // LANES
HALVES = SY // ROWS

STENCIL_WEIGHTS = (
    -5369.0 / 1800.0,
    12.0 / 7.0,
    -15.0 / 56.0,
    10.0 / 189.0,
    -1.0 / 112.0,
    2.0 / 1925.0,
    -1.0 / 16632.0,
)
REACH = len(STENCIL_WEIGHTS) - 1
LOWER_EDGE = 3.0
UPPER_EDGE = 30.0
ANCHOR_POINT = 0.5
HALF_WIDTH = (UPPER_EDGE - LOWER_EDGE) / 2.0
CENTRE = (UPPER_EDGE + LOWER_EDGE) / 2.0
SIGMA_FIRST = HALF_WIDTH / (ANCHOR_POINT - CENTRE)
COPIES = 4
PARTS_FROM = (0, 1, 3, 2)


def step_factors():
    sigma_now = SIGMA_FIRST
    factors = [(SIGMA_FIRST / HALF_WIDTH, 0.0)]
    for _ in range(2, DEGREE + 1):
        sigma_next = 1.0 / (2.0 / SIGMA_FIRST - sigma_now)
        factors.append((2.0 * sigma_next / HALF_WIDTH, sigma_now * sigma_next))
        sigma_now = sigma_next
    return factors


def odd_here():
    return lax.rem(lax.axis_index("dom"), 2)


def plane_here(index):
    owner = lax.rem(lax.axis_index("band") + PARTS_FROM[index // 2], 4)
    return owner * 2 + index % 2


def iota(shape, dim):
    return lax.broadcasted_iota(jnp.int32, shape, dim)


def fold_rows(blocks):
    row = iota((ROWS, LANES), 0)
    distance = 1
    while len(blocks) > 1:
        first = (row // distance) % 2 == 0
        blocks = [
            jnp.where(first, a, b) + pltpu.roll(jnp.where(first, b, a), distance, 0)
            for a, b in zip(blocks[::2], blocks[1::2])
        ]
        distance *= 2
    return blocks[0]


def choose(masks, values):
    result = values[-1]
    for mask, value in zip(masks[:-1], values[:-1]):
        result = jnp.where(mask, value, result)
    return result


def pack_plane(first_tile, tiles, proj_ref, out_ref):
    groups = proj_ref.shape[0] // ROWS
    row = iota((ROWS, LANES), 0)
    block = iota((ROWS, LANES), 1) // SZ
    apart = (row - block + ROWS) % ROWS
    block_is = [block == b for b in range(ROWS)]
    row_is = [row == r for r in range(ROWS)]
    apart_is = [apart == d for d in range(ROWS)]

    def one(index, carry):
        tile, group = index // groups, index % groups
        cells = pl.ds(pl.multiple_of((first_tile + tile) * LANES, LANES), LANES)
        given = [proj_ref[group * ROWS + u, :, cells] for u in range(ROWS)]
        by_lane = []
        for d in range(ROWS):
            mixed = choose(block_is, [given[(b - d) % ROWS] for b in range(ROWS)])
            by_lane.append(pltpu.roll(mixed, (LANES - d * SZ) % LANES, 1) if d else mixed)
        by_row = []
        for e in range(ROWS):
            mixed = choose(apart_is, [by_lane[(d + e) % ROWS] for d in range(ROWS)])
            by_row.append(pltpu.roll(mixed, e, 0) if e else mixed)
        for p in range(ROWS):
            at = pl.ds(pl.multiple_of((index * ROWS + p) * ROWS, ROWS), ROWS)
            out_ref[at, :] = choose(row_is, [by_row[(j - p) % ROWS] for j in range(ROWS)])
        return carry

    lax.fori_loop(0, tiles * groups, one, 0)


def halves_of(value):
    high = value.astype(jnp.bfloat16)
    return high, (value - high.astype(jnp.float32)).astype(jnp.bfloat16)


def thirds_of(value):
    rest, parts = value, []
    for _ in range(3):
        high = rest.astype(jnp.bfloat16).astype(jnp.float32)
        parts.append(high)
        rest = rest - high
    return jnp.concatenate(parts, axis=0).astype(jnp.bfloat16)


def sum_thirds(value):
    return value[:ROWS] + value[ROWS : 2 * ROWS] + value[2 * ROWS :]


def table_kernel(atom_row_ref, member_ref, along_z_ref, along_y_ref):
    atoms = iota(member_ref.shape, 0)
    member_ref[...] = (atoms == atom_row_ref[...]).astype(jnp.float32).astype(jnp.bfloat16)
    high, low = halves_of(band_matrix(LANES, LANES, 3.0 * STENCIL_WEIGHTS[0]))
    along_z_ref[...] = jnp.concatenate([high, low, high], axis=0)
    high, low = halves_of(band_matrix(along_y_ref.shape[0], SY, 0.0))
    along_y_ref[...] = jnp.concatenate([high, high, low], axis=1)


def total_of(products):
    while len(products) > 1:
        pairs = [a + b for a, b in zip(products[::2], products[1::2])]
        products = pairs + products[len(pairs) * 2 :]
    return products[0]


def values_of(ref, base, groups, half, group, p):
    at = base + ((half * groups + group) * ROWS + p) * ROWS
    return ref[at : at + ROWS, :]


def project(field, chunks, corner_ref, flat_ref, start_ref=None):
    groups = flat_ref.shape[0]
    lane_block = iota((ROWS, LANES), 1) // SZ

    def one(group, carry):
        corners = [corner_ref[0, group * ROWS + u] for u in range(ROWS)]
        shifts = [
            lax.rem(LANES + u * SZ - corner_ref[2, group * ROWS + u], LANES) for u in range(ROWS)
        ]
        sums = [[] for _ in range(ROWS)]
        for plane, ref, base in chunks:
            for half in range(HALVES):
                box = None
                for u in range(ROWS):
                    turned = pltpu.roll(field(corners[u] + plane, half), shifts[u], 1)
                    box = turned if u == 0 else jnp.where(lane_block == u, turned, box)
                for p in range(ROWS):
                    sums[p].append(values_of(ref, base, groups, half, group, p) * box)
        flat = fold_rows([total_of(products) for products in sums])
        flat_ref[group] = flat if start_ref is None else flat + start_ref[group]
        return carry

    for group in range(groups):
        one(group, 0)


def sum_atoms(flat_ref, member_ref):
    flat = jnp.concatenate([flat_ref[g] for g in range(flat_ref.shape[0])], axis=1)
    return sum_thirds(
        lax.dot_general(
            thirds_of(flat), member_ref[...], (((1,), (1,)), ((), ())),
            preferred_element_type=jnp.float32,
        )
    )


def box_values(scaled, chunks, member_ref, flat_ref, box_ref):
    groups = flat_ref.shape[0]
    flat = sum_thirds(
        jnp.dot(thirds_of(scaled), member_ref[...], preferred_element_type=jnp.float32)
    )
    for g in range(groups):
        flat_ref[g] = flat[:, g * LANES : (g + 1) * LANES]
    for group in range(groups):
        factors = [
            jnp.broadcast_to(flat_ref[group, pl.ds(p, 1), :], (ROWS, LANES)) for p in range(ROWS)
        ]
        for plane, ref, base in chunks:
            for half in range(HALVES):
                box_ref[group, plane * HALVES + half] = total_of(
                    [
                        values_of(ref, base, groups, half, group, p) * factors[p]
                        for p in range(ROWS)
                    ]
                )


def deposit(corner_ref, box_ref, parts_ref):
    copies = parts_ref.shape[0]
    lane_block = iota((ROWS, LANES), 1) // SZ
    for group in range(box_ref.shape[0]):
        for u in range(ROWS):
            slot = group * ROWS + u
            planes = pl.ds(corner_ref[0, slot], SX)
            shift = lax.rem(LANES + corner_ref[2, slot] - u * SZ, LANES)
            for half in range(HALVES):
                at = (u % copies, planes, pl.ds(half * ROWS, ROWS), slice(None))
                added = [
                    pltpu.roll(
                        jnp.where(lane_block == u, box_ref[group, x * HALVES + half], 0.0), shift, 1
                    )
                    for x in range(SX)
                ]
                parts_ref[at] = parts_ref[at] + jnp.stack(added)


def band_matrix(size, block, centre):
    row = iota((size, size), 0)
    column = iota((size, size), 1)
    apart = jnp.abs(row - column)
    table = jnp.where(apart == 0, centre, 0.0)
    for k in range(1, REACH + 1):
        table = jnp.where(apart == k, STENCIL_WEIGHTS[k], table)
    return jnp.where(row // block == column // block, table, 0.0)


def laplacian(padded_ref, extent, along_z_ref, along_y_ref):
    inner = padded_ref[REACH : REACH + extent]
    high, low = halves_of(inner.reshape(extent * SY, LANES))
    along_z = jnp.dot(
        jnp.concatenate([high, high, low], axis=1), along_z_ref[...],
        preferred_element_type=jnp.float32,
    )
    along_y = jnp.dot(
        along_y_ref[...], jnp.concatenate([high, low, high], axis=0),
        preferred_element_type=jnp.float32,
    )
    total = (along_z + along_y).reshape(inner.shape)
    for k in range(1, REACH + 1):
        total = total + STENCIL_WEIGHTS[k] * (
            padded_ref[REACH + k : REACH + k + extent] + padded_ref[REACH - k : REACH - k + extent]
        )
    return total


HALO_ROWS = REACH * SY


def to_rows(table):
    blocks = [table[:, at : at + LANES] for at in range(0, table.shape[1], LANES)]
    return jnp.concatenate(blocks, axis=0)


def from_rows(rows):
    blocks = [rows[at : at + ROWS] for at in range(0, rows.shape[0], ROWS)]
    return jnp.concatenate(blocks, axis=1)


def write_halos(field_ref, odd, mate_ref, cross_ref):
    extent = field_ref.shape[0]
    mate_start = (1 - odd) * (extent - REACH)
    cross_start = odd * (extent - REACH)
    for start, ref in ((mate_start, mate_ref), (cross_start, cross_ref)):
        ref[:HALO_ROWS] = field_ref[pl.ds(start, REACH)].reshape(HALO_ROWS, LANES)


def all_planes(ref):
    rows = ref.shape[0] // SX
    return [(x, ref, x * rows) for x in range(SX)]


def some_planes(first, refs):
    return [(plane_here(first + i), ref, 0) for i, ref in enumerate(refs)]


def field_reader(ref):
    return lambda x, half: ref[x, pl.ds(half * ROWS, ROWS), :]


def halo_kernel(field_ref, mate_ref, cross_ref):
    write_halos(field_ref, odd_here(), mate_ref, cross_ref)


def low_kernel(proj_ref, laden_ref):
    pack_plane(0, HALVES, proj_ref, laden_ref)


def window_kernel(field_ref, laden_ref, out_ref):
    window = field_ref[pl.ds(plane_here(2), REACH)]
    out_ref[out_ref.shape[0] - HALO_ROWS :] = window.reshape(HALO_ROWS, LANES)


def above_kernel(corner_ref, own_laden_ref, high_ref, laden_ref, flat_ref, on_ref):
    rows = on_ref.shape[0]
    on_ref[...] = laden_ref[:rows]

    def field(x, half):
        return laden_ref[pl.ds(pl.multiple_of(rows + x * SY + half * ROWS, ROWS), ROWS), :]

    project(field, [(0, own_laden_ref, 0), (1, high_ref, 0)], corner_ref, flat_ref)


def hand_on_kernel(given_ref, out_ref):
    out_ref[...] = given_ref[...]


def near_kernel(corner_ref, field_ref, low_ref, high_ref, *refs):
    chunks = some_planes(0, [low_ref, high_ref]) + some_planes(4, refs[:-1])
    project(field_reader(field_ref), chunks, corner_ref, refs[-1])


def write_table(flat_ref, member_ref, energy_ref, out_ref):
    sums = sum_atoms(flat_ref, member_ref)
    out_ref[...] = jnp.concatenate([to_rows(sums), to_rows(energy_ref[...])], axis=0)


def last_part_kernel(corner_ref, member_ref, energy_ref, field_ref, near_ref,
                     returned_ref, far_ref, out_ref, flat_ref):
    flat_ref[...] = near_ref[...] + returned_ref[...]
    chunks = some_planes(7, [far_ref])
    project(field_reader(field_ref), chunks, corner_ref, flat_ref, flat_ref)
    write_table(flat_ref, member_ref, energy_ref, out_ref)


def whole_pack_kernel(proj_ref, out_ref):
    pack_plane(0, proj_ref.shape[2] // LANES, proj_ref, out_ref)


def high_kernel(proj_ref, out_ref):
    pack_plane(HALVES, HALVES, proj_ref, out_ref)


def whole_sums_kernel(corner_ref, member_ref, energy_ref, field_ref, whole_ref, out_ref, flat_ref):
    project(field_reader(field_ref), all_planes(whole_ref), corner_ref, flat_ref)
    write_table(flat_ref, member_ref, energy_ref, out_ref)


def step_kernel(index, chunk_count, member_ref, along_z_ref, along_y_ref, field_ref, potential_ref,
                mate_ref, cross_ref, *refs):
    factors = step_factors()
    is_first, is_last = index == 0, index + 1 == len(factors)
    refs = list(refs)
    odd = odd_here()
    own_ref, far_ref = refs.pop(0), refs.pop(0)
    if is_first:
        table = from_rows(own_ref[...] + refs.pop(0)[...] + far_ref[...])
    else:
        table = from_rows(own_ref[HALO_ROWS:] + cross_ref[HALO_ROWS:] + far_ref[...])
    if chunk_count > 1:
        chunks = some_planes(0, refs[:chunk_count])
    else:
        chunks = all_planes(refs[0])
    refs = refs[chunk_count:]
    energy_ref = None if is_first else refs.pop(0)
    before_ref = None if is_first else refs.pop(0)
    corner_hbm = refs.pop(0)
    next_ref = refs.pop(0)
    if not is_last:
        next_mate_ref, next_cross_ref = refs.pop(0), refs.pop(0)
    if is_first:
        energy_ref = refs.pop(0)
    flat_ref, box_ref, parts_ref, padded_ref, corner_ref, corner_sem = refs
    corner_copy = pltpu.make_async_copy(corner_hbm, corner_ref, corner_sem)
    corner_copy.start()
    extent = field_ref.shape[0]
    if is_first:
        atoms = table.shape[1] // 2
        energy_ref[...] = table[:, atoms:]
        table = table[:, :atoms]
    scaled = table * energy_ref[...]
    box_values(scaled, chunks, member_ref, flat_ref, box_ref)

    cells = field_ref[...]
    padded_ref[REACH : REACH + extent] = cells
    mate_at = (1 - odd) * (extent + REACH)
    cross_at = odd * (extent + REACH)
    padded_ref[pl.ds(mate_at, REACH)] = mate_ref[:HALO_ROWS].reshape(REACH, SY, LANES)
    padded_ref[pl.ds(cross_at, REACH)] = cross_ref[:HALO_ROWS].reshape(REACH, SY, LANES)
    value = -0.5 * laplacian(padded_ref, extent, along_z_ref, along_y_ref) + (potential_ref[...] - CENTRE) * cells
    parts_ref[0] = value
    parts_ref[1:] = jnp.zeros((COPIES - 1,) + value.shape, jnp.float32)
    corner_copy.wait()
    deposit(corner_ref, box_ref, parts_ref)
    value = total_of([parts_ref[u] for u in range(COPIES)])
    value = factors[index][0] * value
    if not is_first:
        value = value - factors[index][1] * before_ref[...]
    next_ref[...] = value
    if not is_last:
        project(field_reader(next_ref), chunks, corner_ref, flat_ref)
        sums = sum_atoms(flat_ref, member_ref)
        write_halos(next_ref, odd, next_mate_ref, next_cross_ref)
        next_mate_ref[HALO_ROWS:] = to_rows(sums)
        next_cross_ref[HALO_ROWS:] = to_rows(sums)


VMEM = pl.BlockSpec(memory_space=pltpu.VMEM)
SMEM = pl.BlockSpec(memory_space=pltpu.SMEM)
ANY = pl.BlockSpec(memory_space=pl.ANY)


def swap(values, axis, first):
    count = lax.axis_size(axis)
    pairs = []
    for i in range(first, count - 1, 2):
        pairs += [(i, i + 1), (i + 1, i)]
    return lax.ppermute(values, axis, pairs)


def turn(values, axis, step):
    count = lax.axis_size(axis)
    return lax.ppermute(values, axis, [(i, (i + step) % count) for i in range(count)])


def on_device(wave_block, potential, projectors, kb_energy, slot_atom, slot_corner):
    bands, planes, cells_y, cells_z = wave_block.shape
    assert bands == 1 and cells_y == SY and cells_z == LANES
    slots, proj_count = projectors.shape[:2]
    atom_own = kb_energy.shape[0]
    atoms = atom_own * lax.axis_size("dom")
    groups = slots // ROWS
    tiles = projectors.shape[2] // LANES
    assert proj_count == ROWS and slots % ROWS == 0
    place = lax.axis_index("dom")
    field = wave_block[0]

    def shaped(*shape):
        return jax.ShapeDtypeStruct(shape, jnp.float32)

    def call(kernel, name, out_shape, scalars, operands, scratch, after=(), in_place={}, late=()):
        inputs = len(scalars) + len(operands) + len(late)

        def body(*refs):
            kernel(*refs[:inputs], *refs[inputs + len(after) :])

        return pl.pallas_call(
            body,
            out_shape=out_shape,
            in_specs=[SMEM] * len(scalars) + [VMEM] * len(operands)
            + [ANY] * (len(late) + len(after)),
            out_specs=jax.tree.map(lambda _: VMEM, out_shape),
            scratch_shapes=[
                pltpu.VMEM(shape, jnp.float32) if isinstance(shape, tuple) else shape
                for shape in scratch
            ],
            compiler_params=pltpu.CompilerParams(vmem_limit_bytes=16 * 2**20),
            input_output_aliases=in_place,
            cost_estimate=pl.CostEstimate(flops=0, bytes_accessed=0, transcendentals=0),
            name=name,
        )(*scalars, *operands, *late, *after)

    atom_row = jnp.repeat(slot_atom, SZ)[None, :]
    own_atoms = (jnp.arange(atoms) // atom_own) == place
    energy = jnp.where(own_atoms[None, :], jnp.tile(kb_energy.T, (1, atoms // atom_own)), 0.0)
    flat = (groups, ROWS, LANES)
    boxes = (groups, TILES, ROWS, LANES)
    parts = (COPIES, planes, SY, LANES)
    padded = (planes + 2 * REACH, SY, LANES)
    table_rows = ROWS * atoms // LANES
    sends = [shaped(HALO_ROWS + table_rows, LANES)] * 2

    flat = (groups, ROWS, LANES)
    boxes = (groups, TILES, ROWS, LANES)
    parts = (COPIES, planes, SY, LANES)
    padded = (planes + 2 * REACH, SY, LANES)
    table_rows = ROWS * atoms // LANES
    sends = [shaped(HALO_ROWS + table_rows, LANES)] * 2

    def pack(first_tile, count, after=()):
        return call(
            functools.partial(pack_kernel, first_tile), "pack_projectors",
            shaped(count, groups, ROWS, ROWS, LANES), [], [projectors], [], after,
        )

    tables = call(
        table_kernel, "tables",
        [
            jax.ShapeDtypeStruct(shape, jnp.bfloat16)
            for shape in (
                (atoms, slots * SZ), (3 * LANES, LANES), (planes * SY, 3 * planes * SY)
            )
        ],
        [], [atom_row], [],
    )
    halos = [shaped(HALO_ROWS, LANES)] * 2
    if lax.axis_size("band") == 4 and tiles == 2 * HALVES:
        rows = HALVES * groups * ROWS * ROWS
        plane = shaped(rows, LANES)
        laden = shaped(rows + HALO_ROWS, LANES)
        low = call(low_kernel, "pack_low", laden, [], [projectors], [])
        low = call(
            window_kernel, "add_window", laden, [], [field, low], [], (), {1: 0}
        )
        below_low = turn(low, "band", 1)
        high = call(high_kernel, "pack_high", plane, [], [projectors], [], [low])
        below_high = turn(high, "band", 1)
        returned, on_low = call(
            above_kernel, "project_above", [shaped(*flat), plane], [slot_corner],
            [low, high, below_low], [],
        )
        returned = turn(returned, "band", -1)
        far_low = turn(on_low, "band", 1)

        def hand_on(values, *after):
            return call(hand_on_kernel, "hand_on", plane, [], [values], [], after)

        on_high = hand_on(below_high, on_low, returned)
        far_high = turn(on_high, "band", 1)
        on_far_low = hand_on(far_low, on_high, tables[0], energy)
        above_low = turn(on_far_low, "band", 1)
        mate, cross = call(
            halo_kernel, "cut_halos", halos, [], [field], [], [on_far_low]
        )
        mate, cross = swap(mate, "dom", 0), swap(cross, "dom", 1)
        near = call(
            near_kernel, "project_near", shaped(*flat), [slot_corner],
            [field, low, high, below_low, below_high, far_low], [],
        )
        on_far_high = hand_on(far_high, near, tables[0], energy, mate, cross)
        above_high = turn(on_far_high, "band", 1)
        own = call(
            last_part_kernel, "first_sums", shaped(2 * table_rows, LANES), [slot_corner],
            [tables[0], energy, field, near, returned, far_high], [flat],
        )
        chunks = [low, high, above_low, above_high, below_low, below_high, far_low, far_high]
    else:
        mate, cross = call(halo_kernel, "cut_halos", halos, [], [field], [])
        packed = call(
            whole_pack_kernel, "pack_projectors", shaped(tiles * groups * ROWS * ROWS, LANES),
            [], [projectors], [],
        )
        chunks = [lax.all_gather(packed, "band", axis=0, tiled=True)]
        own = call(
            whole_sums_kernel, "first_sums", shaped(2 * table_rows, LANES), [slot_corner],
            [tables[0], energy, field, *chunks], [flat],
        )
        mate, cross = swap(mate, "dom", 0), swap(cross, "dom", 1)
    own = own + swap(own, "dom", 0)
    other = swap(own, "dom", 1)
    far = swap(other, "dom", 0)
    before = None
    for index in range(DEGREE):
        if index > 0:
            to_mate, to_cross = sent
            mate = swap(to_mate, "dom", 0)
            own = to_cross.at[HALO_ROWS:].add(mate[HALO_ROWS:])
            cross = swap(own, "dom", 1)
            far = swap(cross[HALO_ROWS:], "dom", 0)
        operands = [*tables, field, potential, mate, cross, own, far]
        if index == 0:
            operands.append(other)
        operands += chunks
        out_shape = [shaped(planes, SY, LANES)]
        if index > 0:
            operands += [energy, before]
        if index + 1 < DEGREE:
            out_shape += sends
        if index == 0:
            out_shape += [shaped(ROWS, atoms)]
        result = call(
            functools.partial(step_kernel, index, len(chunks)), f"filter_step_{index + 1}",
            out_shape, [], operands,
            [
                flat, boxes, parts, padded,
                pltpu.SMEM(slot_corner.shape, jnp.int32), pltpu.SemaphoreType.DMA,
            ],
            late=[slot_corner],
        )
        before, field = field, result[0]
        sent = result[1:3]
        if index == 0:
            energy = result[3]
    return field[None]


def solution(mesh):
    placed = (
        P("band", "dom", None, None),
        P("dom", None, None),
        P("dom", None, "band"),
        P("dom", None),
        P("dom"),
        P(None, "dom"),
    )
    return jax.shard_map(
        on_device,
        mesh=mesh,
        in_specs=placed,
        out_specs=P("band", "dom", None, None),
        check_vma=False,
    )
```

```python
import functools

import jax
import jax.numpy as jnp
from jax import lax
from jax.experimental import pallas as pl
from jax.experimental.pallas import tpu as pltpu
from jax.sharding import PartitionSpec as P

SX = 8
SY = 16
SZ = 16
DEGREE = 3
LANES = 128
ROWS = 8
TILES = SX * SY * SZ // LANES
HALVES = SY // ROWS

STENCIL_WEIGHTS = (
    -5369.0 / 1800.0,
    12.0 / 7.0,
    -15.0 / 56.0,
    10.0 / 189.0,
    -1.0 / 112.0,
    2.0 / 1925.0,
    -1.0 / 16632.0,
)
REACH = len(STENCIL_WEIGHTS) - 1
LOWER_EDGE = 3.0
UPPER_EDGE = 30.0
ANCHOR_POINT = 0.5
HALF_WIDTH = (UPPER_EDGE - LOWER_EDGE) / 2.0
CENTRE = (UPPER_EDGE + LOWER_EDGE) / 2.0
SIGMA_FIRST = HALF_WIDTH / (ANCHOR_POINT - CENTRE)
COPIES = 4
PARTS_FROM = (0, 1, 3, 2)


def step_factors():
    sigma_now = SIGMA_FIRST
    factors = [(SIGMA_FIRST / HALF_WIDTH, 0.0)]
    for _ in range(2, DEGREE + 1):
        sigma_next = 1.0 / (2.0 / SIGMA_FIRST - sigma_now)
        factors.append((2.0 * sigma_next / HALF_WIDTH, sigma_now * sigma_next))
        sigma_now = sigma_next
    return factors


def odd_here():
    return lax.rem(lax.axis_index("dom"), 2)


def plane_here(index):
    owner = lax.rem(lax.axis_index("band") + PARTS_FROM[index // 2], 4)
    return owner * 2 + index % 2


def iota(shape, dim):
    return lax.broadcasted_iota(jnp.int32, shape, dim)


def fold_rows(blocks):
    row = iota((ROWS, LANES), 0)
    distance = 1
    while len(blocks) > 1:
        first = (row // distance) % 2 == 0
        blocks = [
            jnp.where(first, a, b) + pltpu.roll(jnp.where(first, b, a), distance, 0)
            for a, b in zip(blocks[::2], blocks[1::2])
        ]
        distance *= 2
    return blocks[0]


def choose(masks, values):
    result = values[-1]
    for mask, value in zip(masks[:-1], values[:-1]):
        result = jnp.where(mask, value, result)
    return result


def pack_plane(first_tile, tiles, proj_ref, out_ref):
    groups = proj_ref.shape[0] // ROWS
    row = iota((ROWS, LANES), 0)
    block = iota((ROWS, LANES), 1) // SZ
    apart = (row - block + ROWS) % ROWS
    block_is = [block == b for b in range(ROWS)]
    row_is = [row == r for r in range(ROWS)]
    apart_is = [apart == d for d in range(ROWS)]

    def one(index, carry):
        tile, group = index // groups, index % groups
        cells = pl.ds(pl.multiple_of((first_tile + tile) * LANES, LANES), LANES)
        given = [proj_ref[group * ROWS + u, :, cells] for u in range(ROWS)]
        by_lane = []
        for d in range(ROWS):
            mixed = choose(block_is, [given[(b - d) % ROWS] for b in range(ROWS)])
            by_lane.append(pltpu.roll(mixed, (LANES - d * SZ) % LANES, 1) if d else mixed)
        by_row = []
        for e in range(ROWS):
            mixed = choose(apart_is, [by_lane[(d + e) % ROWS] for d in range(ROWS)])
            by_row.append(pltpu.roll(mixed, e, 0) if e else mixed)
        for p in range(ROWS):
            at = pl.ds(pl.multiple_of((index * ROWS + p) * ROWS, ROWS), ROWS)
            out_ref[at, :] = choose(row_is, [by_row[(j - p) % ROWS] for j in range(ROWS)])
        return carry

    lax.fori_loop(0, tiles * groups, one, 0)


def halves_of(value):
    high = value.astype(jnp.bfloat16)
    return high, (value - high.astype(jnp.float32)).astype(jnp.bfloat16)


def thirds_of(value):
    rest, parts = value, []
    for _ in range(3):
        high = rest.astype(jnp.bfloat16).astype(jnp.float32)
        parts.append(high)
        rest = rest - high
    return jnp.concatenate(parts, axis=0).astype(jnp.bfloat16)


def sum_thirds(value):
    return value[:ROWS] + value[ROWS : 2 * ROWS] + value[2 * ROWS :]


def table_kernel(atom_row_ref, member_ref, along_z_ref, along_y_ref):
    atoms = iota(member_ref.shape, 0)
    member_ref[...] = (atoms == atom_row_ref[...]).astype(jnp.float32).astype(jnp.bfloat16)
    high, low = halves_of(band_matrix(LANES, LANES, 3.0 * STENCIL_WEIGHTS[0]))
    along_z_ref[...] = jnp.concatenate([high, low, high], axis=0)
    high, low = halves_of(band_matrix(along_y_ref.shape[0], SY, 0.0))
    along_y_ref[...] = jnp.concatenate([high, high, low], axis=1)


def total_of(products):
    while len(products) > 1:
        pairs = [a + b for a, b in zip(products[::2], products[1::2])]
        products = pairs + products[len(pairs) * 2 :]
    return products[0]


def values_of(ref, base, groups, half, group, p):
    at = base + ((half * groups + group) * ROWS + p) * ROWS
    return ref[at : at + ROWS, :]


def project(field, chunks, corner_ref, flat_ref, start_ref=None):
    groups = flat_ref.shape[0]
    lane_block = iota((ROWS, LANES), 1) // SZ

    def one(group, carry):
        corners = [corner_ref[0, group * ROWS + u] for u in range(ROWS)]
        shifts = [
            lax.rem(LANES + u * SZ - corner_ref[2, group * ROWS + u], LANES) for u in range(ROWS)
        ]
        sums = [[] for _ in range(ROWS)]
        for plane, ref, base in chunks:
            for half in range(HALVES):
                box = None
                for u in range(ROWS):
                    turned = pltpu.roll(field(corners[u] + plane, half), shifts[u], 1)
                    box = turned if u == 0 else jnp.where(lane_block == u, turned, box)
                for p in range(ROWS):
                    sums[p].append(values_of(ref, base, groups, half, group, p) * box)
        flat = fold_rows([total_of(products) for products in sums])
        flat_ref[group] = flat if start_ref is None else flat + start_ref[group]
        return carry

    for group in range(groups):
        one(group, 0)


def sum_atoms(flat_ref, member_ref):
    flat = jnp.concatenate([flat_ref[g] for g in range(flat_ref.shape[0])], axis=1)
    return sum_thirds(
        lax.dot_general(
            thirds_of(flat), member_ref[...], (((1,), (1,)), ((), ())),
            preferred_element_type=jnp.float32,
        )
    )


def box_values(scaled, chunks, member_ref, flat_ref, box_ref):
    groups = flat_ref.shape[0]
    flat = sum_thirds(
        jnp.dot(thirds_of(scaled), member_ref[...], preferred_element_type=jnp.float32)
    )
    for g in range(groups):
        flat_ref[g] = flat[:, g * LANES : (g + 1) * LANES]
    for group in range(groups):
        factors = [
            jnp.broadcast_to(flat_ref[group, pl.ds(p, 1), :], (ROWS, LANES)) for p in range(ROWS)
        ]
        for plane, ref, base in chunks:
            for half in range(HALVES):
                box_ref[group, plane * HALVES + half] = total_of(
                    [
                        values_of(ref, base, groups, half, group, p) * factors[p]
                        for p in range(ROWS)
                    ]
                )


def deposit(corner_ref, box_ref, parts_ref):
    copies = parts_ref.shape[0]
    lane_block = iota((ROWS, LANES), 1) // SZ
    for group in range(box_ref.shape[0]):
        for u in range(ROWS):
            slot = group * ROWS + u
            planes = pl.ds(corner_ref[0, slot], SX)
            shift = lax.rem(LANES + corner_ref[2, slot] - u * SZ, LANES)
            for half in range(HALVES):
                at = (u % copies, planes, pl.ds(half * ROWS, ROWS), slice(None))
                added = [
                    pltpu.roll(
                        jnp.where(lane_block == u, box_ref[group, x * HALVES + half], 0.0), shift, 1
                    )
                    for x in range(SX)
                ]
                parts_ref[at] = parts_ref[at] + jnp.stack(added)


def band_matrix(size, block, centre):
    row = iota((size, size), 0)
    column = iota((size, size), 1)
    apart = jnp.abs(row - column)
    table = jnp.where(apart == 0, centre, 0.0)
    for k in range(1, REACH + 1):
        table = jnp.where(apart == k, STENCIL_WEIGHTS[k], table)
    return jnp.where(row // block == column // block, table, 0.0)


HALO_ROWS = REACH * SY


def to_rows(table):
    blocks = [table[:, at : at + LANES] for at in range(0, table.shape[1], LANES)]
    return jnp.concatenate(blocks, axis=0)


def from_rows(rows):
    blocks = [rows[at : at + ROWS] for at in range(0, rows.shape[0], ROWS)]
    return jnp.concatenate(blocks, axis=1)


def write_halos(field_ref, odd, mate_ref, cross_ref):
    extent = field_ref.shape[0]
    mate_start = (1 - odd) * (extent - REACH)
    cross_start = odd * (extent - REACH)
    for start, ref in ((mate_start, mate_ref), (cross_start, cross_ref)):
        ref[:HALO_ROWS] = field_ref[pl.ds(start, REACH)].reshape(HALO_ROWS, LANES)


def all_planes(ref):
    rows = ref.shape[0] // SX
    return [(x, ref, x * rows) for x in range(SX)]


def some_planes(first, refs):
    return [(plane_here(first + i), ref, 0) for i, ref in enumerate(refs)]


def field_reader(ref):
    return lambda x, half: ref[x, pl.ds(half * ROWS, ROWS), :]


def halo_kernel(field_ref, mate_ref, cross_ref):
    write_halos(field_ref, odd_here(), mate_ref, cross_ref)


def low_kernel(proj_ref, laden_ref):
    pack_plane(0, HALVES, proj_ref, laden_ref)


def window_kernel(field_ref, laden_ref, out_ref):
    window = field_ref[pl.ds(plane_here(2), REACH)]
    out_ref[out_ref.shape[0] - HALO_ROWS :] = window.reshape(HALO_ROWS, LANES)


def above_kernel(corner_ref, own_laden_ref, high_ref, laden_ref, flat_ref, on_ref):
    rows = on_ref.shape[0]
    on_ref[...] = laden_ref[:rows]

    def field(x, half):
        return laden_ref[pl.ds(pl.multiple_of(rows + x * SY + half * ROWS, ROWS), ROWS), :]

    project(field, [(0, own_laden_ref, 0), (1, high_ref, 0)], corner_ref, flat_ref)


def hand_on_kernel(given_ref, out_ref):
    out_ref[...] = given_ref[...]


def near_kernel(corner_ref, field_ref, low_ref, high_ref, *refs):
    chunks = some_planes(0, [low_ref, high_ref]) + some_planes(4, refs[:-1])
    project(field_reader(field_ref), chunks, corner_ref, refs[-1])


def write_table(flat_ref, member_ref, energy_ref, out_ref):
    sums = sum_atoms(flat_ref, member_ref)
    out_ref[...] = jnp.concatenate([to_rows(sums), to_rows(energy_ref[...])], axis=0)


def last_part_kernel(corner_ref, member_ref, energy_ref, field_ref, near_ref,
                     returned_ref, far_ref, out_ref, flat_ref):
    flat_ref[...] = near_ref[...] + returned_ref[...]
    chunks = some_planes(7, [far_ref])
    project(field_reader(field_ref), chunks, corner_ref, flat_ref, flat_ref)
    write_table(flat_ref, member_ref, energy_ref, out_ref)


def whole_pack_kernel(proj_ref, out_ref):
    pack_plane(0, proj_ref.shape[2] // LANES, proj_ref, out_ref)


def high_kernel(proj_ref, out_ref):
    pack_plane(HALVES, HALVES, proj_ref, out_ref)


def whole_sums_kernel(corner_ref, member_ref, energy_ref, field_ref, whole_ref, out_ref, flat_ref):
    project(field_reader(field_ref), all_planes(whole_ref), corner_ref, flat_ref)
    write_table(flat_ref, member_ref, energy_ref, out_ref)


def local_kernel(index, along_z_ref, along_y_ref, field_ref, potential_ref, mate_ref, *refs):
    refs = list(refs)
    before_ref = refs.pop(0) if index > 0 else None
    out_ref, padded_ref = refs
    first, second = step_factors()[index]
    extent = field_ref.shape[0]
    odd = odd_here()
    cells = field_ref[...]
    padded_ref[REACH : REACH + extent] = cells
    mate_at = (1 - odd) * (extent + REACH)
    cross_at = odd * (extent + REACH)
    padded_ref[pl.ds(mate_at, REACH)] = mate_ref[:HALO_ROWS].reshape(REACH, SY, LANES)
    padded_ref[pl.ds(cross_at, REACH)] = jnp.zeros((REACH, SY, LANES), jnp.float32)
    high, low = halves_of(cells.reshape(extent * SY, LANES))
    along_z = jnp.dot(
        jnp.concatenate([high, high, low], axis=1), along_z_ref[...],
        preferred_element_type=jnp.float32,
    )
    along_y = jnp.dot(
        along_y_ref[...], jnp.concatenate([high, low, high], axis=0),
        preferred_element_type=jnp.float32,
    )
    total = (along_z + along_y).reshape(cells.shape)
    for k in range(1, REACH + 1):
        total = total + STENCIL_WEIGHTS[k] * (
            padded_ref[REACH + k : REACH + k + extent] + padded_ref[REACH - k : REACH - k + extent]
        )
    total = -0.5 * total + (potential_ref[...] - CENTRE) * cells
    if index > 0:
        total = total - (second / first) * before_ref[...]
    out_ref[...] = total


def add_cross_halo(cross_ref, parts_ref, extent):
    odd = odd_here()
    for near in range(REACH):
        total = None
        for k in range(near + 1, REACH + 1):
            plane = odd * (k - 1 - near) + (1 - odd) * (REACH + near - k)
            cells = cross_ref[pl.ds(pl.multiple_of(plane * SY, SY), SY), :]
            term = (-0.5 * STENCIL_WEIGHTS[k]) * cells
            total = term if total is None else total + term
        at = (0, odd * (extent - 1 - near) + (1 - odd) * near)
        parts_ref[at] = parts_ref[at] + total


def step_kernel(index, chunk_count, member_ref, local_ref, cross_ref, *refs):
    first, _ = step_factors()[index]
    is_first, is_last = index == 0, index + 1 == DEGREE
    refs = list(refs)
    own_ref, far_ref = refs.pop(0), refs.pop(0)
    if is_first:
        table = from_rows(own_ref[...] + refs.pop(0)[...] + far_ref[...])
    else:
        table = from_rows(own_ref[HALO_ROWS:] + cross_ref[HALO_ROWS:] + far_ref[...])
    if chunk_count > 1:
        chunks = some_planes(0, refs[:chunk_count])
    else:
        chunks = all_planes(refs[0])
    refs = refs[chunk_count:]
    energy_ref = None if is_first else refs.pop(0)
    corner_hbm = refs.pop(0)
    next_ref = refs.pop(0)
    if not is_last:
        next_mate_ref, next_cross_ref = refs.pop(0), refs.pop(0)
    if is_first:
        energy_ref = refs.pop(0)
    flat_ref, box_ref, parts_ref, corner_ref, corner_sem = refs
    corner_copy = pltpu.make_async_copy(corner_hbm, corner_ref, corner_sem)
    corner_copy.start()
    if is_first:
        atoms = table.shape[1] // 2
        energy_ref[...] = table[:, atoms:]
        table = table[:, :atoms]
    scaled = table * energy_ref[...]
    box_values(scaled, chunks, member_ref, flat_ref, box_ref)
    parts_ref[0] = local_ref[...]
    parts_ref[1:] = jnp.zeros((COPIES - 1,) + local_ref.shape, jnp.float32)
    add_cross_halo(cross_ref, parts_ref, local_ref.shape[0])
    corner_copy.wait()
    deposit(corner_ref, box_ref, parts_ref)
    next_ref[...] = first * total_of([parts_ref[u] for u in range(COPIES)])
    if not is_last:
        project(field_reader(next_ref), chunks, corner_ref, flat_ref)
        sums = sum_atoms(flat_ref, member_ref)
        write_halos(next_ref, odd_here(), next_mate_ref, next_cross_ref)
        next_mate_ref[HALO_ROWS:] = to_rows(sums)
        next_cross_ref[HALO_ROWS:] = to_rows(sums)


VMEM = pl.BlockSpec(memory_space=pltpu.VMEM)
SMEM = pl.BlockSpec(memory_space=pltpu.SMEM)
ANY = pl.BlockSpec(memory_space=pl.ANY)
NO_COST = pl.CostEstimate(flops=0, bytes_accessed=0, transcendentals=0)
LOCAL_COST = pl.CostEstimate(flops=5 * 10**7, bytes_accessed=10**6, transcendentals=0)


def swap(values, axis, first):
    count = lax.axis_size(axis)
    pairs = []
    for i in range(first, count - 1, 2):
        pairs += [(i, i + 1), (i + 1, i)]
    return lax.ppermute(values, axis, pairs)


def turn(values, axis, step):
    count = lax.axis_size(axis)
    return lax.ppermute(values, axis, [(i, (i + step) % count) for i in range(count)])


def on_device(wave_block, potential, projectors, kb_energy, slot_atom, slot_corner):
    bands, planes, cells_y, cells_z = wave_block.shape
    assert bands == 1 and cells_y == SY and cells_z == LANES
    slots, proj_count = projectors.shape[:2]
    atom_own = kb_energy.shape[0]
    atoms = atom_own * lax.axis_size("dom")
    groups = slots // ROWS
    tiles = projectors.shape[2] // LANES
    assert proj_count == ROWS and slots % ROWS == 0
    place = lax.axis_index("dom")
    field = wave_block[0]

    def shaped(*shape):
        return jax.ShapeDtypeStruct(shape, jnp.float32)

    def call(kernel, name, out_shape, scalars, operands, scratch, after=(), in_place={}, late=(),
             cost=NO_COST):
        inputs = len(scalars) + len(operands) + len(late)

        def body(*refs):
            kernel(*refs[:inputs], *refs[inputs + len(after) :])

        return pl.pallas_call(
            body,
            out_shape=out_shape,
            in_specs=[SMEM] * len(scalars) + [VMEM] * len(operands)
            + [ANY] * (len(late) + len(after)),
            out_specs=jax.tree.map(lambda _: VMEM, out_shape),
            scratch_shapes=[
                pltpu.VMEM(shape, jnp.float32) if isinstance(shape, tuple) else shape
                for shape in scratch
            ],
            compiler_params=pltpu.CompilerParams(vmem_limit_bytes=16 * 2**20),
            input_output_aliases=in_place,
            cost_estimate=cost,
            name=name,
        )(*scalars, *operands, *late, *after)

    atom_row = jnp.repeat(slot_atom, SZ)[None, :]
    own_atoms = (jnp.arange(atoms) // atom_own) == place
    energy = jnp.where(own_atoms[None, :], jnp.tile(kb_energy.T, (1, atoms // atom_own)), 0.0)
    flat = (groups, ROWS, LANES)
    boxes = (groups, TILES, ROWS, LANES)
    parts = (COPIES, planes, SY, LANES)
    padded = (planes + 2 * REACH, SY, LANES)
    table_rows = ROWS * atoms // LANES
    sends = [shaped(HALO_ROWS + table_rows, LANES)] * 2

    flat = (groups, ROWS, LANES)
    boxes = (groups, TILES, ROWS, LANES)
    parts = (COPIES, planes, SY, LANES)
    padded = (planes + 2 * REACH, SY, LANES)
    table_rows = ROWS * atoms // LANES
    sends = [shaped(HALO_ROWS + table_rows, LANES)] * 2

    def pack(first_tile, count, after=()):
        return call(
            functools.partial(pack_kernel, first_tile), "pack_projectors",
            shaped(count, groups, ROWS, ROWS, LANES), [], [projectors], [], after,
        )

    tables = call(
        table_kernel, "tables",
        [
            jax.ShapeDtypeStruct(shape, jnp.bfloat16)
            for shape in (
                (atoms, slots * SZ), (3 * LANES, LANES), (planes * SY, 3 * planes * SY)
            )
        ],
        [], [atom_row], [],
    )
    halos = [shaped(HALO_ROWS, LANES)] * 2
    if lax.axis_size("band") == 4 and tiles == 2 * HALVES:
        rows = HALVES * groups * ROWS * ROWS
        plane = shaped(rows, LANES)
        laden = shaped(rows + HALO_ROWS, LANES)
        low = call(low_kernel, "pack_low", laden, [], [projectors], [])
        low = call(
            window_kernel, "add_window", laden, [], [field, low], [], (), {1: 0}
        )
        below_low = turn(low, "band", 1)
        high = call(high_kernel, "pack_high", plane, [], [projectors], [], [low])
        below_high = turn(high, "band", 1)
        returned, on_low = call(
            above_kernel, "project_above", [shaped(*flat), plane], [slot_corner],
            [low, high, below_low], [],
        )
        returned = turn(returned, "band", -1)
        far_low = turn(on_low, "band", 1)

        def hand_on(values, *after):
            return call(hand_on_kernel, "hand_on", plane, [], [values], [], after)

        on_high = hand_on(below_high, on_low, returned)
        far_high = turn(on_high, "band", 1)
        on_far_low = hand_on(far_low, on_high, tables[0], energy)
        above_low = turn(on_far_low, "band", 1)
        mate, cross = call(
            halo_kernel, "cut_halos", halos, [], [field], [], [on_far_low]
        )
        mate, cross = swap(mate, "dom", 0), swap(cross, "dom", 1)
        near = call(
            near_kernel, "project_near", shaped(*flat), [slot_corner],
            [field, low, high, below_low, below_high, far_low], [],
        )
        on_far_high = hand_on(far_high, near, tables[0], energy, mate, cross)
        above_high = turn(on_far_high, "band", 1)
        own = call(
            last_part_kernel, "first_sums", shaped(2 * table_rows, LANES), [slot_corner],
            [tables[0], energy, field, near, returned, far_high], [flat],
        )
        chunks = [low, high, above_low, above_high, below_low, below_high, far_low, far_high]
    else:
        mate, cross = call(halo_kernel, "cut_halos", halos, [], [field], [])
        packed = call(
            whole_pack_kernel, "pack_projectors", shaped(tiles * groups * ROWS * ROWS, LANES),
            [], [projectors], [],
        )
        chunks = [lax.all_gather(packed, "band", axis=0, tiled=True)]
        own = call(
            whole_sums_kernel, "first_sums", shaped(2 * table_rows, LANES), [slot_corner],
            [tables[0], energy, field, *chunks], [flat],
        )
        mate, cross = swap(mate, "dom", 0), swap(cross, "dom", 1)
    own = own + swap(own, "dom", 0)
    other = swap(own, "dom", 1)
    far = swap(other, "dom", 0)
    before = None
    for index in range(DEGREE):
        if index > 0:
            to_mate, to_cross = sent
            mate = swap(to_mate, "dom", 0)
            own = to_cross.at[HALO_ROWS:].add(mate[HALO_ROWS:])
            cross = swap(own, "dom", 1)
            far = swap(cross[HALO_ROWS:], "dom", 0)
        local = call(
            functools.partial(local_kernel, index), f"local_{index + 1}",
            shaped(planes, SY, LANES), [],
            [*tables[1:], field, potential, mate] + ([before] if index > 0 else []), [padded],
            cost=LOCAL_COST,
        )
        operands = [tables[0], local, cross, own, far]
        if index == 0:
            operands.append(other)
        operands += chunks
        out_shape = [shaped(planes, SY, LANES)]
        if index > 0:
            operands.append(energy)
        if index + 1 < DEGREE:
            out_shape += sends
        if index == 0:
            out_shape += [shaped(ROWS, atoms)]
        result = call(
            functools.partial(step_kernel, index, len(chunks)), f"filter_step_{index + 1}",
            out_shape, [], operands,
            [
                flat, boxes, parts,
                pltpu.SMEM(slot_corner.shape, jnp.int32), pltpu.SemaphoreType.DMA,
            ],
            late=[slot_corner],
        )
        before, field = field, result[0]
        sent = result[1:3]
        if index == 0:
            energy = result[3]
    return field[None]


def solution(mesh):
    placed = (
        P("band", "dom", None, None),
        P("dom", None, None),
        P("dom", None, "band"),
        P("dom", None),
        P("dom"),
        P(None, "dom"),
    )
    return jax.shard_map(
        on_device,
        mesh=mesh,
        in_specs=placed,
        out_specs=P("band", "dom", None, None),
        check_vma=False,
    )
```

```python
import functools

import jax
import jax.numpy as jnp
from jax import lax
from jax.experimental import pallas as pl
from jax.experimental.pallas import tpu as pltpu
from jax.sharding import PartitionSpec as P

SX = 8
SY = 16
SZ = 16
DEGREE = 3
LANES = 128
ROWS = 8
TILES = SX * SY * SZ // LANES
HALVES = SY // ROWS

STENCIL_WEIGHTS = (
    -5369.0 / 1800.0,
    12.0 / 7.0,
    -15.0 / 56.0,
    10.0 / 189.0,
    -1.0 / 112.0,
    2.0 / 1925.0,
    -1.0 / 16632.0,
)
REACH = len(STENCIL_WEIGHTS) - 1
LOWER_EDGE = 3.0
UPPER_EDGE = 30.0
ANCHOR_POINT = 0.5
HALF_WIDTH = (UPPER_EDGE - LOWER_EDGE) / 2.0
CENTRE = (UPPER_EDGE + LOWER_EDGE) / 2.0
SIGMA_FIRST = HALF_WIDTH / (ANCHOR_POINT - CENTRE)
COPIES = 4
PARTS_FROM = (0, 1, 3, 2)


def step_factors():
    sigma_now = SIGMA_FIRST
    factors = [(SIGMA_FIRST / HALF_WIDTH, 0.0)]
    for _ in range(2, DEGREE + 1):
        sigma_next = 1.0 / (2.0 / SIGMA_FIRST - sigma_now)
        factors.append((2.0 * sigma_next / HALF_WIDTH, sigma_now * sigma_next))
        sigma_now = sigma_next
    return factors


def odd_here():
    return lax.rem(lax.axis_index("dom"), 2)


def plane_here(index):
    owner = lax.rem(lax.axis_index("band") + PARTS_FROM[index // 2], 4)
    return owner * 2 + index % 2


def iota(shape, dim):
    return lax.broadcasted_iota(jnp.int32, shape, dim)


def fold_rows(blocks):
    row = iota((ROWS, LANES), 0)
    distance = 1
    while len(blocks) > 1:
        first = (row // distance) % 2 == 0
        blocks = [
            jnp.where(first, a, b) + pltpu.roll(jnp.where(first, b, a), distance, 0)
            for a, b in zip(blocks[::2], blocks[1::2])
        ]
        distance *= 2
    return blocks[0]


def choose(masks, values):
    result = values[-1]
    for mask, value in zip(masks[:-1], values[:-1]):
        result = jnp.where(mask, value, result)
    return result


def pack_plane(first_tile, tiles, proj_ref, out_ref):
    groups = proj_ref.shape[0] // ROWS
    row = iota((ROWS, LANES), 0)
    block = iota((ROWS, LANES), 1) // SZ
    apart = (row - block + ROWS) % ROWS
    block_is = [block == b for b in range(ROWS)]
    row_is = [row == r for r in range(ROWS)]
    apart_is = [apart == d for d in range(ROWS)]

    def one(index, carry):
        tile, group = index // groups, index % groups
        cells = pl.ds(pl.multiple_of((first_tile + tile) * LANES, LANES), LANES)
        given = [proj_ref[group * ROWS + u, :, cells] for u in range(ROWS)]
        by_lane = []
        for d in range(ROWS):
            mixed = choose(block_is, [given[(b - d) % ROWS] for b in range(ROWS)])
            by_lane.append(pltpu.roll(mixed, (LANES - d * SZ) % LANES, 1) if d else mixed)
        by_row = []
        for e in range(ROWS):
            mixed = choose(apart_is, [by_lane[(d + e) % ROWS] for d in range(ROWS)])
            by_row.append(pltpu.roll(mixed, e, 0) if e else mixed)
        for p in range(ROWS):
            at = pl.ds(pl.multiple_of((index * ROWS + p) * ROWS, ROWS), ROWS)
            out_ref[at, :] = choose(row_is, [by_row[(j - p) % ROWS] for j in range(ROWS)])
        return carry

    lax.fori_loop(0, tiles * groups, one, 0)


def halves_of(value):
    high = value.astype(jnp.bfloat16)
    return high, (value - high.astype(jnp.float32)).astype(jnp.bfloat16)


def thirds_of(value):
    rest, parts = value, []
    for _ in range(3):
        high = rest.astype(jnp.bfloat16).astype(jnp.float32)
        parts.append(high)
        rest = rest - high
    return jnp.concatenate(parts, axis=0).astype(jnp.bfloat16)


def sum_thirds(value):
    return value[:ROWS] + value[ROWS : 2 * ROWS] + value[2 * ROWS :]


def table_kernel(atom_row_ref, member_ref, along_z_ref, along_y_ref):
    atoms = iota(member_ref.shape, 0)
    member_ref[...] = (atoms == atom_row_ref[...]).astype(jnp.float32).astype(jnp.bfloat16)
    high, low = halves_of(band_matrix(LANES, LANES, 3.0 * STENCIL_WEIGHTS[0]))
    along_z_ref[...] = jnp.concatenate([high, low, high], axis=0)
    high, low = halves_of(band_matrix(along_y_ref.shape[0], SY, 0.0))
    along_y_ref[...] = jnp.concatenate([high, high, low], axis=1)


def total_of(products):
    while len(products) > 1:
        pairs = [a + b for a, b in zip(products[::2], products[1::2])]
        products = pairs + products[len(pairs) * 2 :]
    return products[0]


def values_of(ref, base, groups, half, group, p):
    at = base + ((half * groups + group) * ROWS + p) * ROWS
    return ref[at : at + ROWS, :]


def project(field, chunks, corner_ref, flat_ref, start_ref=None):
    groups = flat_ref.shape[0]
    lane_block = iota((ROWS, LANES), 1) // SZ

    def one(group, carry):
        corners = [corner_ref[0, group * ROWS + u] for u in range(ROWS)]
        shifts = [
            lax.rem(LANES + u * SZ - corner_ref[2, group * ROWS + u], LANES) for u in range(ROWS)
        ]
        sums = [[] for _ in range(ROWS)]
        for plane, ref, base in chunks:
            for half in range(HALVES):
                box = None
                for u in range(ROWS):
                    turned = pltpu.roll(field(corners[u] + plane, half), shifts[u], 1)
                    box = turned if u == 0 else jnp.where(lane_block == u, turned, box)
                for p in range(ROWS):
                    sums[p].append(values_of(ref, base, groups, half, group, p) * box)
        flat = fold_rows([total_of(products) for products in sums])
        flat_ref[group] = flat if start_ref is None else flat + start_ref[group]
        return carry

    for group in range(groups):
        one(group, 0)


def sum_atoms(flat_ref, member_ref):
    flat = jnp.concatenate([flat_ref[g] for g in range(flat_ref.shape[0])], axis=1)
    return sum_thirds(
        lax.dot_general(
            thirds_of(flat), member_ref[...], (((1,), (1,)), ((), ())),
            preferred_element_type=jnp.float32,
        )
    )


def box_values(scaled, chunks, member_ref, flat_ref, box_ref):
    groups = flat_ref.shape[0]
    flat = sum_thirds(
        jnp.dot(thirds_of(scaled), member_ref[...], preferred_element_type=jnp.float32)
    )
    for g in range(groups):
        flat_ref[g] = flat[:, g * LANES : (g + 1) * LANES]
    for group in range(groups):
        factors = [
            jnp.broadcast_to(flat_ref[group, pl.ds(p, 1), :], (ROWS, LANES)) for p in range(ROWS)
        ]
        for plane, ref, base in chunks:
            for half in range(HALVES):
                box_ref[group, plane * HALVES + half] = total_of(
                    [
                        values_of(ref, base, groups, half, group, p) * factors[p]
                        for p in range(ROWS)
                    ]
                )


def deposit(corner_ref, box_ref, parts_refs):
    lane_block = iota((ROWS, LANES), 1) // SZ
    for group in range(box_ref.shape[0]):
        for u in range(ROWS):
            slot = group * ROWS + u
            part_ref = parts_refs[u % len(parts_refs)]
            planes = pl.ds(corner_ref[0, slot], SX)
            shift = lax.rem(LANES + corner_ref[2, slot] - u * SZ, LANES)
            turned = [
                pltpu.roll(jnp.where(lane_block == u, box_ref[group, tile], 0.0), shift, 1)
                for tile in range(TILES)
            ]
            added = [
                jnp.concatenate(turned[x * HALVES : (x + 1) * HALVES], axis=0) for x in range(SX)
            ]
            part_ref[planes] = part_ref[planes] + jnp.stack(added)


def band_matrix(size, block, centre):
    row = iota((size, size), 0)
    column = iota((size, size), 1)
    apart = jnp.abs(row - column)
    table = jnp.where(apart == 0, centre, 0.0)
    for k in range(1, REACH + 1):
        table = jnp.where(apart == k, STENCIL_WEIGHTS[k], table)
    return jnp.where(row // block == column // block, table, 0.0)


HALO_ROWS = REACH * SY


def to_rows(table):
    blocks = [table[:, at : at + LANES] for at in range(0, table.shape[1], LANES)]
    return jnp.concatenate(blocks, axis=0)


def from_rows(rows):
    blocks = [rows[at : at + ROWS] for at in range(0, rows.shape[0], ROWS)]
    return jnp.concatenate(blocks, axis=1)


def write_halos(field_ref, odd, mate_ref, cross_ref):
    extent = field_ref.shape[0]
    mate_start = (1 - odd) * (extent - REACH)
    cross_start = odd * (extent - REACH)
    for start, ref in ((mate_start, mate_ref), (cross_start, cross_ref)):
        ref[:HALO_ROWS] = field_ref[pl.ds(start, REACH)].reshape(HALO_ROWS, LANES)


def all_planes(ref):
    rows = ref.shape[0] // SX
    return [(x, ref, x * rows) for x in range(SX)]


def some_planes(first, refs):
    return [(plane_here(first + i), ref, 0) for i, ref in enumerate(refs)]


def field_reader(ref):
    return lambda x, half: ref[x, pl.ds(half * ROWS, ROWS), :]


def halo_kernel(field_ref, mate_ref, cross_ref):
    write_halos(field_ref, odd_here(), mate_ref, cross_ref)


def low_kernel(proj_ref, laden_ref):
    pack_plane(0, HALVES, proj_ref, laden_ref)


def window_kernel(field_ref, laden_ref, out_ref):
    window = field_ref[pl.ds(plane_here(2), REACH)]
    out_ref[out_ref.shape[0] - HALO_ROWS :] = window.reshape(HALO_ROWS, LANES)


def above_kernel(corner_ref, own_laden_ref, high_ref, laden_ref, flat_ref, on_ref):
    rows = on_ref.shape[0]
    on_ref[...] = laden_ref[:rows]

    def field(x, half):
        return laden_ref[pl.ds(pl.multiple_of(rows + x * SY + half * ROWS, ROWS), ROWS), :]

    project(field, [(0, own_laden_ref, 0), (1, high_ref, 0)], corner_ref, flat_ref)


def hand_on_kernel(given_ref, out_ref):
    out_ref[...] = given_ref[...]


def near_kernel(corner_ref, field_ref, low_ref, high_ref, *refs):
    chunks = some_planes(0, [low_ref, high_ref]) + some_planes(4, refs[:-1])
    project(field_reader(field_ref), chunks, corner_ref, refs[-1])


def write_table(flat_ref, member_ref, energy_ref, out_ref):
    sums = sum_atoms(flat_ref, member_ref)
    out_ref[...] = jnp.concatenate([to_rows(sums), to_rows(energy_ref[...])], axis=0)


def last_part_kernel(corner_ref, member_ref, energy_ref, field_ref, near_ref,
                     returned_ref, far_ref, out_ref, flat_ref):
    flat_ref[...] = near_ref[...] + returned_ref[...]
    chunks = some_planes(7, [far_ref])
    project(field_reader(field_ref), chunks, corner_ref, flat_ref, flat_ref)
    write_table(flat_ref, member_ref, energy_ref, out_ref)


def whole_pack_kernel(proj_ref, out_ref):
    pack_plane(0, proj_ref.shape[2] // LANES, proj_ref, out_ref)


def high_kernel(proj_ref, out_ref):
    pack_plane(HALVES, HALVES, proj_ref, out_ref)


def whole_sums_kernel(corner_ref, member_ref, energy_ref, field_ref, whole_ref, out_ref, flat_ref):
    project(field_reader(field_ref), all_planes(whole_ref), corner_ref, flat_ref)
    write_table(flat_ref, member_ref, energy_ref, out_ref)


def local_kernel(index, along_z_ref, along_y_ref, field_ref, potential_ref, mate_ref, *refs):
    refs = list(refs)
    before_ref = refs.pop(0) if index > 0 else None
    out_ref, padded_ref = refs
    first, second = step_factors()[index]
    extent = field_ref.shape[0]
    odd = odd_here()
    cells = field_ref[...]
    padded_ref[REACH : REACH + extent] = cells
    mate_at = (1 - odd) * (extent + REACH)
    cross_at = odd * (extent + REACH)
    padded_ref[pl.ds(mate_at, REACH)] = mate_ref[:HALO_ROWS].reshape(REACH, SY, LANES)
    padded_ref[pl.ds(cross_at, REACH)] = jnp.zeros((REACH, SY, LANES), jnp.float32)
    high, low = halves_of(cells.reshape(extent * SY, LANES))
    along_z = jnp.dot(
        jnp.concatenate([high, high, low], axis=1), along_z_ref[...],
        preferred_element_type=jnp.float32,
    )
    along_y = jnp.dot(
        along_y_ref[...], jnp.concatenate([high, low, high], axis=0),
        preferred_element_type=jnp.float32,
    )
    total = (along_z + along_y).reshape(cells.shape)
    for k in range(1, REACH + 1):
        total = total + STENCIL_WEIGHTS[k] * (
            padded_ref[REACH + k : REACH + k + extent] + padded_ref[REACH - k : REACH - k + extent]
        )
    total = -0.5 * total + (potential_ref[...] - CENTRE) * cells
    if index > 0:
        total = total - (second / first) * before_ref[...]
    out_ref[...] = total


def add_cross_halo(cross_ref, part_ref, extent):
    odd = odd_here()
    for near in range(REACH):
        total = None
        for k in range(near + 1, REACH + 1):
            plane = odd * (k - 1 - near) + (1 - odd) * (REACH + near - k)
            cells = cross_ref[pl.ds(pl.multiple_of(plane * SY, SY), SY), :]
            term = (-0.5 * STENCIL_WEIGHTS[k]) * cells
            total = term if total is None else total + term
        at = odd * (extent - 1 - near) + (1 - odd) * near
        part_ref[at] = part_ref[at] + total


def step_kernel(index, chunk_count, member_ref, local_ref, cross_ref, *refs):
    first, _ = step_factors()[index]
    is_first, is_last = index == 0, index + 1 == DEGREE
    refs = list(refs)
    own_ref, far_ref = refs.pop(0), refs.pop(0)
    if is_first:
        table = from_rows(own_ref[...] + refs.pop(0)[...] + far_ref[...])
    else:
        table = from_rows(own_ref[HALO_ROWS:] + cross_ref[HALO_ROWS:] + far_ref[...])
    if chunk_count > 1:
        chunks = some_planes(0, refs[:chunk_count])
    else:
        chunks = all_planes(refs[0])
    refs = refs[chunk_count:]
    energy_ref = None if is_first else refs.pop(0)
    corner_hbm = refs.pop(0)
    next_ref = refs.pop(0)
    if not is_last:
        next_mate_ref, next_cross_ref = refs.pop(0), refs.pop(0)
    if is_first:
        energy_ref = refs.pop(0)
    flat_ref, box_ref, corner_ref, corner_sem, *parts_refs = refs
    corner_copy = pltpu.make_async_copy(corner_hbm, corner_ref, corner_sem)
    corner_copy.start()
    if is_first:
        atoms = table.shape[1] // 2
        energy_ref[...] = table[:, atoms:]
        table = table[:, :atoms]
    scaled = table * energy_ref[...]
    box_values(scaled, chunks, member_ref, flat_ref, box_ref)
    parts_refs[0][...] = local_ref[...]
    for part_ref in parts_refs[1:]:
        part_ref[...] = jnp.zeros(part_ref.shape, jnp.float32)
    add_cross_halo(cross_ref, parts_refs[0], local_ref.shape[0])
    corner_copy.wait()
    deposit(corner_ref, box_ref, parts_refs)
    next_ref[...] = first * total_of([part_ref[...] for part_ref in parts_refs])
    if not is_last:
        project(field_reader(next_ref), chunks, corner_ref, flat_ref)
        sums = sum_atoms(flat_ref, member_ref)
        write_halos(next_ref, odd_here(), next_mate_ref, next_cross_ref)
        next_mate_ref[HALO_ROWS:] = to_rows(sums)
        next_cross_ref[HALO_ROWS:] = to_rows(sums)


VMEM = pl.BlockSpec(memory_space=pltpu.VMEM)
SMEM = pl.BlockSpec(memory_space=pltpu.SMEM)
ANY = pl.BlockSpec(memory_space=pl.ANY)
NO_COST = pl.CostEstimate(flops=0, bytes_accessed=0, transcendentals=0)
LOCAL_COST = pl.CostEstimate(flops=5 * 10**7, bytes_accessed=10**6, transcendentals=0)


def swap(values, axis, first):
    count = lax.axis_size(axis)
    pairs = []
    for i in range(first, count - 1, 2):
        pairs += [(i, i + 1), (i + 1, i)]
    return lax.ppermute(values, axis, pairs)


def turn(values, axis, step):
    count = lax.axis_size(axis)
    return lax.ppermute(values, axis, [(i, (i + step) % count) for i in range(count)])


def on_device(wave_block, potential, projectors, kb_energy, slot_atom, slot_corner):
    bands, planes, cells_y, cells_z = wave_block.shape
    assert bands == 1 and cells_y == SY and cells_z == LANES
    slots, proj_count = projectors.shape[:2]
    atom_own = kb_energy.shape[0]
    atoms = atom_own * lax.axis_size("dom")
    groups = slots // ROWS
    tiles = projectors.shape[2] // LANES
    assert proj_count == ROWS and slots % ROWS == 0
    place = lax.axis_index("dom")
    field = wave_block[0]

    def shaped(*shape):
        return jax.ShapeDtypeStruct(shape, jnp.float32)

    def call(kernel, name, out_shape, scalars, operands, scratch, after=(), in_place={}, late=(),
             cost=NO_COST):
        inputs = len(scalars) + len(operands) + len(late)

        def body(*refs):
            kernel(*refs[:inputs], *refs[inputs + len(after) :])

        return pl.pallas_call(
            body,
            out_shape=out_shape,
            in_specs=[SMEM] * len(scalars) + [VMEM] * len(operands)
            + [ANY] * (len(late) + len(after)),
            out_specs=jax.tree.map(lambda _: VMEM, out_shape),
            scratch_shapes=[
                pltpu.VMEM(shape, jnp.float32) if isinstance(shape, tuple) else shape
                for shape in scratch
            ],
            compiler_params=pltpu.CompilerParams(vmem_limit_bytes=16 * 2**20),
            input_output_aliases=in_place,
            cost_estimate=cost,
            name=name,
        )(*scalars, *operands, *late, *after)

    atom_row = jnp.repeat(slot_atom, SZ)[None, :]
    own_atoms = (jnp.arange(atoms) // atom_own) == place
    energy = jnp.where(own_atoms[None, :], jnp.tile(kb_energy.T, (1, atoms // atom_own)), 0.0)
    flat = (groups, ROWS, LANES)
    boxes = (groups, TILES, ROWS, LANES)
    parts = (planes, SY, LANES)
    padded = (planes + 2 * REACH, SY, LANES)
    table_rows = ROWS * atoms // LANES
    sends = [shaped(HALO_ROWS + table_rows, LANES)] * 2

    flat = (groups, ROWS, LANES)
    boxes = (groups, TILES, ROWS, LANES)
    parts = (planes, SY, LANES)
    padded = (planes + 2 * REACH, SY, LANES)
    table_rows = ROWS * atoms // LANES
    sends = [shaped(HALO_ROWS + table_rows, LANES)] * 2

    def pack(first_tile, count, after=()):
        return call(
            functools.partial(pack_kernel, first_tile), "pack_projectors",
            shaped(count, groups, ROWS, ROWS, LANES), [], [projectors], [], after,
        )

    tables = call(
        table_kernel, "tables",
        [
            jax.ShapeDtypeStruct(shape, jnp.bfloat16)
            for shape in (
                (atoms, slots * SZ), (3 * LANES, LANES), (planes * SY, 3 * planes * SY)
            )
        ],
        [], [atom_row], [],
    )
    halos = [shaped(HALO_ROWS, LANES)] * 2
    if lax.axis_size("band") == 4 and tiles == 2 * HALVES:
        rows = HALVES * groups * ROWS * ROWS
        plane = shaped(rows, LANES)
        laden = shaped(rows + HALO_ROWS, LANES)
        low = call(low_kernel, "pack_low", laden, [], [projectors], [])
        low = call(
            window_kernel, "add_window", laden, [], [field, low], [], (), {1: 0}
        )
        below_low = turn(low, "band", 1)
        high = call(high_kernel, "pack_high", plane, [], [projectors], [], [low])
        below_high = turn(high, "band", 1)
        returned, on_low = call(
            above_kernel, "project_above", [shaped(*flat), plane], [slot_corner],
            [low, high, below_low], [],
        )
        returned = turn(returned, "band", -1)
        far_low = turn(on_low, "band", 1)

        def hand_on(values, *after):
            return call(hand_on_kernel, "hand_on", plane, [], [values], [], after)

        on_high = hand_on(below_high, on_low, returned)
        far_high = turn(on_high, "band", 1)
        on_far_low = hand_on(far_low, on_high, tables[0], energy)
        above_low = turn(on_far_low, "band", 1)
        mate, cross = call(
            halo_kernel, "cut_halos", halos, [], [field], [], [on_far_low]
        )
        mate, cross = swap(mate, "dom", 0), swap(cross, "dom", 1)
        near = call(
            near_kernel, "project_near", shaped(*flat), [slot_corner],
            [field, low, high, below_low, below_high, far_low], [],
        )
        on_far_high = hand_on(far_high, near, tables[0], energy, mate, cross)
        above_high = turn(on_far_high, "band", 1)
        own = call(
            last_part_kernel, "first_sums", shaped(2 * table_rows, LANES), [slot_corner],
            [tables[0], energy, field, near, returned, far_high], [flat],
        )
        chunks = [low, high, above_low, above_high, below_low, below_high, far_low, far_high]
    else:
        mate, cross = call(halo_kernel, "cut_halos", halos, [], [field], [])
        packed = call(
            whole_pack_kernel, "pack_projectors", shaped(tiles * groups * ROWS * ROWS, LANES),
            [], [projectors], [],
        )
        chunks = [lax.all_gather(packed, "band", axis=0, tiled=True)]
        own = call(
            whole_sums_kernel, "first_sums", shaped(2 * table_rows, LANES), [slot_corner],
            [tables[0], energy, field, *chunks], [flat],
        )
        mate, cross = swap(mate, "dom", 0), swap(cross, "dom", 1)
    own = own + swap(own, "dom", 0)
    other = swap(own, "dom", 1)
    far = swap(other, "dom", 0)
    before = None
    for index in range(DEGREE):
        if index > 0:
            to_mate, to_cross = sent
            mate = swap(to_mate, "dom", 0)
            own = to_cross.at[HALO_ROWS:].add(mate[HALO_ROWS:])
            cross = swap(own, "dom", 1)
            far = swap(cross[HALO_ROWS:], "dom", 0)
        local = call(
            functools.partial(local_kernel, index), f"local_{index + 1}",
            shaped(planes, SY, LANES), [],
            [*tables[1:], field, potential, mate] + ([before] if index > 0 else []), [padded],
            cost=LOCAL_COST,
        )
        operands = [tables[0], local, cross, own, far]
        if index == 0:
            operands.append(other)
        operands += chunks
        out_shape = [shaped(planes, SY, LANES)]
        if index > 0:
            operands.append(energy)
        if index + 1 < DEGREE:
            out_shape += sends
        if index == 0:
            out_shape += [shaped(ROWS, atoms)]
        result = call(
            functools.partial(step_kernel, index, len(chunks)), f"filter_step_{index + 1}",
            out_shape, [], operands,
            [
                flat, boxes,
                pltpu.SMEM(slot_corner.shape, jnp.int32), pltpu.SemaphoreType.DMA,
                *[parts] * COPIES,
            ],
            late=[slot_corner],
        )
        before, field = field, result[0]
        sent = result[1:3]
        if index == 0:
            energy = result[3]
    return field[None]


def solution(mesh):
    placed = (
        P("band", "dom", None, None),
        P("dom", None, None),
        P("dom", None, "band"),
        P("dom", None),
        P("dom"),
        P(None, "dom"),
    )
    return jax.shard_map(
        on_device,
        mesh=mesh,
        in_specs=placed,
        out_specs=P("band", "dom", None, None),
        check_vma=False,
    )
```

```python
import functools

import jax
import jax.numpy as jnp
from jax import lax
from jax.experimental import pallas as pl
from jax.experimental.pallas import tpu as pltpu
from jax.sharding import PartitionSpec as P

SX = 8
SY = 16
SZ = 16
DEGREE = 3
LANES = 128
ROWS = 8
TILES = SX * SY * SZ // LANES
HALVES = SY // ROWS

STENCIL_WEIGHTS = (
    -5369.0 / 1800.0,
    12.0 / 7.0,
    -15.0 / 56.0,
    10.0 / 189.0,
    -1.0 / 112.0,
    2.0 / 1925.0,
    -1.0 / 16632.0,
)
REACH = len(STENCIL_WEIGHTS) - 1
LOWER_EDGE = 3.0
UPPER_EDGE = 30.0
ANCHOR_POINT = 0.5
HALF_WIDTH = (UPPER_EDGE - LOWER_EDGE) / 2.0
CENTRE = (UPPER_EDGE + LOWER_EDGE) / 2.0
SIGMA_FIRST = HALF_WIDTH / (ANCHOR_POINT - CENTRE)
PARTS_FROM = (0, 1, 3, 2)


def step_factors():
    sigma_now = SIGMA_FIRST
    factors = [(SIGMA_FIRST / HALF_WIDTH, 0.0)]
    for _ in range(2, DEGREE + 1):
        sigma_next = 1.0 / (2.0 / SIGMA_FIRST - sigma_now)
        factors.append((2.0 * sigma_next / HALF_WIDTH, sigma_now * sigma_next))
        sigma_now = sigma_next
    return factors


def odd_here():
    return lax.rem(lax.axis_index("dom"), 2)


def plane_here(index):
    owner = lax.rem(lax.axis_index("band") + PARTS_FROM[index // 2], 4)
    return owner * 2 + index % 2


def iota(shape, dim):
    return lax.broadcasted_iota(jnp.int32, shape, dim)


def fold_rows(blocks):
    row = iota((ROWS, LANES), 0)
    distance = 1
    while len(blocks) > 1:
        first = (row // distance) % 2 == 0
        blocks = [
            jnp.where(first, a, b) + pltpu.roll(jnp.where(first, b, a), distance, 0)
            for a, b in zip(blocks[::2], blocks[1::2])
        ]
        distance *= 2
    return blocks[0]


def choose(masks, values):
    result = values[-1]
    for mask, value in zip(masks[:-1], values[:-1]):
        result = jnp.where(mask, value, result)
    return result


def pack_plane(first_tile, tiles, proj_ref, out_ref):
    groups = proj_ref.shape[0] // ROWS
    row = iota((ROWS, LANES), 0)
    block = iota((ROWS, LANES), 1) // SZ
    apart = (row - block + ROWS) % ROWS
    block_is = [block == b for b in range(ROWS)]
    row_is = [row == r for r in range(ROWS)]
    apart_is = [apart == d for d in range(ROWS)]

    def one(index, carry):
        tile, group = index // groups, index % groups
        cells = pl.ds(pl.multiple_of((first_tile + tile) * LANES, LANES), LANES)
        given = [proj_ref[group * ROWS + u, :, cells] for u in range(ROWS)]
        by_lane = []
        for d in range(ROWS):
            mixed = choose(block_is, [given[(b - d) % ROWS] for b in range(ROWS)])
            by_lane.append(pltpu.roll(mixed, (LANES - d * SZ) % LANES, 1) if d else mixed)
        by_row = []
        for e in range(ROWS):
            mixed = choose(apart_is, [by_lane[(d + e) % ROWS] for d in range(ROWS)])
            by_row.append(pltpu.roll(mixed, e, 0) if e else mixed)
        for p in range(ROWS):
            at = pl.ds(pl.multiple_of((index * ROWS + p) * ROWS, ROWS), ROWS)
            out_ref[at, :] = choose(row_is, [by_row[(j - p) % ROWS] for j in range(ROWS)])
        return carry

    lax.fori_loop(0, tiles * groups, one, 0)


def halves_of(value):
    high = value.astype(jnp.bfloat16)
    return high, (value - high.astype(jnp.float32)).astype(jnp.bfloat16)


def thirds_of(value):
    rest, parts = value, []
    for _ in range(3):
        high = rest.astype(jnp.bfloat16).astype(jnp.float32)
        parts.append(high)
        rest = rest - high
    return jnp.concatenate(parts, axis=0).astype(jnp.bfloat16)


def sum_thirds(value):
    return value[:ROWS] + value[ROWS : 2 * ROWS] + value[2 * ROWS :]


def table_kernel(atom_row_ref, cell_row_ref, member_ref, along_z_ref, along_y_ref, select_ref):
    cells = iota(select_ref.shape, 0)
    select_ref[...] = (cells == cell_row_ref[...]).astype(jnp.float32).astype(jnp.bfloat16)
    atoms = iota(member_ref.shape, 0)
    member_ref[...] = (atoms == atom_row_ref[...]).astype(jnp.float32).astype(jnp.bfloat16)
    high, low = halves_of(band_matrix(LANES, LANES, 3.0 * STENCIL_WEIGHTS[0]))
    along_z_ref[...] = jnp.concatenate([high, low, high], axis=0)
    high, low = halves_of(band_matrix(along_y_ref.shape[0], SY, 0.0))
    along_y_ref[...] = jnp.concatenate([high, high, low], axis=1)


def total_of(products):
    while len(products) > 1:
        pairs = [a + b for a, b in zip(products[::2], products[1::2])]
        products = pairs + products[len(pairs) * 2 :]
    return products[0]


def values_of(ref, base, groups, half, group, p):
    at = base + ((half * groups + group) * ROWS + p) * ROWS
    return ref[at : at + ROWS, :]


def project(field, chunks, corner_ref, flat_ref, start_ref=None):
    groups = flat_ref.shape[0]
    lane_block = iota((ROWS, LANES), 1) // SZ

    def one(group, carry):
        corners = [corner_ref[0, group * ROWS + u] for u in range(ROWS)]
        shifts = [
            lax.rem(LANES + u * SZ - corner_ref[2, group * ROWS + u], LANES) for u in range(ROWS)
        ]
        sums = [[] for _ in range(ROWS)]
        for plane, ref, base in chunks:
            for half in range(HALVES):
                box = None
                for u in range(ROWS):
                    turned = pltpu.roll(field(corners[u] + plane, half), shifts[u], 1)
                    box = turned if u == 0 else jnp.where(lane_block == u, turned, box)
                for p in range(ROWS):
                    sums[p].append(values_of(ref, base, groups, half, group, p) * box)
        flat = fold_rows([total_of(products) for products in sums])
        flat_ref[group] = flat if start_ref is None else flat + start_ref[group]
        return carry

    for group in range(groups):
        one(group, 0)


def sum_atoms(flat_ref, member_ref):
    flat = jnp.concatenate([flat_ref[g] for g in range(flat_ref.shape[0])], axis=1)
    return sum_thirds(
        lax.dot_general(
            thirds_of(flat), member_ref[...], (((1,), (1,)), ((), ())),
            preferred_element_type=jnp.float32,
        )
    )


def stacked_halves(value):
    return jnp.concatenate(halves_of(value), axis=0)


def sum_halves(value):
    rows = value.shape[0] // 2
    return value[:rows] + value[rows:]


def group_lanes(group):
    return pl.ds(group * LANES, LANES)


def project_slab(field, chunks, corner_ref, select_ref, lanes_ref, flat_ref):
    groups = flat_ref.shape[0]
    lane_block = iota((ROWS, LANES), 1) // SZ
    windows = jnp.dot(
        stacked_halves(field.reshape(-1, LANES)), select_ref[...], preferred_element_type=jnp.float32
    )
    lanes_ref[...] = sum_halves(windows).reshape(lanes_ref.shape)
    for group in range(groups):
        corners = [corner_ref[0, group * ROWS + u] for u in range(ROWS)]
        sums = [[] for _ in range(ROWS)]
        for plane, ref, base in chunks:
            for half in range(HALVES):
                rows = pl.ds(half * ROWS, ROWS)
                box = None
                for u in range(ROWS):
                    cells = lanes_ref[corners[u] + plane, rows, group_lanes(group)]
                    box = cells if u == 0 else jnp.where(lane_block == u, cells, box)
                for p in range(ROWS):
                    sums[p].append(values_of(ref, base, groups, half, group, p) * box)
        flat_ref[group] = fold_rows([total_of(products) for products in sums])


def box_values(scaled, chunks, member_ref, flat_ref, box_ref):
    groups = flat_ref.shape[0]
    margin = (box_ref.shape[1] - SX) // 2
    flat = sum_thirds(
        jnp.dot(thirds_of(scaled), member_ref[...], preferred_element_type=jnp.float32)
    )
    for g in range(groups):
        flat_ref[g] = flat[:, g * LANES : (g + 1) * LANES]
    empty = jnp.zeros((groups, margin) + box_ref.shape[2:], jnp.float32)
    box_ref[:, :margin] = empty
    box_ref[:, margin + SX :] = empty
    for group in range(groups):
        factors = [
            jnp.broadcast_to(flat_ref[group, pl.ds(p, 1), :], (ROWS, LANES)) for p in range(ROWS)
        ]
        for plane, ref, base in chunks:
            for half in range(HALVES):
                box_ref[group, margin + plane, half] = total_of(
                    [
                        values_of(ref, base, groups, half, group, p) * factors[p]
                        for p in range(ROWS)
                    ]
                )


def deposit(corner_ref, box_ref, select_ref, lanes_ref):
    extent = lanes_ref.shape[0]
    groups = box_ref.shape[0]
    margin = (box_ref.shape[1] - SX) // 2
    lane_block = iota((ROWS, LANES), 1) // SZ
    for group in range(groups):
        corners = [corner_ref[0, group * ROWS + u] for u in range(ROWS)]
        for x in range(extent):
            for half in range(HALVES):
                value = None
                for u in range(ROWS):
                    cells = box_ref[group, margin + x - corners[u], half]
                    value = cells if u == 0 else jnp.where(lane_block == u, cells, value)
                lanes_ref[x, pl.ds(half * ROWS, ROWS), group_lanes(group)] = value
    spread = lanes_ref[...].reshape(extent * SY, groups * LANES)
    placed = lax.dot_general(
        stacked_halves(spread), select_ref[...], (((1,), (1,)), ((), ())),
        preferred_element_type=jnp.float32,
    )
    return sum_halves(placed).reshape(extent, SY, LANES)


def band_matrix(size, block, centre):
    row = iota((size, size), 0)
    column = iota((size, size), 1)
    apart = jnp.abs(row - column)
    table = jnp.where(apart == 0, centre, 0.0)
    for k in range(1, REACH + 1):
        table = jnp.where(apart == k, STENCIL_WEIGHTS[k], table)
    return jnp.where(row // block == column // block, table, 0.0)


HALO_ROWS = REACH * SY


def to_rows(table):
    blocks = [table[:, at : at + LANES] for at in range(0, table.shape[1], LANES)]
    return jnp.concatenate(blocks, axis=0)


def from_rows(rows):
    blocks = [rows[at : at + ROWS] for at in range(0, rows.shape[0], ROWS)]
    return jnp.concatenate(blocks, axis=1)


def write_halos(field_ref, odd, mate_ref, cross_ref):
    extent = field_ref.shape[0]
    mate_start = (1 - odd) * (extent - REACH)
    cross_start = odd * (extent - REACH)
    for start, ref in ((mate_start, mate_ref), (cross_start, cross_ref)):
        ref[:HALO_ROWS] = field_ref[pl.ds(start, REACH)].reshape(HALO_ROWS, LANES)


def all_planes(ref):
    rows = ref.shape[0] // SX
    return [(x, ref, x * rows) for x in range(SX)]


def some_planes(first, refs):
    return [(plane_here(first + i), ref, 0) for i, ref in enumerate(refs)]


def field_reader(ref):
    return lambda x, half: ref[x, pl.ds(half * ROWS, ROWS), :]


def halo_kernel(field_ref, mate_ref, cross_ref):
    write_halos(field_ref, odd_here(), mate_ref, cross_ref)


def low_kernel(proj_ref, laden_ref):
    pack_plane(0, HALVES, proj_ref, laden_ref)


def window_kernel(field_ref, laden_ref, out_ref):
    window = field_ref[pl.ds(plane_here(2), REACH)]
    out_ref[out_ref.shape[0] - HALO_ROWS :] = window.reshape(HALO_ROWS, LANES)


def above_kernel(corner_ref, own_laden_ref, high_ref, laden_ref, flat_ref, on_ref):
    rows = on_ref.shape[0]
    on_ref[...] = laden_ref[:rows]

    def field(x, half):
        return laden_ref[pl.ds(pl.multiple_of(rows + x * SY + half * ROWS, ROWS), ROWS), :]

    project(field, [(0, own_laden_ref, 0), (1, high_ref, 0)], corner_ref, flat_ref)


def hand_on_kernel(given_ref, out_ref):
    out_ref[...] = given_ref[...]


def near_kernel(corner_ref, field_ref, low_ref, high_ref, *refs):
    chunks = some_planes(0, [low_ref, high_ref]) + some_planes(4, refs[:-1])
    project(field_reader(field_ref), chunks, corner_ref, refs[-1])


def write_table(flat_ref, member_ref, energy_ref, out_ref):
    sums = sum_atoms(flat_ref, member_ref)
    out_ref[...] = jnp.concatenate([to_rows(sums), to_rows(energy_ref[...])], axis=0)


def last_part_kernel(corner_ref, member_ref, energy_ref, field_ref, near_ref,
                     returned_ref, far_ref, out_ref, flat_ref):
    flat_ref[...] = near_ref[...] + returned_ref[...]
    chunks = some_planes(7, [far_ref])
    project(field_reader(field_ref), chunks, corner_ref, flat_ref, flat_ref)
    write_table(flat_ref, member_ref, energy_ref, out_ref)


def whole_pack_kernel(proj_ref, out_ref):
    pack_plane(0, proj_ref.shape[2] // LANES, proj_ref, out_ref)


def high_kernel(proj_ref, out_ref):
    pack_plane(HALVES, HALVES, proj_ref, out_ref)


def whole_sums_kernel(corner_ref, member_ref, energy_ref, field_ref, whole_ref, out_ref, flat_ref):
    project(field_reader(field_ref), all_planes(whole_ref), corner_ref, flat_ref)
    write_table(flat_ref, member_ref, energy_ref, out_ref)


def local_kernel(index, along_z_ref, along_y_ref, field_ref, potential_ref, mate_ref, *refs):
    refs = list(refs)
    before_ref = refs.pop(0) if index > 0 else None
    out_ref, padded_ref = refs
    first, second = step_factors()[index]
    extent = field_ref.shape[0]
    odd = odd_here()
    cells = field_ref[...]
    padded_ref[REACH : REACH + extent] = cells
    mate_at = (1 - odd) * (extent + REACH)
    cross_at = odd * (extent + REACH)
    padded_ref[pl.ds(mate_at, REACH)] = mate_ref[:HALO_ROWS].reshape(REACH, SY, LANES)
    padded_ref[pl.ds(cross_at, REACH)] = jnp.zeros((REACH, SY, LANES), jnp.float32)
    high, low = halves_of(cells.reshape(extent * SY, LANES))
    along_z = jnp.dot(
        jnp.concatenate([high, high, low], axis=1), along_z_ref[...],
        preferred_element_type=jnp.float32,
    )
    along_y = jnp.dot(
        along_y_ref[...], jnp.concatenate([high, low, high], axis=0),
        preferred_element_type=jnp.float32,
    )
    total = (along_z + along_y).reshape(cells.shape)
    for k in range(1, REACH + 1):
        total = total + STENCIL_WEIGHTS[k] * (
            padded_ref[REACH + k : REACH + k + extent] + padded_ref[REACH - k : REACH - k + extent]
        )
    total = -0.5 * total + (potential_ref[...] - CENTRE) * cells
    if index > 0:
        total = total - (second / first) * before_ref[...]
    out_ref[...] = total


def add_cross_halo(cross_ref, part_ref, extent):
    odd = odd_here()
    for near in range(REACH):
        total = None
        for k in range(near + 1, REACH + 1):
            plane = odd * (k - 1 - near) + (1 - odd) * (REACH + near - k)
            cells = cross_ref[pl.ds(pl.multiple_of(plane * SY, SY), SY), :]
            term = (-0.5 * STENCIL_WEIGHTS[k]) * cells
            total = term if total is None else total + term
        at = odd * (extent - 1 - near) + (1 - odd) * near
        part_ref[at] = part_ref[at] + total


def step_kernel(index, chunk_count, member_ref, select_ref, local_ref, cross_ref, *refs):
    first, _ = step_factors()[index]
    is_first, is_last = index == 0, index + 1 == DEGREE
    refs = list(refs)
    own_ref, far_ref = refs.pop(0), refs.pop(0)
    if is_first:
        table = from_rows(own_ref[...] + refs.pop(0)[...] + far_ref[...])
    else:
        table = from_rows(own_ref[HALO_ROWS:] + cross_ref[HALO_ROWS:] + far_ref[...])
    if chunk_count > 1:
        chunks = some_planes(0, refs[:chunk_count])
    else:
        chunks = all_planes(refs[0])
    refs = refs[chunk_count:]
    energy_ref = None if is_first else refs.pop(0)
    corner_hbm = refs.pop(0)
    next_ref = refs.pop(0)
    if not is_last:
        next_mate_ref, next_cross_ref = refs.pop(0), refs.pop(0)
    if is_first:
        energy_ref = refs.pop(0)
    flat_ref, box_ref, lanes_ref, corner_ref, corner_sem = refs
    corner_copy = pltpu.make_async_copy(corner_hbm, corner_ref, corner_sem)
    corner_copy.start()
    if is_first:
        atoms = table.shape[1] // 2
        energy_ref[...] = table[:, atoms:]
        table = table[:, :atoms]
    scaled = table * energy_ref[...]
    box_values(scaled, chunks, member_ref, flat_ref, box_ref)
    next_ref[...] = local_ref[...]
    add_cross_halo(cross_ref, next_ref, local_ref.shape[0])
    corner_copy.wait()
    value = first * (next_ref[...] + deposit(corner_ref, box_ref, select_ref, lanes_ref))
    next_ref[...] = value
    if not is_last:
        project_slab(value, chunks, corner_ref, select_ref, lanes_ref, flat_ref)
        sums = sum_atoms(flat_ref, member_ref)
        write_halos(next_ref, odd_here(), next_mate_ref, next_cross_ref)
        next_mate_ref[HALO_ROWS:] = to_rows(sums)
        next_cross_ref[HALO_ROWS:] = to_rows(sums)


VMEM = pl.BlockSpec(memory_space=pltpu.VMEM)
SMEM = pl.BlockSpec(memory_space=pltpu.SMEM)
ANY = pl.BlockSpec(memory_space=pl.ANY)
NO_COST = pl.CostEstimate(flops=0, bytes_accessed=0, transcendentals=0)
LOCAL_COST = pl.CostEstimate(flops=5 * 10**7, bytes_accessed=10**6, transcendentals=0)


def swap(values, axis, first):
    count = lax.axis_size(axis)
    pairs = []
    for i in range(first, count - 1, 2):
        pairs += [(i, i + 1), (i + 1, i)]
    return lax.ppermute(values, axis, pairs)


def turn(values, axis, step):
    count = lax.axis_size(axis)
    return lax.ppermute(values, axis, [(i, (i + step) % count) for i in range(count)])


def on_device(wave_block, potential, projectors, kb_energy, slot_atom, slot_corner):
    bands, planes, cells_y, cells_z = wave_block.shape
    assert bands == 1 and cells_y == SY and cells_z == LANES
    slots, proj_count = projectors.shape[:2]
    atom_own = kb_energy.shape[0]
    atoms = atom_own * lax.axis_size("dom")
    groups = slots // ROWS
    tiles = projectors.shape[2] // LANES
    assert proj_count == ROWS and slots % ROWS == 0
    place = lax.axis_index("dom")
    field = wave_block[0]

    def shaped(*shape):
        return jax.ShapeDtypeStruct(shape, jnp.float32)

    def call(kernel, name, out_shape, scalars, operands, scratch, after=(), in_place={}, late=(),
             cost=NO_COST):
        inputs = len(scalars) + len(operands) + len(late)

        def body(*refs):
            kernel(*refs[:inputs], *refs[inputs + len(after) :])

        return pl.pallas_call(
            body,
            out_shape=out_shape,
            in_specs=[SMEM] * len(scalars) + [VMEM] * len(operands)
            + [ANY] * (len(late) + len(after)),
            out_specs=jax.tree.map(lambda _: VMEM, out_shape),
            scratch_shapes=[
                pltpu.VMEM(shape, jnp.float32) if isinstance(shape, tuple) else shape
                for shape in scratch
            ],
            compiler_params=pltpu.CompilerParams(vmem_limit_bytes=16 * 2**20),
            input_output_aliases=in_place,
            cost_estimate=cost,
            name=name,
        )(*scalars, *operands, *late, *after)

    atom_row = jnp.repeat(slot_atom, SZ)[None, :]
    cell_row = (slot_corner[2][:, None] + jnp.arange(SZ, dtype=jnp.int32)[None, :]).reshape(1, -1)
    own_atoms = (jnp.arange(atoms) // atom_own) == place
    energy = jnp.where(own_atoms[None, :], jnp.tile(kb_energy.T, (1, atoms // atom_own)), 0.0)
    flat = (groups, ROWS, LANES)
    boxes = (groups, 2 * planes - SX, HALVES, ROWS, LANES)
    padded = (planes + 2 * REACH, SY, LANES)
    table_rows = ROWS * atoms // LANES
    sends = [shaped(HALO_ROWS + table_rows, LANES)] * 2

    flat = (groups, ROWS, LANES)
    boxes = (groups, 2 * planes - SX, HALVES, ROWS, LANES)
    padded = (planes + 2 * REACH, SY, LANES)
    table_rows = ROWS * atoms // LANES
    sends = [shaped(HALO_ROWS + table_rows, LANES)] * 2

    def pack(first_tile, count, after=()):
        return call(
            functools.partial(pack_kernel, first_tile), "pack_projectors",
            shaped(count, groups, ROWS, ROWS, LANES), [], [projectors], [], after,
        )

    tables = call(
        table_kernel, "tables",
        [
            jax.ShapeDtypeStruct(shape, jnp.bfloat16)
            for shape in (
                (atoms, slots * SZ), (3 * LANES, LANES), (planes * SY, 3 * planes * SY),
                (LANES, slots * SZ),
            )
        ],
        [], [atom_row, cell_row], [],
    )
    halos = [shaped(HALO_ROWS, LANES)] * 2
    if lax.axis_size("band") == 4 and tiles == 2 * HALVES:
        rows = HALVES * groups * ROWS * ROWS
        plane = shaped(rows, LANES)
        laden = shaped(rows + HALO_ROWS, LANES)
        low = call(low_kernel, "pack_low", laden, [], [projectors], [])
        low = call(
            window_kernel, "add_window", laden, [], [field, low], [], (), {1: 0}
        )
        below_low = turn(low, "band", 1)
        high = call(high_kernel, "pack_high", plane, [], [projectors], [], [low])
        below_high = turn(high, "band", 1)
        returned, on_low = call(
            above_kernel, "project_above", [shaped(*flat), plane], [slot_corner],
            [low, high, below_low], [],
        )
        returned = turn(returned, "band", -1)
        far_low = turn(on_low, "band", 1)

        def hand_on(values, *after):
            return call(hand_on_kernel, "hand_on", plane, [], [values], [], after)

        on_high = hand_on(below_high, on_low, returned)
        far_high = turn(on_high, "band", 1)
        on_far_low = hand_on(far_low, on_high, tables[0], energy)
        above_low = turn(on_far_low, "band", 1)
        mate, cross = call(
            halo_kernel, "cut_halos", halos, [], [field], [], [on_far_low]
        )
        mate, cross = swap(mate, "dom", 0), swap(cross, "dom", 1)
        near = call(
            near_kernel, "project_near", shaped(*flat), [slot_corner],
            [field, low, high, below_low, below_high, far_low], [],
        )
        on_far_high = hand_on(far_high, near, tables[0], energy, mate, cross)
        above_high = turn(on_far_high, "band", 1)
        own = call(
            last_part_kernel, "first_sums", shaped(2 * table_rows, LANES), [slot_corner],
            [tables[0], energy, field, near, returned, far_high], [flat],
        )
        chunks = [low, high, above_low, above_high, below_low, below_high, far_low, far_high]
    else:
        mate, cross = call(halo_kernel, "cut_halos", halos, [], [field], [])
        packed = call(
            whole_pack_kernel, "pack_projectors", shaped(tiles * groups * ROWS * ROWS, LANES),
            [], [projectors], [],
        )
        chunks = [lax.all_gather(packed, "band", axis=0, tiled=True)]
        own = call(
            whole_sums_kernel, "first_sums", shaped(2 * table_rows, LANES), [slot_corner],
            [tables[0], energy, field, *chunks], [flat],
        )
        mate, cross = swap(mate, "dom", 0), swap(cross, "dom", 1)
    own = own + swap(own, "dom", 0)
    other = swap(own, "dom", 1)
    far = swap(other, "dom", 0)
    before = None
    for index in range(DEGREE):
        if index > 0:
            to_mate, to_cross = sent
            mate = swap(to_mate, "dom", 0)
            own = to_cross.at[HALO_ROWS:].add(mate[HALO_ROWS:])
            cross = swap(own, "dom", 1)
            far = swap(cross[HALO_ROWS:], "dom", 0)
        local = call(
            functools.partial(local_kernel, index), f"local_{index + 1}",
            shaped(planes, SY, LANES), [],
            [*tables[1:3], field, potential, mate] + ([before] if index > 0 else []), [padded],
            cost=LOCAL_COST,
        )
        operands = [tables[0], tables[3], local, cross, own, far]
        if index == 0:
            operands.append(other)
        operands += chunks
        out_shape = [shaped(planes, SY, LANES)]
        if index > 0:
            operands.append(energy)
        if index + 1 < DEGREE:
            out_shape += sends
        if index == 0:
            out_shape += [shaped(ROWS, atoms)]
        result = call(
            functools.partial(step_kernel, index, len(chunks)), f"filter_step_{index + 1}",
            out_shape, [], operands,
            [
                flat, boxes, (planes, SY, slots * SZ),
                pltpu.SMEM(slot_corner.shape, jnp.int32), pltpu.SemaphoreType.DMA,
            ],
            late=[slot_corner],
        )
        before, field = field, result[0]
        sent = result[1:3]
        if index == 0:
            energy = result[3]
    return field[None]


def solution(mesh):
    placed = (
        P("band", "dom", None, None),
        P("dom", None, None),
        P("dom", None, "band"),
        P("dom", None),
        P("dom"),
        P(None, "dom"),
    )
    return jax.shard_map(
        on_device,
        mesh=mesh,
        in_specs=placed,
        out_specs=P("band", "dom", None, None),
        check_vma=False,
    )
```

```python
import functools

import jax
import jax.numpy as jnp
from jax import lax
from jax.experimental import pallas as pl
from jax.experimental.pallas import tpu as pltpu
from jax.sharding import PartitionSpec as P

SX = 8
SY = 16
SZ = 16
DEGREE = 3
LANES = 128
ROWS = 8
TILES = SX * SY * SZ // LANES
HALVES = SY // ROWS

STENCIL_WEIGHTS = (
    -5369.0 / 1800.0,
    12.0 / 7.0,
    -15.0 / 56.0,
    10.0 / 189.0,
    -1.0 / 112.0,
    2.0 / 1925.0,
    -1.0 / 16632.0,
)
REACH = len(STENCIL_WEIGHTS) - 1
LOWER_EDGE = 3.0
UPPER_EDGE = 30.0
ANCHOR_POINT = 0.5
HALF_WIDTH = (UPPER_EDGE - LOWER_EDGE) / 2.0
CENTRE = (UPPER_EDGE + LOWER_EDGE) / 2.0
SIGMA_FIRST = HALF_WIDTH / (ANCHOR_POINT - CENTRE)
PARTS_FROM = (0, 1, 3, 2)


def step_factors():
    sigma_now = SIGMA_FIRST
    factors = [(SIGMA_FIRST / HALF_WIDTH, 0.0)]
    for _ in range(2, DEGREE + 1):
        sigma_next = 1.0 / (2.0 / SIGMA_FIRST - sigma_now)
        factors.append((2.0 * sigma_next / HALF_WIDTH, sigma_now * sigma_next))
        sigma_now = sigma_next
    return factors


def odd_here():
    return lax.rem(lax.axis_index("dom"), 2)


def plane_here(index):
    owner = lax.rem(lax.axis_index("band") + PARTS_FROM[index // 2], 4)
    return owner * 2 + index % 2


def iota(shape, dim):
    return lax.broadcasted_iota(jnp.int32, shape, dim)


def fold_rows(blocks):
    row = iota((ROWS, LANES), 0)
    distance = 1
    while len(blocks) > 1:
        first = (row // distance) % 2 == 0
        blocks = [
            jnp.where(first, a, b) + pltpu.roll(jnp.where(first, b, a), distance, 0)
            for a, b in zip(blocks[::2], blocks[1::2])
        ]
        distance *= 2
    return blocks[0]


def choose(masks, values):
    result = values[-1]
    for mask, value in zip(masks[:-1], values[:-1]):
        result = jnp.where(mask, value, result)
    return result


def pack_plane(first_tile, tiles, proj_ref, out_ref):
    groups = proj_ref.shape[0] // ROWS
    row = iota((ROWS, LANES), 0)
    block = iota((ROWS, LANES), 1) // SZ
    apart = (row - block + ROWS) % ROWS
    block_is = [block == b for b in range(ROWS)]
    row_is = [row == r for r in range(ROWS)]
    apart_is = [apart == d for d in range(ROWS)]

    def one(index, carry):
        tile, group = index // groups, index % groups
        cells = pl.ds(pl.multiple_of((first_tile + tile) * LANES, LANES), LANES)
        given = [proj_ref[group * ROWS + u, :, cells] for u in range(ROWS)]
        by_lane = []
        for d in range(ROWS):
            mixed = choose(block_is, [given[(b - d) % ROWS] for b in range(ROWS)])
            by_lane.append(pltpu.roll(mixed, (LANES - d * SZ) % LANES, 1) if d else mixed)
        by_row = []
        for e in range(ROWS):
            mixed = choose(apart_is, [by_lane[(d + e) % ROWS] for d in range(ROWS)])
            by_row.append(pltpu.roll(mixed, e, 0) if e else mixed)
        for p in range(ROWS):
            at = pl.ds(pl.multiple_of((index * ROWS + p) * ROWS, ROWS), ROWS)
            out_ref[at, :] = choose(row_is, [by_row[(j - p) % ROWS] for j in range(ROWS)])
        return carry

    lax.fori_loop(0, tiles * groups, one, 0)


def halves_of(value):
    high = value.astype(jnp.bfloat16)
    return high, (value - high.astype(jnp.float32)).astype(jnp.bfloat16)


def thirds_of(value):
    rest, parts = value, []
    for _ in range(3):
        high = rest.astype(jnp.bfloat16).astype(jnp.float32)
        parts.append(high)
        rest = rest - high
    return jnp.concatenate(parts, axis=0).astype(jnp.bfloat16)


def sum_thirds(value):
    return value[:ROWS] + value[ROWS : 2 * ROWS] + value[2 * ROWS :]


def table_kernel(atom_row_ref, cell_row_ref, member_ref, along_z_ref, along_y_ref, select_ref):
    cells = iota(select_ref.shape, 0)
    select_ref[...] = (cells == cell_row_ref[...]).astype(jnp.float32).astype(jnp.bfloat16)
    atoms = iota(member_ref.shape, 0)
    member_ref[...] = (atoms == atom_row_ref[...]).astype(jnp.float32).astype(jnp.bfloat16)
    high, low = halves_of(band_matrix(LANES, LANES, 3.0 * STENCIL_WEIGHTS[0]))
    along_z_ref[...] = jnp.concatenate([high, low, high], axis=0)
    high, low = halves_of(band_matrix(along_y_ref.shape[0], SY, 0.0))
    along_y_ref[...] = jnp.concatenate([high, high, low], axis=1)


def total_of(products):
    while len(products) > 1:
        pairs = [a + b for a, b in zip(products[::2], products[1::2])]
        products = pairs + products[len(pairs) * 2 :]
    return products[0]


def values_of(ref, base, groups, half, group, p):
    at = base + ((half * groups + group) * ROWS + p) * ROWS
    return ref[at : at + ROWS, :]


def project(field, chunks, corner_ref, flat_ref, start_ref=None):
    groups = flat_ref.shape[0]
    lane_block = iota((ROWS, LANES), 1) // SZ

    def one(group, carry):
        corners = [corner_ref[0, group * ROWS + u] for u in range(ROWS)]
        shifts = [
            lax.rem(LANES + u * SZ - corner_ref[2, group * ROWS + u], LANES) for u in range(ROWS)
        ]
        sums = [[] for _ in range(ROWS)]
        for plane, ref, base in chunks:
            for half in range(HALVES):
                box = None
                for u in range(ROWS):
                    turned = pltpu.roll(field(corners[u] + plane, half), shifts[u], 1)
                    box = turned if u == 0 else jnp.where(lane_block == u, turned, box)
                for p in range(ROWS):
                    sums[p].append(values_of(ref, base, groups, half, group, p) * box)
        flat = fold_rows([total_of(products) for products in sums])
        flat_ref[group] = flat if start_ref is None else flat + start_ref[group]
        return carry

    for group in range(groups):
        one(group, 0)


def sum_atoms(flat_ref, member_ref):
    flat = jnp.concatenate([flat_ref[g] for g in range(flat_ref.shape[0])], axis=1)
    return sum_thirds(
        lax.dot_general(
            thirds_of(flat), member_ref[...], (((1,), (1,)), ((), ())),
            preferred_element_type=jnp.float32,
        )
    )


def stacked_halves(value):
    return jnp.concatenate(halves_of(value), axis=0)


def sum_halves(value):
    rows = value.shape[0] // 2
    return value[:rows] + value[rows:]


def group_lanes(group):
    return pl.ds(group * LANES, LANES)


def project_slab(field, chunks, corner_ref, select_ref, lanes_ref, flat_ref):
    groups = flat_ref.shape[0]
    lane_block = iota((ROWS, LANES), 1) // SZ
    windows = jnp.dot(
        stacked_halves(field.reshape(-1, LANES)), select_ref[...], preferred_element_type=jnp.float32
    )
    lanes_ref[...] = sum_halves(windows).reshape(lanes_ref.shape)
    for group in range(groups):
        corners = [corner_ref[0, group * ROWS + u] for u in range(ROWS)]
        sums = [[] for _ in range(ROWS)]
        for plane, ref, base in chunks:
            for half in range(HALVES):
                rows = pl.ds(half * ROWS, ROWS)
                box = None
                for u in range(ROWS):
                    cells = lanes_ref[corners[u] + plane, rows, group_lanes(group)]
                    box = cells if u == 0 else jnp.where(lane_block == u, cells, box)
                for p in range(ROWS):
                    sums[p].append(values_of(ref, base, groups, half, group, p) * box)
        flat_ref[group] = fold_rows([total_of(products) for products in sums])


def box_values(scaled, chunks, member_ref, flat_ref, box_ref):
    groups = flat_ref.shape[0]
    margin = (box_ref.shape[1] - SX) // 2
    flat = sum_thirds(
        jnp.dot(thirds_of(scaled), member_ref[...], preferred_element_type=jnp.float32)
    )
    for g in range(groups):
        flat_ref[g] = flat[:, g * LANES : (g + 1) * LANES]
    empty = jnp.zeros((groups, margin) + box_ref.shape[2:], jnp.float32)
    box_ref[:, :margin] = empty
    box_ref[:, margin + SX :] = empty
    for group in range(groups):
        factors = [
            jnp.broadcast_to(flat_ref[group, pl.ds(p, 1), :], (ROWS, LANES)) for p in range(ROWS)
        ]
        for plane, ref, base in chunks:
            for half in range(HALVES):
                box_ref[group, margin + plane, half] = total_of(
                    [
                        values_of(ref, base, groups, half, group, p) * factors[p]
                        for p in range(ROWS)
                    ]
                )


def deposit(corner_ref, box_ref, select_ref, lanes_ref):
    extent = lanes_ref.shape[0]
    groups = box_ref.shape[0]
    margin = (box_ref.shape[1] - SX) // 2
    lane_block = iota((ROWS, LANES), 1) // SZ
    for group in range(groups):
        corners = [corner_ref[0, group * ROWS + u] for u in range(ROWS)]
        for x in range(extent):
            for half in range(HALVES):
                value = None
                for u in range(ROWS):
                    cells = box_ref[group, margin + x - corners[u], half]
                    value = cells if u == 0 else jnp.where(lane_block == u, cells, value)
                lanes_ref[x, pl.ds(half * ROWS, ROWS), group_lanes(group)] = value
    spread = lanes_ref[...].reshape(extent * SY, groups * LANES)
    placed = lax.dot_general(
        stacked_halves(spread), select_ref[...], (((1,), (1,)), ((), ())),
        preferred_element_type=jnp.float32,
    )
    return sum_halves(placed).reshape(extent, SY, LANES)


def band_matrix(size, block, centre):
    row = iota((size, size), 0)
    column = iota((size, size), 1)
    apart = jnp.abs(row - column)
    table = jnp.where(apart == 0, centre, 0.0)
    for k in range(1, REACH + 1):
        table = jnp.where(apart == k, STENCIL_WEIGHTS[k], table)
    return jnp.where(row // block == column // block, table, 0.0)


HALO_ROWS = REACH * SY


def to_rows(table):
    blocks = [table[:, at : at + LANES] for at in range(0, table.shape[1], LANES)]
    return jnp.concatenate(blocks, axis=0)


def from_rows(rows):
    blocks = [rows[at : at + ROWS] for at in range(0, rows.shape[0], ROWS)]
    return jnp.concatenate(blocks, axis=1)


def write_halos(field_ref, odd, mate_ref, cross_ref):
    extent = field_ref.shape[0]
    mate_start = (1 - odd) * (extent - REACH)
    cross_start = odd * (extent - REACH)
    for start, ref in ((mate_start, mate_ref), (cross_start, cross_ref)):
        ref[:HALO_ROWS] = field_ref[pl.ds(start, REACH)].reshape(HALO_ROWS, LANES)


def all_planes(ref):
    rows = ref.shape[0] // SX
    return [(x, ref, x * rows) for x in range(SX)]


def some_planes(first, refs):
    return [(plane_here(first + i), ref, 0) for i, ref in enumerate(refs)]


def field_reader(ref):
    return lambda x, half: ref[x, pl.ds(half * ROWS, ROWS), :]


def halo_kernel(field_ref, mate_ref, cross_ref):
    write_halos(field_ref, odd_here(), mate_ref, cross_ref)


def low_kernel(proj_ref, laden_ref):
    pack_plane(0, HALVES, proj_ref, laden_ref)


def window_kernel(field_ref, laden_ref, out_ref):
    window = field_ref[pl.ds(plane_here(2), REACH)]
    out_ref[out_ref.shape[0] - HALO_ROWS :] = window.reshape(HALO_ROWS, LANES)


def above_kernel(corner_ref, own_laden_ref, high_ref, laden_ref, flat_ref, on_ref):
    rows = on_ref.shape[0]
    on_ref[...] = laden_ref[:rows]

    def field(x, half):
        return laden_ref[pl.ds(pl.multiple_of(rows + x * SY + half * ROWS, ROWS), ROWS), :]

    project(field, [(0, own_laden_ref, 0), (1, high_ref, 0)], corner_ref, flat_ref)


def hand_on_kernel(given_ref, out_ref):
    out_ref[...] = given_ref[...]


def near_kernel(corner_ref, field_ref, low_ref, high_ref, *refs):
    chunks = some_planes(0, [low_ref, high_ref]) + some_planes(4, refs[:-1])
    project(field_reader(field_ref), chunks, corner_ref, refs[-1])


def write_table(flat_ref, member_ref, energy_ref, out_ref):
    sums = sum_atoms(flat_ref, member_ref)
    out_ref[...] = jnp.concatenate([to_rows(sums), to_rows(energy_ref[...])], axis=0)


def last_part_kernel(corner_ref, member_ref, energy_ref, field_ref, near_ref,
                     returned_ref, far_ref, out_ref, flat_ref):
    flat_ref[...] = near_ref[...] + returned_ref[...]
    chunks = some_planes(7, [far_ref])
    project(field_reader(field_ref), chunks, corner_ref, flat_ref, flat_ref)
    write_table(flat_ref, member_ref, energy_ref, out_ref)


def whole_pack_kernel(proj_ref, out_ref):
    pack_plane(0, proj_ref.shape[2] // LANES, proj_ref, out_ref)


def high_kernel(proj_ref, out_ref):
    pack_plane(HALVES, HALVES, proj_ref, out_ref)


def whole_sums_kernel(corner_ref, member_ref, energy_ref, field_ref, whole_ref, out_ref, flat_ref):
    project(field_reader(field_ref), all_planes(whole_ref), corner_ref, flat_ref)
    write_table(flat_ref, member_ref, energy_ref, out_ref)


def local_kernel(index, along_z_ref, along_y_ref, field_ref, potential_ref, mate_ref, *refs):
    refs = list(refs)
    before_ref = refs.pop(0) if index > 0 else None
    out_ref, padded_ref = refs
    first, second = step_factors()[index]
    extent = field_ref.shape[0]
    odd = odd_here()
    cells = field_ref[...]
    padded_ref[REACH : REACH + extent] = cells
    mate_at = (1 - odd) * (extent + REACH)
    cross_at = odd * (extent + REACH)
    padded_ref[pl.ds(mate_at, REACH)] = mate_ref[:HALO_ROWS].reshape(REACH, SY, LANES)
    padded_ref[pl.ds(cross_at, REACH)] = jnp.zeros((REACH, SY, LANES), jnp.float32)
    high, low = halves_of(cells.reshape(extent * SY, LANES))
    along_z = jnp.dot(
        jnp.concatenate([high, high, low], axis=1), along_z_ref[...],
        preferred_element_type=jnp.float32,
    )
    along_y = jnp.dot(
        along_y_ref[...], jnp.concatenate([high, low, high], axis=0),
        preferred_element_type=jnp.float32,
    )
    total = (along_z + along_y).reshape(cells.shape)
    for k in range(1, REACH + 1):
        total = total + STENCIL_WEIGHTS[k] * (
            padded_ref[REACH + k : REACH + k + extent] + padded_ref[REACH - k : REACH - k + extent]
        )
    total = -0.5 * total + (potential_ref[...] - CENTRE) * cells
    if index > 0:
        total = total - (second / first) * before_ref[...]
    out_ref[...] = total


def add_cross_halo(cross_ref, part_ref, extent):
    odd = odd_here()
    for near in range(REACH):
        total = None
        for k in range(near + 1, REACH + 1):
            plane = odd * (k - 1 - near) + (1 - odd) * (REACH + near - k)
            cells = cross_ref[pl.ds(pl.multiple_of(plane * SY, SY), SY), :]
            term = (-0.5 * STENCIL_WEIGHTS[k]) * cells
            total = term if total is None else total + term
        at = odd * (extent - 1 - near) + (1 - odd) * near
        part_ref[at] = part_ref[at] + total


def step_kernel(index, chunk_count, member_ref, select_ref, local_ref, cross_ref, *refs):
    first, _ = step_factors()[index]
    is_first, is_last = index == 0, index + 1 == DEGREE
    refs = list(refs)
    own_ref, far_ref = refs.pop(0), refs.pop(0)
    if is_first:
        table = from_rows(own_ref[...] + refs.pop(0)[...] + far_ref[...])
    else:
        table = from_rows(own_ref[HALO_ROWS:] + cross_ref[HALO_ROWS:] + far_ref[...])
    if chunk_count > 1:
        chunks = some_planes(0, refs[:chunk_count])
    else:
        chunks = all_planes(refs[0])
    refs = refs[chunk_count:]
    energy_ref = None if is_first else refs.pop(0)
    corner_hbm = refs.pop(0)
    next_ref = refs.pop(0)
    if not is_last:
        next_mate_ref, next_cross_ref = refs.pop(0), refs.pop(0)
    if is_first:
        energy_ref = refs.pop(0)
    flat_ref, box_ref, lanes_ref, corner_ref, corner_sem = refs
    corner_copy = pltpu.make_async_copy(corner_hbm, corner_ref, corner_sem)
    corner_copy.start()
    if is_first:
        atoms = table.shape[1] // 2
        energy_ref[...] = table[:, atoms:]
        table = table[:, :atoms]
    scaled = table * energy_ref[...]
    box_values(scaled, chunks, member_ref, flat_ref, box_ref)
    next_ref[...] = local_ref[...]
    add_cross_halo(cross_ref, next_ref, local_ref.shape[0])
    corner_copy.wait()
    value = first * (next_ref[...] + deposit(corner_ref, box_ref, select_ref, lanes_ref))
    next_ref[...] = value
    if not is_last:
        project_slab(value, chunks, corner_ref, select_ref, lanes_ref, flat_ref)
        sums = sum_atoms(flat_ref, member_ref)
        write_halos(next_ref, odd_here(), next_mate_ref, next_cross_ref)
        next_mate_ref[HALO_ROWS:] = to_rows(sums)
        next_cross_ref[HALO_ROWS:] = to_rows(sums)


VMEM = pl.BlockSpec(memory_space=pltpu.VMEM)
SMEM = pl.BlockSpec(memory_space=pltpu.SMEM)
ANY = pl.BlockSpec(memory_space=pl.ANY)
NO_COST = pl.CostEstimate(flops=0, bytes_accessed=0, transcendentals=0)
LOCAL_COST = pl.CostEstimate(flops=5 * 10**7, bytes_accessed=10**6, transcendentals=0)


def swap(values, axis, first):
    count = lax.axis_size(axis)
    pairs = []
    for i in range(first, count - 1, 2):
        pairs += [(i, i + 1), (i + 1, i)]
    return lax.ppermute(values, axis, pairs)


def turn(values, axis, step):
    count = lax.axis_size(axis)
    return lax.ppermute(values, axis, [(i, (i + step) % count) for i in range(count)])


def on_device(wave_block, potential, projectors, kb_energy, slot_atom, slot_corner):
    bands, planes, cells_y, cells_z = wave_block.shape
    assert bands == 1 and cells_y == SY and cells_z == LANES
    slots, proj_count = projectors.shape[:2]
    atom_own = kb_energy.shape[0]
    atoms = atom_own * lax.axis_size("dom")
    groups = slots // ROWS
    tiles = projectors.shape[2] // LANES
    assert proj_count == ROWS and slots % ROWS == 0
    place = lax.axis_index("dom")
    field = wave_block[0]

    def shaped(*shape):
        return jax.ShapeDtypeStruct(shape, jnp.float32)

    def call(kernel, name, out_shape, scalars, operands, scratch, after=(), in_place={}, late=(),
             cost=NO_COST):
        inputs = len(scalars) + len(operands) + len(late)

        def body(*refs):
            kernel(*refs[:inputs], *refs[inputs + len(after) :])

        return pl.pallas_call(
            body,
            out_shape=out_shape,
            in_specs=[SMEM] * len(scalars) + [VMEM] * len(operands)
            + [ANY] * (len(late) + len(after)),
            out_specs=jax.tree.map(lambda _: VMEM, out_shape),
            scratch_shapes=[
                pltpu.VMEM(shape, jnp.float32) if isinstance(shape, tuple) else shape
                for shape in scratch
            ],
            compiler_params=pltpu.CompilerParams(vmem_limit_bytes=16 * 2**20),
            input_output_aliases=in_place,
            cost_estimate=cost,
            name=name,
        )(*scalars, *operands, *late, *after)

    atom_row = jnp.repeat(slot_atom, SZ)[None, :]
    cell_row = (slot_corner[2][:, None] + jnp.arange(SZ, dtype=jnp.int32)[None, :]).reshape(1, -1)
    own_atoms = (jnp.arange(atoms) // atom_own) == place
    energy = jnp.where(own_atoms[None, :], jnp.tile(kb_energy.T, (1, atoms // atom_own)), 0.0)
    flat = (groups, ROWS, LANES)
    boxes = (groups, 2 * planes - SX, HALVES, ROWS, LANES)
    padded = (planes + 2 * REACH, SY, LANES)
    table_rows = ROWS * atoms // LANES
    sends = [shaped(HALO_ROWS + table_rows, LANES)] * 2

    flat = (groups, ROWS, LANES)
    boxes = (groups, 2 * planes - SX, HALVES, ROWS, LANES)
    padded = (planes + 2 * REACH, SY, LANES)
    table_rows = ROWS * atoms // LANES
    sends = [shaped(HALO_ROWS + table_rows, LANES)] * 2

    def pack(first_tile, count, after=()):
        return call(
            functools.partial(pack_kernel, first_tile), "pack_projectors",
            shaped(count, groups, ROWS, ROWS, LANES), [], [projectors], [], after,
        )

    tables = call(
        table_kernel, "tables",
        [
            jax.ShapeDtypeStruct(shape, jnp.bfloat16)
            for shape in (
                (atoms, slots * SZ), (3 * LANES, LANES), (planes * SY, 3 * planes * SY),
                (LANES, slots * SZ),
            )
        ],
        [], [atom_row, cell_row], [],
    )
    halos = [shaped(HALO_ROWS, LANES)] * 2
    if lax.axis_size("band") == 4 and tiles == 2 * HALVES:
        rows = HALVES * groups * ROWS * ROWS
        plane = shaped(rows, LANES)
        laden = shaped(rows + HALO_ROWS, LANES)
        low = call(low_kernel, "pack_low", laden, [], [projectors], [])
        low = call(
            window_kernel, "add_window", laden, [], [field, low], [], (), {1: 0}
        )
        below_low = turn(low, "band", 1)
        high = call(high_kernel, "pack_high", plane, [], [projectors], [], [low])
        below_high = turn(high, "band", 1)
        returned, on_low = call(
            above_kernel, "project_above", [shaped(*flat), plane], [slot_corner],
            [low, high, below_low], [],
        )
        returned = turn(returned, "band", -1)
        far_low = turn(on_low, "band", 1)

        def hand_on(values, *after):
            return call(hand_on_kernel, "hand_on", plane, [], [values], [], after)

        on_high = hand_on(below_high, on_low, returned)
        far_high = turn(on_high, "band", 1)
        on_far_low = hand_on(far_low, on_high, tables[0], energy)
        above_low = turn(on_far_low, "band", 1)
        near = call(
            near_kernel, "project_near", shaped(*flat), [slot_corner],
            [field, low, high, below_low, below_high, far_low], [],
        )
        mate, cross = call(
            halo_kernel, "cut_halos", halos, [], [field], [], [on_far_low, near]
        )
        mate, cross = swap(mate, "dom", 0), swap(cross, "dom", 1)
        on_far_high = hand_on(far_high, near, tables[0], energy, mate, cross)
        above_high = turn(on_far_high, "band", 1)
        own = call(
            last_part_kernel, "first_sums", shaped(2 * table_rows, LANES), [slot_corner],
            [tables[0], energy, field, near, returned, far_high], [flat],
        )
        chunks = [low, high, above_low, above_high, below_low, below_high, far_low, far_high]
    else:
        mate, cross = call(halo_kernel, "cut_halos", halos, [], [field], [])
        packed = call(
            whole_pack_kernel, "pack_projectors", shaped(tiles * groups * ROWS * ROWS, LANES),
            [], [projectors], [],
        )
        chunks = [lax.all_gather(packed, "band", axis=0, tiled=True)]
        own = call(
            whole_sums_kernel, "first_sums", shaped(2 * table_rows, LANES), [slot_corner],
            [tables[0], energy, field, *chunks], [flat],
        )
        mate, cross = swap(mate, "dom", 0), swap(cross, "dom", 1)
    own = own + swap(own, "dom", 0)
    other = swap(own, "dom", 1)
    far = swap(other, "dom", 0)
    before = None
    for index in range(DEGREE):
        if index > 0:
            to_mate, to_cross = sent
            mate = swap(to_mate, "dom", 0)
            own = to_cross.at[HALO_ROWS:].add(mate[HALO_ROWS:])
            cross = swap(own, "dom", 1)
            far = swap(cross[HALO_ROWS:], "dom", 0)
        local = call(
            functools.partial(local_kernel, index), f"local_{index + 1}",
            shaped(planes, SY, LANES), [],
            [*tables[1:3], field, potential, mate] + ([before] if index > 0 else []), [padded],
            cost=LOCAL_COST,
        )
        operands = [tables[0], tables[3], local, cross, own, far]
        if index == 0:
            operands.append(other)
        operands += chunks
        out_shape = [shaped(planes, SY, LANES)]
        if index > 0:
            operands.append(energy)
        if index + 1 < DEGREE:
            out_shape += sends
        if index == 0:
            out_shape += [shaped(ROWS, atoms)]
        result = call(
            functools.partial(step_kernel, index, len(chunks)), f"filter_step_{index + 1}",
            out_shape, [], operands,
            [
                flat, boxes, (planes, SY, slots * SZ),
                pltpu.SMEM(slot_corner.shape, jnp.int32), pltpu.SemaphoreType.DMA,
            ],
            late=[slot_corner],
        )
        before, field = field, result[0]
        sent = result[1:3]
        if index == 0:
            energy = result[3]
    return field[None]


def solution(mesh):
    placed = (
        P("band", "dom", None, None),
        P("dom", None, None),
        P("dom", None, "band"),
        P("dom", None),
        P("dom"),
        P(None, "dom"),
    )
    return jax.shard_map(
        on_device,
        mesh=mesh,
        in_specs=placed,
        out_specs=P("band", "dom", None, None),
        check_vma=False,
    )
```
